128 devices in a mesh: dp: 4 (over z), ctx: 4 (over y), tensor: 8 (over x, core).
Axes of the slice: x: 4, y: 4, z: 4, core: 2. Of those that a mesh axis runs over, the one named last changes fastest.
Arguments:
- query_rows: bfloat16 [4, 512, 4096], P('dp', 'ctx', 'tensor'), may hold values from -200 to 200
- key_rows: bfloat16 [4, 512, 256], P('dp', 'ctx'), may hold values from -6 to 6
- value_rows: bfloat16 [4, 512, 256], P('dp', 'ctx'), may hold values from -6 to 6
- residual: bfloat16 [4, 512, 4096], P('dp', ('ctx', 'tensor')), may hold values from -6 to 6
- out_proj: bfloat16 [4096, 4096], P('tensor'), may hold values from -0.09375 to 0.09375
- post_gain: bfloat16 [4096], replicated, may hold values from 0.099609375 to 1.8984375
- router: bfloat16 [4096, 64], replicated, may hold values from -10 to 10
- routes: int32 [4, 512, 8], P('dp', ('ctx', 'tensor')), may hold values from 0 to 63, all different within a row; in each aligned block of 16 rows (0 to 15, 16 to 31, ..., all dimensions but the last counted through in order) at most 4 rows name the same one
- w_gate: bfloat16 [64, 4096, 1536], P(('ctx', 'tensor'), None, 'dp'), may hold values from -0.09375 to 0.09375
- w_up: bfloat16 [64, 4096, 1536], P(('ctx', 'tensor'), None, 'dp'), may hold values from -0.09375 to 0.09375
- w_down: bfloat16 [64, 1536, 4096], P(('ctx', 'tensor'), 'dp'), may hold values from -80 to 80
Outputs:
- layer_out: bfloat16 [4, 512, 4096], P('dp', ('ctx', 'tensor'))
The draws below stay inside these ranges and needn't reach their ends.
Inputs may be any that keep to these rules, and one draw needn't show every extreme that they name: `routes`: the 8 experts of a token differ. Among the 16 tokens of one device (aligned blocks of the token rows), no expert is named by more than 4 of them, a bound that some block reaches.
All inputs are finite; a program needn't handle non-finite values.
Results may differ from the reference program's by a relative error of at most 0.014.
Values may be sent and summed in bfloat16 or wider, within the bound.
A program may use at most 128 MiB of HBM per device.

```python
import math
import jax
import jax.numpy as jnp
import numpy as np
from jax import lax

D = 4096
QH = 32
KVH = 2
HEAD_WIDTH = 128
FF = 1536
TOP = 8
SEQ = 512
TOK_DEV = 16
EXPERTS = 64
FF_DEV = 384
CAP = 4
N_DP = 4
N_CTX = 4
N_TENSOR = 8


def shared_keys(key):
    return jnp.clip(jax.random.normal(key, (N_DP, SEQ, KVH * HEAD_WIDTH), jnp.float32), -6.0, 6.0)


def expert_kinds(key):
    ranking = jax.random.permutation(jax.random.fold_in(key, 101), EXPERTS)
    return ranking < max(1, EXPERTS // 4)


def channel_kinds(key):
    ranking = jax.random.permutation(jax.random.fold_in(key, 103), D)
    fixed_count = max(1, D // 512)
    fixed_set = ranking < fixed_count
    return fixed_set


def channel_pushes():
    fixed_count = max(1, D // 512)
    fixed_rms = math.sqrt(0.25 * (D - fixed_count) / D + fixed_count * 16.0 / D)
    push_down = 4.0 * fixed_rms / (fixed_count * 4.0)
    return push_down


def draw_key_rows(key, part):
    base = shared_keys(key)
    return base.astype(jnp.bfloat16)


def draw_query_rows(key, part):
    key = jax.random.fold_in(key, 7)
    drawn = jnp.clip(jax.random.normal(key, (N_DP, SEQ, QH * HEAD_WIDTH), jnp.float32), -6.0, 6.0)
    return drawn.astype(jnp.bfloat16)


def draw_residual(key, part):
    fixed_set = channel_kinds(key)
    key = jax.random.fold_in(key, 11)
    jitter = 0.5 * jnp.clip(jax.random.normal(key, (N_DP, SEQ, D), jnp.float32), -6.0, 6.0)
    stream_vals = jitter
    stream_vals = jnp.where(fixed_set[None, None, :], 4.0 + 0.5 * jitter, stream_vals)
    return stream_vals.astype(jnp.bfloat16)


def draw_router(key, part):
    loud_set = expert_kinds(key)
    fixed_set = channel_kinds(key)
    push_down = channel_pushes()
    key = jax.random.fold_in(key, 5)
    column_scale = jnp.where(loud_set, 0.2, 0.7)
    jitter = jnp.clip(jax.random.normal(key, (D, EXPERTS), jnp.float32), -6.0, 6.0)
    jitter = jitter * column_scale[None, :] / math.sqrt(D)
    offsets = jnp.where(jnp.logical_and(fixed_set[:, None], loud_set[None, :]), -push_down, 0.0)
    return (jitter + offsets).astype(jnp.bfloat16)


def draw_w_down(key, part):
    loud_set = expert_kinds(key)
    key = jax.random.fold_in(key, 13)
    entries = jnp.clip(jax.random.normal(key, (EXPERTS, FF, D), jnp.float32), -6.0, 6.0) / math.sqrt(FF)
    factor = jnp.where(loud_set, 100.0, 1.0)
    return (entries * factor[:, None, None]).astype(jnp.bfloat16)


def block_levels(key, shape, split, low, top_value):
    level = 1.0
    for dim, shards_of in split:
        draws = jax.random.uniform(jax.random.fold_in(jax.random.fold_in(key, 6), dim), (shards_of,), jnp.float32, low / len(split), top_value / len(split))
        level = level * jnp.repeat(jnp.exp(draws), shape[dim] // shards_of).reshape((-1,) + (1,) * (len(shape) - 1 - dim))
    return level


def shared_out(key, own, number, rows, number_of, top, bound, slope):
    sequence = jax.random.permutation(key, number_of)
    heavy_load, ordinary = portions_of(number_of, rows * top, bound, slope, True), portions_of(number_of, rows * top, bound, slope, False)
    places = jnp.arange(number_of)

    def named(lengths, rotation):
        used = int((lengths > 0).sum())
        fixed = max(1, used // 4)
        moved = fixed + (places - fixed + rotation * (used - fixed)) % max(1, number_of - fixed)
        return jnp.zeros((number_of,), jnp.int32).at[sequence[jnp.where(places < fixed, places, moved)]].set(jnp.asarray(lengths, jnp.int32))

    lengths = jnp.where(number % 4 == 0, named(heavy_load, number // 4), named(ordinary, number - number // 4 - 1))
    mixed = jax.random.permutation(jax.random.fold_in(own, 3), number_of)
    giver, receiver = mixed[0:number_of // 2 * 2:2], mixed[1:number_of // 2 * 2:2]
    room = jnp.minimum(lengths[giver] - 1, bound - lengths[receiver]) // 2
    room = jnp.where((giver == sequence[0]) | (receiver == sequence[0]) | (lengths[receiver] == 0), 0, jnp.maximum(room, 0))
    moved = jax.random.randint(jax.random.fold_in(own, 4), (number_of // 2,), 0, 1 << 20) % (room + 1)
    lengths = lengths.at[giver].add(-moved).at[receiver].add(moved)
    labels = jnp.searchsorted(jnp.cumsum(lengths), jnp.arange(rows * top), side="right").astype(jnp.int32)
    table = labels.reshape(top, rows).T
    table = table[jax.random.permutation(jax.random.fold_in(own, 1), rows)]
    rotation = jax.random.randint(jax.random.fold_in(own, 2), (rows, 1), 0, top)
    return jnp.take_along_axis(table, (jnp.arange(top)[None, :] + rotation) % top, axis=1)


def portions_of(number_of, total, most, lean, full):
    weights = [(1 << 20) // math.isqrt(grade ** lean) + 1 for grade in range(1, number_of + 1)]
    largest = most if full else min(most, max(-(-total // number_of), total * weights[0] // sum(weights)))
    least = 1 if total - largest >= number_of - 1 else 0
    counts, surplus = [largest] + [least] * (number_of - 1), total - largest - least * (number_of - 1)
    while surplus > 0:
        candidates = [i for i in range(1, number_of) if counts[i] < largest] or [i for i in range(1, number_of) if counts[i] < most]
        whole, left = sum([weights[i] for i in candidates]), surplus
        for i in candidates:
            extra = min(most - counts[i], max(1, left * weights[i] // whole), surplus)
            counts[i] = counts[i] + extra
            surplus = surplus - extra
    return np.array(counts)


def normal_values(own_key, shape, deviation, reach, pieces=(), kind=jnp.bfloat16):
    values = jax.random.normal(own_key, shape, jnp.float32) * deviation
    if len(pieces) > 0:
        values = block_levels(own_key, shape, pieces, -0.22, 0.18) * values
    return jnp.clip(values, min=-reach, max=reach).astype(kind)


def setup_inputs(seed: int = 0) -> dict:
    arg_keys = jax.random.split(jax.random.key(seed), 12)
    query_rows = draw_query_rows(jax.random.fold_in(arg_keys[11], 71), 0)
    key_rows = draw_key_rows(jax.random.fold_in(arg_keys[11], 71), 0)
    value_rows = normal_values(arg_keys[2], (N_DP, SEQ, KVH * HEAD_WIDTH), 1.0, 6.0, ((0, 4), (1, 4)))
    residual = draw_residual(jax.random.fold_in(arg_keys[11], 71), 0)
    out_proj = normal_values(arg_keys[4], (QH * HEAD_WIDTH, D), (QH * HEAD_WIDTH) ** -0.5, 0.09375, ((0, 8),))
    post_gain = jnp.clip(1.0 + 0.18 * jax.random.normal(arg_keys[5], (D,), jnp.float32), 0.099609375, 1.8984375).astype(jnp.bfloat16)
    router = draw_router(jax.random.fold_in(arg_keys[11], 71), 0)
    routes_keys = jax.random.split(jax.random.fold_in(arg_keys[7], 1), N_DP * SEQ // TOK_DEV)
    routes_turns = jax.random.permutation(jax.random.fold_in(arg_keys[7], 3), N_DP * SEQ // TOK_DEV)
    routes = jax.vmap(lambda own, number: shared_out(jax.random.fold_in(arg_keys[7], 2), own, number, TOK_DEV, EXPERTS, TOP, CAP, 2))(routes_keys, routes_turns).reshape((N_DP, SEQ, TOP))
    w_gate = normal_values(arg_keys[8], (EXPERTS, D, FF), D ** -0.5, 0.09375, ((0, 32), (2, 4)))
    w_up = normal_values(arg_keys[9], (EXPERTS, D, FF), D ** -0.5, 0.09375, ((0, 32), (2, 4)))
    w_down = draw_w_down(jax.random.fold_in(arg_keys[11], 71), 0)
    return {"query_rows": query_rows, "key_rows": key_rows, "value_rows": value_rows, "residual": residual, "out_proj": out_proj, "post_gain": post_gain, "router": router, "routes": routes, "w_gate": w_gate, "w_up": w_up, "w_down": w_down}


def rotate(rows, heads, offset):
    batch, length, width = rows.shape
    values = rows.astype(jnp.float32).reshape(batch, length, heads, HEAD_WIDTH)
    half = HEAD_WIDTH // 2
    places = (offset + jnp.arange(length)).astype(jnp.float32)
    freqs = jnp.power(jnp.float32(1000000.0), -(jnp.arange(half).astype(jnp.float32) * 2.0 / HEAD_WIDTH))
    angles = places[:, None] * freqs[None, :]
    cosine = jnp.cos(angles)[None, :, None, :]
    sine = jnp.sin(angles)[None, :, None, :]
    first = values[..., :half]
    second = values[..., half:]
    turned = jnp.concatenate([first * cosine - second * sine, second * cosine + first * sine], axis=-1)
    return turned.astype(jnp.bfloat16)

def reference(query_rows, key_rows, value_rows, residual, out_proj, post_gain, router, routes, w_gate, w_up, w_down):
    group = QH // KVH
    qrot = rotate(query_rows, QH, 0)
    krot = rotate(key_rows, KVH, 0)
    values = value_rows.reshape(N_DP, SEQ, KVH, HEAD_WIDTH)
    causal = jnp.arange(SEQ)[:, None] >= jnp.arange(SEQ)[None, :]

    def one_head(head_id):
        head_query_rows = lax.dynamic_index_in_dim(qrot, head_id, 2, keepdims=False).astype(jnp.float32)
        head_key_rows = lax.dynamic_index_in_dim(krot, head_id // group, 2, keepdims=False).astype(jnp.float32)
        head_value_rows = lax.dynamic_index_in_dim(values, head_id // group, 2, keepdims=False).astype(jnp.float32)
        attention_score = jnp.einsum('pwv,phv->pwh', head_query_rows, head_key_rows) / jnp.sqrt(jnp.float32(HEAD_WIDTH))
        attention_score = jnp.where(causal[None], attention_score, jnp.float32(-1e+30))
        peak = lax.optimization_barrier(jnp.max(attention_score, axis=-1, keepdims=True))
        expon = jnp.where(causal[None], jnp.exp(attention_score - peak), jnp.float32(0.0))
        total = lax.optimization_barrier(jnp.sum(expon, axis=-1))
        softmax_weights = lax.optimization_barrier(expon.astype(jnp.bfloat16)).astype(jnp.float32)
        summed_output = jnp.einsum('gvj,gjw->gvw', softmax_weights, head_value_rows)
        return (summed_output / total[..., None]).astype(jnp.bfloat16)
    heads_out = lax.map(one_head, jnp.arange(QH))
    attended = jnp.transpose(heads_out, (1, 2, 0, 3)).reshape(N_DP * SEQ, QH * HEAD_WIDTH)
    projected = jnp.dot(attended, out_proj, preferred_element_type=jnp.float32)
    mixed = (residual.reshape(N_DP * SEQ, D).astype(jnp.float32) + projected).astype(jnp.bfloat16)
    mixed_wide = lax.optimization_barrier(mixed).astype(jnp.float32)
    scale = lax.rsqrt(lax.optimization_barrier(jnp.mean(mixed_wide * mixed_wide, axis=-1, keepdims=True)) + 1e-06)
    normed = (mixed_wide * scale * post_gain.astype(jnp.float32)).astype(jnp.bfloat16)
    logits = jnp.dot(normed, router, preferred_element_type=jnp.float32)
    flat_routes = routes.reshape(N_DP * SEQ, TOP)
    chosen = jnp.take_along_axis(logits, flat_routes, axis=1)
    gates = jax.nn.softmax(chosen, axis=-1)
    count_tokens = N_DP * SEQ
    limit = N_DP * N_CTX * N_TENSOR * CAP
    route_list = flat_routes.reshape(-1)
    gate_list = gates.reshape(-1)
    token_list = (jnp.arange(count_tokens * TOP) // TOP).astype(jnp.int32)
    padded = jnp.concatenate([normed, jnp.zeros((1, D), jnp.bfloat16)], axis=0)

    def one_expert(carry, inputs):
        gate_mat, up_mat, down_mat, expert_id = inputs
        struck = (route_list == expert_id).astype(jnp.int32)
        place = jnp.cumsum(struck) - 1
        place = jnp.where(struck > 0, place, limit).astype(jnp.int32)
        table = jnp.full((limit,), count_tokens, jnp.int32).at[place].set(token_list, mode='drop')
        weight_tab = jnp.zeros((limit,), jnp.float32).at[place].set(gate_list, mode='drop')
        rows = padded[table]
        gate_val = jnp.dot(rows, gate_mat, preferred_element_type=jnp.float32)
        up_val = jnp.dot(rows, up_mat, preferred_element_type=jnp.float32)
        hidden = (jax.nn.silu(gate_val) * up_val).astype(jnp.bfloat16)
        summed_output = jnp.zeros((limit, D), jnp.float32)
        for block in range(N_DP):
            part = jnp.dot(hidden[:, block * FF_DEV:(block + 1) * FF_DEV], down_mat[block * FF_DEV:(block + 1) * FF_DEV], preferred_element_type=jnp.float32).astype(jnp.bfloat16)
            summed_output = summed_output + lax.optimization_barrier(part).astype(jnp.float32)
        expert_out = lax.optimization_barrier(summed_output.astype(jnp.bfloat16)).astype(jnp.float32)
        carry = carry.at[table].add(weight_tab[:, None] * expert_out, mode='drop')
        return (carry, None)
    start = jnp.zeros((count_tokens, D), jnp.float32)
    moe_sum, unused = lax.scan(one_expert, start, (w_gate, w_up, w_down, jnp.arange(EXPERTS).astype(jnp.int32)))
    layer_out = (mixed_wide + moe_sum).astype(jnp.bfloat16)
    return layer_out.reshape(N_DP, SEQ, D)
```

```python
import functools

import jax
import jax.numpy as jnp
import numpy as np
from jax import lax
from jax.experimental import pallas as pl
from jax.experimental.pallas import tpu as pltpu
from jax.sharding import PartitionSpec as P

MESH = pl.DeviceIdType.MESH
F32 = jnp.float32
BF16 = jnp.bfloat16

D = 4096
HEAD = 128
HEADS = 4
SEQ = 512
LOCAL = 128
TOK = 16
EXPERTS = 64
FF = 384
CAP = 4
GATES = 128
WIDE = D + GATES
W = WIDE // 3
GROUP = 256
SLOTS = TOK * CAP

ORDER = (("x", "y", "z"), ("y", "z", "x"), ("z", "x", "y"))
PARTS = range(3)
AG_ROUNDS = ((0, 512), (512, 512), (1024, 384))
RS_ROUNDS = ((0, 384), (384, 512), (896, 512))
VMEM = 63 * 2**20


def rope_tables():
    half = HEAD // 2
    places = np.arange(SEQ).astype(np.float32)
    freqs = np.power(
        np.float32(1000000.0), -(np.arange(half).astype(np.float32) * np.float32(2.0) / np.float32(HEAD))
    ).astype(np.float32)
    angles = (places[:, None] * freqs[None, :]).astype(np.float32)
    cosine, sine = np.cos(angles), np.sin(angles)
    return (
        np.concatenate([cosine, cosine], axis=1).astype(np.float32),
        np.concatenate([-sine, sine], axis=1).astype(np.float32),
    )


def place():
    t = lax.axis_index("tensor")
    return {"x": t // 2, "y": lax.axis_index("ctx"), "z": lax.axis_index("dp")}, t % 2


def device(me, k, axis, step):
    value = (me[axis] + step) % 4
    if axis == "x":
        return {"tensor": value * 2 + k}
    return {"ctx" if axis == "y" else "dp": value}


def sibling(me, k):
    return {"tensor": me["x"] * 2 + 1 - k}


def greet(me, k, axes):
    barrier = pltpu.get_barrier_semaphore()
    for axis in axes:
        for step in (1, 2, 3):
            pl.semaphore_signal(
                barrier, inc=1, device_id=device(me, k, axis, step), device_id_type=MESH
            )
    pl.semaphore_signal(barrier, inc=1, device_id=sibling(me, k), device_id_type=MESH)
    pl.semaphore_wait(barrier, 3 * len(axes) + 1)


def send(src, dst, to, send_sem, recv_sem):
    pltpu.make_async_remote_copy(
        src_ref=src,
        dst_ref=dst,
        send_sem=send_sem,
        recv_sem=recv_sem,
        device_id=to,
        device_id_type=MESH,
    ).start()


def wait(ref, sem):
    pltpu.make_async_copy(ref, ref, sem).wait()


def turn(values, cosine, sine):
    values = values.astype(F32)
    return (values * cosine + pltpu.roll(values, HEAD // 2, 1) * sine).astype(BF16)


def front_kernel(
    query_ref, key_ref, value_ref, residual_ref, proj_hbm, gain_ref, router_ref, routes_ref,
    cos_ref, sin_ref, rows_ref, mixed_ref,
    proj, kv, qrot, krot, partial, far, from_sibling, from_ring,
    proj_sem, kv_send, kv_recv, sib_send, sib_recv, ring_send, ring_recv,
):
    me, k = place()
    t = lax.axis_index("tensor")
    y = me["y"]
    load = pltpu.make_async_copy(proj_hbm, proj, proj_sem)
    load.start()
    head = pl.multiple_of((t // 4) * HEAD, HEAD)
    kv[y, 0] = key_ref[0, :, pl.ds(head, HEAD)]
    kv[y, 1] = value_ref[0, :, pl.ds(head, HEAD)]
    greet(me, k, "xy")
    for step in (1, 2, 3):
        send(kv.at[y], kv.at[y], device(me, k, "y", step), kv_send, kv_recv)
    own = pl.ds(pl.multiple_of(y * LOCAL, LOCAL), LOCAL)
    cosine, sine = cos_ref[own, :], sin_ref[own, :]
    for h in range(HEADS):
        qrot[pl.ds(h * LOCAL, LOCAL), :] = turn(query_ref[0, :, h * HEAD : (h + 1) * HEAD], cosine, sine)
    wait(kv.at[pl.ds(0, 3)], kv_recv)
    for c in range(4):
        span = pl.ds(c * LOCAL, LOCAL)
        krot[span, :] = turn(kv[c, 0], cos_ref[span, :], sin_ref[span, :])
    values = kv[:, 1].reshape(SEQ, HEAD)
    place_q = y * LOCAL + lax.broadcasted_iota(jnp.int32, (LOCAL, SEQ), 0)
    causal = place_q >= lax.broadcasted_iota(jnp.int32, (LOCAL, SEQ), 1)
    attended = []
    for h in range(HEADS):
        score = lax.dot_general(
            qrot[pl.ds(h * LOCAL, LOCAL), :], krot[...], (((1,), (1,)), ((), ())),
            preferred_element_type=F32,
        ) / jnp.sqrt(F32(HEAD))
        score = jnp.where(causal, score, F32(-1e30))
        peak = jnp.max(score, axis=-1, keepdims=True)
        expon = jnp.where(causal, jnp.exp(score - peak), F32(0.0))
        total = jnp.sum(expon, axis=-1, keepdims=True)
        summed = jnp.dot(expon.astype(BF16), values, preferred_element_type=F32)
        attended.append((summed / total).astype(BF16))
    attended = jnp.concatenate(attended, axis=1)
    load.wait()
    for c in range(8):
        cols = slice(c * 512, (c + 1) * 512)
        out = jnp.dot(attended, proj[:, cols], preferred_element_type=F32)
        partial[:, :, :, cols] = out.reshape(4, 2, TOK, 512)
        far[:, :, cols] = partial[:, 1 - k, :, cols].astype(BF16)
    to = sibling(me, k)
    send(far, from_sibling, to, sib_send, sib_recv)
    wait(far, sib_send)
    wait(from_sibling, sib_recv)
    for step in (2, 1, 3):
        v = (me["x"] + step) % 4
        far[v] = (partial[v, k] + from_sibling[v].astype(F32)).astype(BF16)
        send(far.at[v], from_ring.at[step - 1], device(me, k, "x", step), ring_send, ring_recv)
    own_sum = partial[me["x"], k] + from_sibling[me["x"]].astype(F32)
    wait(from_ring, ring_recv)
    projected = own_sum + from_ring[0].astype(F32) + from_ring[1].astype(F32) + from_ring[2].astype(F32)
    mixed = (residual_ref[0].astype(F32) + projected).astype(BF16)
    mixed_ref[...] = mixed
    wide = mixed.astype(F32)
    scale = lax.rsqrt(jnp.mean(wide * wide, axis=-1, keepdims=True) + 1e-06)
    normed = (wide * scale * gain_ref[...].astype(F32)).astype(BF16)
    rows_ref[:, GATES:] = normed
    logits = jnp.dot(normed, router_ref[...], preferred_element_type=F32)
    lane = lax.broadcasted_iota(jnp.int32, (TOK, EXPERTS), 1)
    routes = routes_ref[0]
    chosen = routes[:, 0:1] == lane
    for j in range(1, 8):
        chosen = jnp.logical_or(chosen, routes[:, j : j + 1] == lane)
    peak = jnp.max(jnp.where(chosen, logits, F32(-3e38)), axis=-1, keepdims=True)
    expon = jnp.where(chosen, jnp.exp(logits - peak), F32(0.0))
    gates = expon / jnp.sum(expon, axis=-1, keepdims=True)
    high = gates.astype(BF16).astype(F32)
    rows_ref[:, :GATES] = jnp.concatenate([high, gates - high], axis=1).astype(BF16)
    wait(kv.at[pl.ds(0, 3)], kv_send)
    wait(from_ring, ring_send)


def front(query_rows, key_rows, value_rows, residual, out_proj, post_gain, router, routes):
    cosine, sine = rope_tables()
    vmem = pl.BlockSpec(memory_space=pltpu.VMEM)
    dma = pltpu.SemaphoreType.DMA
    return pl.pallas_call(
        front_kernel,
        out_shape=(
            jax.ShapeDtypeStruct((TOK, WIDE), BF16),
            jax.ShapeDtypeStruct((TOK, D), BF16),
        ),
        in_specs=[vmem] * 4 + [pl.BlockSpec(memory_space=pl.ANY)] + [vmem] * 5,
        out_specs=(vmem, vmem),
        scratch_shapes=[
            pltpu.VMEM((HEADS * HEAD, D), BF16),
            pltpu.VMEM((4, 2, LOCAL, HEAD), BF16),
            pltpu.VMEM((HEADS * LOCAL, HEAD), BF16),
            pltpu.VMEM((SEQ, HEAD), BF16),
            pltpu.VMEM((4, 2, TOK, D), F32),
            pltpu.VMEM((4, TOK, D), BF16),
            pltpu.VMEM((4, TOK, D), BF16),
            pltpu.VMEM((3, TOK, D), BF16),
            dma, dma, dma, dma, dma, dma, dma,
        ],
        compiler_params=pltpu.CompilerParams(
            collective_id=0, has_side_effects=True, vmem_limit_bytes=48 * 2**20
        ),
    )(
        query_rows, key_rows, value_rows, residual, out_proj, post_gain.reshape(1, D), router, routes,
        jnp.asarray(cosine), jnp.asarray(sine),
    )


def expert_kernel(
    rows_ref, mixed_ref, gate_hbm, up_hbm, down_hbm, out_ref,
    x0, x1, x2, rd0, rd1, rd2, rf0, rf1, rf2, rr0, rr1, rr2, rb0, rb1, rb2, ra0, ra1, ra2,
    wgu, wd, packed, acc, hidden, pick, unpick, row_gate,
    w_sem, p1s, p1r, p2s, p2r, p3s, p3r, ds, dr,
    qds, qdr, qfs, qfr, q3s, q3r, q2s, q2r, q1s, q1r,
):
    xs, rd, rf, rr = (x0, x1, x2), (rd0, rd1, rd2), (rf0, rf1, rf2), (rr0, rr1, rr2)
    rb, ra = (rb0, rb1, rb2), (ra0, ra1, ra2)
    me, k = place()
    twin = sibling(me, k)

    loads = []
    for e in range(2):
        loads.append(pltpu.make_async_copy(gate_hbm.at[e], wgu.at[e, :, pl.ds(0, FF)], w_sem.at[e]))
        loads.append(pltpu.make_async_copy(up_hbm.at[e], wgu.at[e, :, pl.ds(FF, FF)], w_sem.at[2 + e]))
    loads.append(pltpu.make_async_copy(down_hbm, wd, w_sem.at[4]))
    for load in loads:
        load.start()
    for p in PARTS:
        xs[p][k, me["z"], me["y"], me["x"]] = rows_ref[:, p * W : (p + 1) * W]
    greet(me, k, "xyz")

    def at(ref, lead, cols, fix):
        index = [fix.get(axis, slice(None)) for axis in "zyx"]
        return ref.at[(*lead, *index, slice(None), pl.ds(*cols))]


    def p1_start(p):
        a = ORDER[p][0]
        block = at(xs[p], (k,), (0, W), me)
        for step in (2, 1, 3):
            send(block, block, device(me, k, a, step), p1s.at[p], p1r.at[p])

    def p1_wait(p):
        wait(xs[p].at[0, 0, 0, pl.ds(0, 3)], p1r.at[p])

    def p2_start(p, r):
        a, b, c = ORDER[p]
        unit = at(xs[p], (k,), AG_ROUNDS[r], {b: me[b], c: me[c]})
        for step in (2, 1, 3):
            send(unit, unit, device(me, k, b, step), p2s.at[p, r], p2r.at[p, r])

    def p2_bytes(p, r):
        return xs[p].at[0, 0, pl.ds(0, 3), :, :, pl.ds(*AG_ROUNDS[r])]

    def p3_unit(p, r, step, half=None):
        a, b, c = ORDER[p]
        fix = {c: (me[c] + step) % 4}
        if half is not None:
            fix[b] = pl.ds(2 * half, 2)
        return at(xs[p], (k,), AG_ROUNDS[r], fix)

    def p3_send(p, r, step, half, way):
        unit = p3_unit(p, r, step, half)
        recv = p3r.at[p, r, 2] if half is not None else p3r.at[p, r, 0 if way == 1 else 1]
        send(unit, unit, device(me, k, ORDER[p][2], way), p3s.at[p, r], recv)

    def twin_send(p, r, step):
        unit = p3_unit(p, r, step)
        send(unit, unit, twin, ds.at[p, r], dr.at[p, r])

    def p3_start(r):
        for p in PARTS:
            wait(p2_bytes(p, r), p2r.at[p, r])
            p3_send(p, r, 0, None, 1)
            p3_send(p, r, 0, None, -1)

    def p3_forward(r):
        for p in PARTS:
            wait(p3_unit(p, r, -1), p3r.at[p, r, 0])
            p3_send(p, r, -1, 0, 1)
            wait(p3_unit(p, r, 1), p3r.at[p, r, 1])
            p3_send(p, r, 1, 1, -1)
        for p in PARTS:
            for step in (0, -1, 1):
                twin_send(p, r, step)

    def p3_finish(r):
        for p in PARTS:
            wait(p3_unit(p, r, 2), p3r.at[p, r, 2])
            twin_send(p, r, 2)

    def twin_wait(r):
        for p in PARTS:
            wait(xs[p].at[1 - k, :, :, :, :, pl.ds(*AG_ROUNDS[r])], dr.at[p, r])


    def selections():
        first = 2 * (me["y"] * 8 + lax.axis_index("tensor"))
        rows = lax.broadcasted_iota(jnp.int32, (8, GATES), 0)
        lanes = lax.broadcasted_iota(jnp.int32, (8, GATES), 1)
        mine = jnp.logical_and(lanes % EXPERTS == first + rows, rows < 2).astype(F32).astype(BF16)
        s = lax.broadcasted_iota(jnp.int32, (GROUP, GROUP), 0)
        u = lax.broadcasted_iota(jnp.int32, (GROUP, GROUP), 1)
        earlier = jnp.logical_and(s // TOK == u // TOK, s < u).astype(F32).astype(BF16)
        base = (lax.broadcasted_iota(jnp.int32, (1, GROUP), 1) // TOK * CAP).astype(F32)
        slots = lax.broadcasted_iota(jnp.int32, (SLOTS, GROUP), 0).astype(F32)

        def one(g, carry):
            tile = x0[g // 4, g % 4, :, :, :, :GATES].reshape(GROUP, GATES)
            gate = lax.dot_general(mine, tile, (((1,), (1,)), ((), ())), preferred_element_type=F32)
            named = (gate > 0).astype(F32)
            rank = jnp.dot(named.astype(BF16), earlier, preferred_element_type=F32)
            both = []
            for e in range(2):
                hit = jnp.logical_and(slots == rank[e : e + 1] + base, gate[e : e + 1] > 0).astype(F32)
                worth = jnp.sum(hit * gate[e : e + 1], axis=1, keepdims=True)
                row_gate[e, pl.ds(g * SLOTS, SLOTS), :] = jnp.broadcast_to(worth, (SLOTS, 128))
                both.append(hit)
            both = jnp.concatenate(both, axis=0)
            pick[g] = both.astype(BF16)
            unpick[g] = both.T.astype(BF16)
            return carry

        lax.fori_loop(0, 8, one, 0)

    def spans(r):
        found, at_col = [], 0
        for p in PARTS:
            lo, size = AG_ROUNDS[r]
            if p == 0 and lo == 0:
                lo, size = GATES, size - GATES
            found.append((p, lo, size, at_col))
            at_col += size
        return found

    def compact(r):
        for p, lo, size, col in spans(r):
            def one(g, carry, p=p, lo=lo, size=size, col=col):
                tokens = xs[p][g // 4, g % 4, :, :, :, lo : lo + size].reshape(GROUP, size)
                rows = jnp.dot(pick[g], tokens, preferred_element_type=F32).astype(BF16)
                for e in range(2):
                    packed[e, pl.ds(g * SLOTS, SLOTS), col : col + size] = rows[e * SLOTS : (e + 1) * SLOTS]
                return carry

            lax.fori_loop(0, 8, one, 0)

    def gate_up(r):
        def one(e, carry):
            total = None
            for p, lo, size, col in spans(r):
                from_row = p * W + lo - GATES
                term = jnp.dot(
                    packed[e, :, col : col + size], wgu[e, from_row : from_row + size, :],
                    preferred_element_type=F32,
                )
                total = term if total is None else total + term
            if r > 0:
                total = total + acc[e]
            if r < len(AG_ROUNDS) - 1:
                acc[e] = total
            else:
                gate, up = total[:, :FF], total[:, FF:]
                hidden[e] = (gate / (1.0 + jnp.exp(-gate)) * up).astype(BF16)
            return carry

        lax.fori_loop(0, 2, one, 0)


    def out_cols(p, r):
        lo, size = RS_ROUNDS[r]
        if p == 0 and lo == 0:
            lo, size = GATES, size - GATES
        return lo, size

    def down(r):
        for p in PARTS:
            lo, size = out_cols(p, r)
            col = p * W + lo - GATES

            def product(e, carry, lo=lo, size=size, col=col):
                part = jnp.dot(hidden[e], wd[e, :, col : col + size], preferred_element_type=F32)
                packed[e, :, :size] = (part * row_gate[e, :, 0:1]).astype(BF16)
                return carry

            lax.fori_loop(0, 2, product, 0)

            def one(i, carry, p=p, lo=lo, size=size):
                g = (i + 4 * (1 - k)) % 8
                rows = jnp.concatenate(
                    [packed[e, pl.ds(g * SLOTS, SLOTS), :size] for e in range(2)], axis=0
                )
                tokens = jnp.dot(unpick[g], rows, preferred_element_type=F32).astype(BF16)
                xs[p][g // 4, g % 4, :, :, :, lo : lo + size] = tokens.reshape(4, 4, TOK, size)
                return carry

            lax.fori_loop(0, 4, one, 0)
            cols = (lo, size)
            send(at(xs[p], (1 - k,), cols, {}), at(rd[p], (), cols, {}), twin, qds.at[p, r], qdr.at[p, r])
            lax.fori_loop(4, 8, one, 0)

    def total_into(dst, refs):
        total = refs[0][...].astype(F32)
        for ref in refs[1:]:
            total = total + ref[...].astype(F32)
        dst[...] = total.astype(BF16)

    def unit_of(ref, lead, p, r, step, pieces=1, piece=0):
        a, b, c = ORDER[p]
        fix = {c: (me[c] + step) % 4}
        if pieces == 2:
            fix[b] = pl.ds(2 * piece, 2)
        elif pieces == 4:
            fix[b] = piece
        return at(ref, lead, out_cols(p, r), fix)

    def add_unit(p, r, step):
        def one(i, carry):
            mine = unit_of(xs[p], (k,), p, r, step, 4, i)
            total_into(mine, [mine, unit_of(rd[p], (), p, r, step, 4, i)])
            return carry

        lax.fori_loop(0, 4, one, 0)

    def piece_of(ref, lead, p, r, fix):
        a, b, c = ORDER[p]
        index = [fix.get(axis, slice(None)) for axis in "zyx" if axis != c]
        return ref.at[(*lead, *index, slice(None), pl.ds(*out_cols(p, r)))]

    def halves(p, half):
        return 2 * half

    def s1(r):
        for p in PARTS:
            cols = out_cols(p, r)
            wait(at(rd[p], (), cols, {}), qdr.at[p, r])
            add_unit(p, r, 2)
            c = ORDER[p][2]
            for half, way in ((0, 1), (1, -1)):
                src = unit_of(xs[p], (k,), p, r, 2, 2, half)
                send(src, half_slot(p, r, half), device(me, k, c, way), qfs.at[p, r], qfr.at[p, r, half])
            add_unit(p, r, 1)
            add_unit(p, r, -1)

    def half_slot(p, r, half, i=None):
        b = ORDER[p][1]
        fix = {} if i is None else {b: i}
        a, b, c = ORDER[p]
        index = [fix.get(axis, slice(None)) for axis in "zyx" if axis != c]
        return rf[p].at[(half, *index, slice(None), pl.ds(*out_cols(p, r)))]

    def s2(r):
        for p in PARTS:
            c = ORDER[p][2]
            for half, way in ((0, 1), (1, -1)):
                wait(half_slot(p, r, half), qfr.at[p, r, half])

                def one(i, carry, half=half, way=way):
                    mine = unit_of(xs[p], (k,), p, r, way, 4, 2 * half + i)
                    total_into(mine, [mine, half_slot(p, r, half, i)])
                    return carry

                lax.fori_loop(0, 2, one, 0)
                src = unit_of(xs[p], (k,), p, r, way)
                slot = piece_of(rr[p], (half,), p, r, {})
                send(src, slot, device(me, k, c, way), q3s.at[p, r], q3r.at[p, r])
            add_unit(p, r, 0)

    def s3(r):
        for p in PARTS:
            a, b, c = ORDER[p]
            wait(piece_of(rr[p], (slice(None),), p, r, {}), q3r.at[p, r])

            def one(i, carry, b=b):
                mine = unit_of(xs[p], (k,), p, r, 0, 4, i)
                total_into(mine, [mine] + [piece_of(rr[p], (h,), p, r, {b: i}) for h in range(2)])
                return carry

            lax.fori_loop(0, 4, one, 0)
            for step in (2, 1, 3):
                src = unit_of(xs[p], (k,), p, r, 0, 4, (me[b] + step) % 4)
                slot = rb[p].at[step - 1, :, :, pl.ds(*out_cols(p, r))]
                send(src, slot, device(me, k, b, step), q2s.at[p, r], q2r.at[p, r])

    def s4(r):
        for p in PARTS:
            a, b, c = ORDER[p]
            cols = pl.ds(*out_cols(p, r))
            wait(rb[p].at[:, :, :, cols], q2r.at[p, r])
            mine = unit_of(xs[p], (k,), p, r, 0, 4, me[b])
            total_into(mine, [mine] + [rb[p].at[j, :, :, cols] for j in range(3)])
            for step in (2, 1, 3):
                src = at(xs[p], (k,), out_cols(p, r), {**me, a: (me[a] + step) % 4})
                send(src, ra[p].at[step - 1, :, cols], device(me, k, a, step), q1s.at[p, r], q1r.at[p, r])

    def s5(r):
        for p in PARTS:
            lo, size = out_cols(p, r)
            cols = pl.ds(lo, size)
            wait(ra[p].at[:, :, cols], q1r.at[p, r])
            total = at(xs[p], (k,), (lo, size), me)[...].astype(F32)
            for j in range(3):
                total = total + ra[p][j, :, cols].astype(F32)
            col = p * W + lo - GATES
            span = slice(col, col + size)
            out_ref[:, span] = (mixed_ref[:, span].astype(F32) + total).astype(BF16)


    for p in PARTS:
        p1_start(p)
    for p in PARTS:
        p1_wait(p)
        for r in range(3):
            p2_start(p, r)
    p3_start(0)
    p3_start(1)
    p3_forward(0)
    p3_start(2)
    p3_finish(0)
    for load in loads:
        load.wait()
    twin_wait(0)
    selections()
    p3_forward(1)
    compact(0)
    gate_up(0)
    p3_finish(1)
    p3_forward(2)
    twin_wait(1)
    compact(1)
    gate_up(1)
    p3_finish(2)
    twin_wait(2)
    compact(2)
    gate_up(2)
    for p in PARTS:
        wait(xs[p].at[0, 0, 0, pl.ds(0, 3)], p1s.at[p])
        for r in range(3):
            cols = pl.ds(*AG_ROUNDS[r])
            wait(p2_bytes(p, r), p2s.at[p, r])
            wait(xs[p].at[0, pl.ds(0, 3), :, :, :, cols], p3s.at[p, r])
            wait(xs[p].at[0, :, :, :, :, cols], ds.at[p, r])
    down(0)
    s1(0)
    down(1)
    s2(0)
    s1(1)
    down(2)
    s2(1)
    s1(2)
    s3(0)
    s2(2)
    s4(0)
    s3(1)
    s5(0)
    s4(1)
    s3(2)
    s5(1)
    s4(2)
    s5(2)
    for p in PARTS:
        for r in range(3):
            cols = pl.ds(*out_cols(p, r))
            wait(xs[p].at[0, :, :, :, :, cols], qds.at[p, r])
            wait(rf[p].at[:, :, :, :, cols], qfs.at[p, r])
            wait(rr[p].at[:, :, :, :, cols], q3s.at[p, r])
            wait(rb[p].at[:, :, :, cols], q2s.at[p, r])
            wait(ra[p].at[:, :, cols], q1s.at[p, r])


def experts(rows, mixed, w_gate, w_up, w_down):
    vmem = pl.BlockSpec(memory_space=pltpu.VMEM)
    hbm = pl.BlockSpec(memory_space=pl.ANY)
    dma = pltpu.SemaphoreType.DMA

    def half_shape(p):
        a, b, c = ORDER[p]
        return (2, *[2 if axis == b else 4 for axis in "zyx" if axis != c], TOK, W)

    scratch = (
        [pltpu.VMEM((2, 4, 4, 4, TOK, W), BF16)] * 3
        + [pltpu.VMEM((4, 4, 4, TOK, W), BF16)] * 3
        + [pltpu.VMEM(half_shape(p), BF16) for p in PARTS]
        + [pltpu.VMEM((2, 4, 4, TOK, W), BF16)] * 3
        + [pltpu.VMEM((3, 4, TOK, W), BF16)] * 3
        + [pltpu.VMEM((3, TOK, W), BF16)] * 3
        + [
            pltpu.VMEM((2, D, 2 * FF), BF16),
            pltpu.VMEM((2, FF, D), BF16),
            pltpu.VMEM((2, 8 * SLOTS, 1536), BF16),
            pltpu.VMEM((2, 8 * SLOTS, 2 * FF), F32),
            pltpu.VMEM((2, 8 * SLOTS, FF), BF16),
            pltpu.VMEM((8, 2 * SLOTS, GROUP), BF16),
            pltpu.VMEM((8, GROUP, 2 * SLOTS), BF16),
            pltpu.VMEM((2, 8 * SLOTS, 128), F32),
        ]
        + [dma((5,)), dma((3,)), dma((3,)), dma((3, 3)), dma((3, 3)), dma((3, 3)), dma((3, 3, 3)), dma((3, 3)), dma((3, 3))]
        + [dma((3, 3)), dma((3, 3)), dma((3, 3)), dma((3, 3, 2))]
        + [dma((3, 3))] * 6
    )
    return pl.pallas_call(
        expert_kernel,
        out_shape=jax.ShapeDtypeStruct((TOK, D), BF16),
        in_specs=[vmem, vmem, hbm, hbm, hbm],
        out_specs=vmem,
        scratch_shapes=scratch,
        compiler_params=pltpu.CompilerParams(
            collective_id=1, has_side_effects=True, vmem_limit_bytes=VMEM
        ),
    )(rows, mixed, w_gate, w_up, w_down)


def on_device(
    query_rows,
    key_rows,
    value_rows,
    residual,
    out_proj,
    post_gain,
    router,
    routes,
    w_gate,
    w_up,
    w_down,
):
    rows, mixed = front(
        query_rows, key_rows, value_rows, residual, out_proj, post_gain, router, routes
    )
    return experts(rows, mixed, w_gate, w_up, w_down)[None]


def solution(mesh):
    in_specs = (
        P("dp", "ctx", "tensor"),
        P("dp", "ctx", None),
        P("dp", "ctx", None),
        P("dp", ("ctx", "tensor"), None),
        P("tensor", None),
        P(),
        P(),
        P("dp", ("ctx", "tensor"), None),
        P(("ctx", "tensor"), None, "dp"),
        P(("ctx", "tensor"), None, "dp"),
        P(("ctx", "tensor"), "dp", None),
    )
    out_specs = P("dp", ("ctx", "tensor"), None)
    return jax.shard_map(
        on_device, mesh=mesh, in_specs=in_specs, out_specs=out_specs, check_vma=False
    )
```

```python
import functools

import jax
import jax.numpy as jnp
import numpy as np
from jax import lax
from jax.experimental import pallas as pl
from jax.experimental.pallas import tpu as pltpu
from jax.sharding import PartitionSpec as P

MESH = pl.DeviceIdType.MESH
F32 = jnp.float32
BF16 = jnp.bfloat16

D = 4096
HEAD = 128
HEADS = 4
SEQ = 512
LOCAL = 128
TOK = 16
EXPERTS = 64
FF = 384
CAP = 4
GATES = 128
WIDE = D + GATES
W = WIDE // 3
GROUP = 256
SLOTS = TOK * CAP

ORDER = (("x", "y", "z"), ("y", "z", "x"), ("z", "x", "y"))
PARTS = range(3)
AG_ROUNDS = ((0, 512), (512, 512), (1024, 384))
RS_ROUNDS = ((0, 384), (384, 512), (896, 512))
VMEM = 63 * 2**20


def rope_tables():
    half = HEAD // 2
    places = np.arange(SEQ).astype(np.float32)
    freqs = np.power(
        np.float32(1000000.0), -(np.arange(half).astype(np.float32) * np.float32(2.0) / np.float32(HEAD))
    ).astype(np.float32)
    angles = (places[:, None] * freqs[None, :]).astype(np.float32)
    cosine, sine = np.cos(angles), np.sin(angles)
    return (
        np.concatenate([cosine, cosine], axis=1).astype(np.float32),
        np.concatenate([-sine, sine], axis=1).astype(np.float32),
    )


def place():
    t = lax.axis_index("tensor")
    return {"x": t // 2, "y": lax.axis_index("ctx"), "z": lax.axis_index("dp")}, t % 2


def device(me, k, axis, step):
    value = (me[axis] + step) % 4
    if axis == "x":
        return {"tensor": value * 2 + k}
    return {"ctx" if axis == "y" else "dp": value}


def sibling(me, k):
    return {"tensor": me["x"] * 2 + 1 - k}


def greet(me, k, axes):
    barrier = pltpu.get_barrier_semaphore()
    for axis in axes:
        for step in (1, 2, 3):
            pl.semaphore_signal(
                barrier, inc=1, device_id=device(me, k, axis, step), device_id_type=MESH
            )
    pl.semaphore_signal(barrier, inc=1, device_id=sibling(me, k), device_id_type=MESH)
    pl.semaphore_wait(barrier, 3 * len(axes) + 1)


def send(src, dst, to, send_sem, recv_sem):
    pltpu.make_async_remote_copy(
        src_ref=src,
        dst_ref=dst,
        send_sem=send_sem,
        recv_sem=recv_sem,
        device_id=to,
        device_id_type=MESH,
    ).start()


def wait(ref, sem):
    pltpu.make_async_copy(ref, ref, sem).wait()


def turn(values, cosine, sine):
    values = values.astype(F32)
    return (values * cosine + pltpu.roll(values, HEAD // 2, 1) * sine).astype(BF16)


def front_kernel(
    query_ref, key_ref, value_ref, residual_ref, proj_hbm, gain_ref, router_ref, routes_ref,
    cos_ref, sin_ref, rows_ref, mixed_ref,
    proj, kv, qrot, krot, partial, far, from_sibling, from_ring,
    proj_sem, kv_send, kv_recv, sib_send, sib_recv, ring_send, ring_recv,
):
    me, k = place()
    t = lax.axis_index("tensor")
    y = me["y"]
    load = pltpu.make_async_copy(proj_hbm, proj, proj_sem)
    load.start()
    head = pl.multiple_of((t // 4) * HEAD, HEAD)
    kv[y, 0] = key_ref[0, :, pl.ds(head, HEAD)]
    kv[y, 1] = value_ref[0, :, pl.ds(head, HEAD)]
    greet(me, k, "xy")
    for step in (1, 2, 3):
        send(kv.at[y], kv.at[y], device(me, k, "y", step), kv_send, kv_recv)
    own = pl.ds(pl.multiple_of(y * LOCAL, LOCAL), LOCAL)
    cosine, sine = cos_ref[own, :], sin_ref[own, :]
    for h in range(HEADS):
        qrot[pl.ds(h * LOCAL, LOCAL), :] = turn(query_ref[0, :, h * HEAD : (h + 1) * HEAD], cosine, sine)
    wait(kv.at[pl.ds(0, 3)], kv_recv)
    for c in range(4):
        span = pl.ds(c * LOCAL, LOCAL)
        krot[span, :] = turn(kv[c, 0], cos_ref[span, :], sin_ref[span, :])
    values = kv[:, 1].reshape(SEQ, HEAD)
    place_q = y * LOCAL + lax.broadcasted_iota(jnp.int32, (LOCAL, SEQ), 0)
    causal = place_q >= lax.broadcasted_iota(jnp.int32, (LOCAL, SEQ), 1)
    attended = []
    for h in range(HEADS):
        score = lax.dot_general(
            qrot[pl.ds(h * LOCAL, LOCAL), :], krot[...], (((1,), (1,)), ((), ())),
            preferred_element_type=F32,
        ) / jnp.sqrt(F32(HEAD))
        score = jnp.where(causal, score, F32(-1e30))
        peak = jnp.max(score, axis=-1, keepdims=True)
        expon = jnp.where(causal, jnp.exp(score - peak), F32(0.0))
        total = jnp.sum(expon, axis=-1, keepdims=True)
        summed = jnp.dot(expon.astype(BF16), values, preferred_element_type=F32)
        attended.append((summed / total).astype(BF16))
    attended = jnp.concatenate(attended, axis=1)
    load.wait()
    for c in range(8):
        cols = slice(c * 512, (c + 1) * 512)
        out = jnp.dot(attended, proj[:, cols], preferred_element_type=F32)
        partial[:, :, :, cols] = out.reshape(4, 2, TOK, 512)
        far[:, :, cols] = partial[:, 1 - k, :, cols].astype(BF16)
    to = sibling(me, k)
    send(far, from_sibling, to, sib_send, sib_recv)
    wait(far, sib_send)
    wait(from_sibling, sib_recv)
    for step in (2, 1, 3):
        v = (me["x"] + step) % 4
        far[v] = (partial[v, k] + from_sibling[v].astype(F32)).astype(BF16)
        send(far.at[v], from_ring.at[step - 1], device(me, k, "x", step), ring_send, ring_recv)
    own_sum = partial[me["x"], k] + from_sibling[me["x"]].astype(F32)
    wait(from_ring, ring_recv)
    projected = own_sum + from_ring[0].astype(F32) + from_ring[1].astype(F32) + from_ring[2].astype(F32)
    mixed = (residual_ref[0].astype(F32) + projected).astype(BF16)
    mixed_ref[...] = mixed
    wide = mixed.astype(F32)
    scale = lax.rsqrt(jnp.mean(wide * wide, axis=-1, keepdims=True) + 1e-06)
    normed = (wide * scale * gain_ref[...].astype(F32)).astype(BF16)
    rows_ref[:, GATES:] = normed
    logits = jnp.dot(normed, router_ref[...], preferred_element_type=F32)
    lane = lax.broadcasted_iota(jnp.int32, (TOK, EXPERTS), 1)
    routes = routes_ref[0]
    chosen = routes[:, 0:1] == lane
    for j in range(1, 8):
        chosen = jnp.logical_or(chosen, routes[:, j : j + 1] == lane)
    peak = jnp.max(jnp.where(chosen, logits, F32(-3e38)), axis=-1, keepdims=True)
    expon = jnp.where(chosen, jnp.exp(logits - peak), F32(0.0))
    gates = expon / jnp.sum(expon, axis=-1, keepdims=True)
    high = gates.astype(BF16).astype(F32)
    rows_ref[:, :GATES] = jnp.concatenate([high, gates - high], axis=1).astype(BF16)
    wait(kv.at[pl.ds(0, 3)], kv_send)
    wait(from_ring, ring_send)


def front(query_rows, key_rows, value_rows, residual, out_proj, post_gain, router, routes):
    cosine, sine = rope_tables()
    vmem = pl.BlockSpec(memory_space=pltpu.VMEM)
    dma = pltpu.SemaphoreType.DMA
    return pl.pallas_call(
        front_kernel,
        out_shape=(
            jax.ShapeDtypeStruct((TOK, WIDE), BF16),
            jax.ShapeDtypeStruct((TOK, D), BF16),
        ),
        in_specs=[vmem] * 4 + [pl.BlockSpec(memory_space=pl.ANY)] + [vmem] * 5,
        out_specs=(vmem, vmem),
        scratch_shapes=[
            pltpu.VMEM((HEADS * HEAD, D), BF16),
            pltpu.VMEM((4, 2, LOCAL, HEAD), BF16),
            pltpu.VMEM((HEADS * LOCAL, HEAD), BF16),
            pltpu.VMEM((SEQ, HEAD), BF16),
            pltpu.VMEM((4, 2, TOK, D), F32),
            pltpu.VMEM((4, TOK, D), BF16),
            pltpu.VMEM((4, TOK, D), BF16),
            pltpu.VMEM((3, TOK, D), BF16),
            dma, dma, dma, dma, dma, dma, dma,
        ],
        compiler_params=pltpu.CompilerParams(
            collective_id=0, has_side_effects=True, vmem_limit_bytes=48 * 2**20
        ),
    )(
        query_rows, key_rows, value_rows, residual, out_proj, post_gain.reshape(1, D), router, routes,
        jnp.asarray(cosine), jnp.asarray(sine),
    )


def expert_kernel(
    rows_ref, mixed_ref, gate_hbm, up_hbm, down_hbm, out_ref,
    x0, x1, x2, rd0, rd1, rd2, rf0, rf1, rf2, rr0, rr1, rr2, rb0, rb1, rb2, ra0, ra1, ra2,
    wgu, wd, packed, acc, hidden, pick, unpick, row_gate,
    w_sem, p1s, p1r, p2s, p2r, p3s, p3r, ds, dr,
    qds, qdr, qfs, qfr, q3s, q3r, q2s, q2r, q1s, q1r,
):
    xs, rd, rf, rr = (x0, x1, x2), (rd0, rd1, rd2), (rf0, rf1, rf2), (rr0, rr1, rr2)
    rb, ra = (rb0, rb1, rb2), (ra0, ra1, ra2)
    me, k = place()
    twin = sibling(me, k)

    def spans(r):
        found, at_col = [], 0
        for p in PARTS:
            lo, size = AG_ROUNDS[r]
            if p == 0 and lo == 0:
                lo, size = GATES, size - GATES
            found.append((p, lo, size, at_col))
            at_col += size
        return found

    def weights(r):
        copies = []
        for e in range(2):
            for n, hbm in enumerate((gate_hbm, up_hbm)):
                for p, lo, size, col in spans(r):
                    from_row = p * W + lo - GATES
                    copies.append(
                        pltpu.make_async_copy(
                            hbm.at[e, pl.ds(from_row, size), :],
                            wgu.at[r % 2, e, pl.ds(col, size), pl.ds(n * FF, FF)],
                            w_sem.at[r],
                        )
                    )
        return copies

    def weights_start(r):
        for copy in weights(r):
            copy.start()

    def weights_wait(r):
        total = sum(size for p, lo, size, col in spans(r))
        wait(wgu.at[r % 2, :, pl.ds(0, total), :], w_sem.at[r])

    load_down = pltpu.make_async_copy(down_hbm, wd, w_sem.at[3])
    weights_start(0)
    weights_start(1)
    load_down.start()
    for p in PARTS:
        xs[p][k, me["z"], me["y"], me["x"]] = rows_ref[:, p * W : (p + 1) * W]
    greet(me, k, "xyz")

    def at(ref, lead, cols, fix):
        index = [fix.get(axis, slice(None)) for axis in "zyx"]
        return ref.at[(*lead, *index, slice(None), pl.ds(*cols))]


    def p1_start(p):
        a = ORDER[p][0]
        block = at(xs[p], (k,), (0, W), me)
        for step in (2, 1, 3):
            send(block, block, device(me, k, a, step), p1s.at[p], p1r.at[p])

    def p1_wait(p):
        wait(xs[p].at[0, 0, 0, pl.ds(0, 3)], p1r.at[p])

    def p2_start(p, r):
        a, b, c = ORDER[p]
        unit = at(xs[p], (k,), AG_ROUNDS[r], {b: me[b], c: me[c]})
        for step in (2, 1, 3):
            send(unit, unit, device(me, k, b, step), p2s.at[p, r], p2r.at[p, r])

    def p2_bytes(p, r):
        return xs[p].at[0, 0, pl.ds(0, 3), :, :, pl.ds(*AG_ROUNDS[r])]

    def p3_unit(p, r, step, half=None):
        a, b, c = ORDER[p]
        fix = {c: (me[c] + step) % 4}
        if half is not None:
            fix[b] = pl.ds(2 * half, 2)
        return at(xs[p], (k,), AG_ROUNDS[r], fix)

    def p3_send(p, r, step, half, way):
        unit = p3_unit(p, r, step, half)
        recv = p3r.at[p, r, 2] if half is not None else p3r.at[p, r, 0 if way == 1 else 1]
        send(unit, unit, device(me, k, ORDER[p][2], way), p3s.at[p, r], recv)

    def twin_send(p, r, step):
        unit = p3_unit(p, r, step)
        send(unit, unit, twin, ds.at[p, r], dr.at[p, r])

    def p3_start(r):
        for p in PARTS:
            wait(p2_bytes(p, r), p2r.at[p, r])
            p3_send(p, r, 0, None, 1)
            p3_send(p, r, 0, None, -1)

    def p3_forward(r):
        for p in PARTS:
            wait(p3_unit(p, r, -1), p3r.at[p, r, 0])
            p3_send(p, r, -1, 0, 1)
            wait(p3_unit(p, r, 1), p3r.at[p, r, 1])
            p3_send(p, r, 1, 1, -1)
        for p in PARTS:
            for step in (0, -1, 1):
                twin_send(p, r, step)

    def p3_finish(r):
        for p in PARTS:
            wait(p3_unit(p, r, 2), p3r.at[p, r, 2])
            twin_send(p, r, 2)

    def twin_wait(r):
        for p in PARTS:
            wait(xs[p].at[1 - k, :, :, :, :, pl.ds(*AG_ROUNDS[r])], dr.at[p, r])


    def selections():
        first = 2 * (me["y"] * 8 + lax.axis_index("tensor"))
        rows = lax.broadcasted_iota(jnp.int32, (8, GATES), 0)
        lanes = lax.broadcasted_iota(jnp.int32, (8, GATES), 1)
        mine = jnp.logical_and(lanes % EXPERTS == first + rows, rows < 2).astype(F32).astype(BF16)
        s = lax.broadcasted_iota(jnp.int32, (GROUP, GROUP), 0)
        u = lax.broadcasted_iota(jnp.int32, (GROUP, GROUP), 1)
        earlier = jnp.logical_and(s // TOK == u // TOK, s < u).astype(F32).astype(BF16)
        base = (lax.broadcasted_iota(jnp.int32, (1, GROUP), 1) // TOK * CAP).astype(F32)
        slots = lax.broadcasted_iota(jnp.int32, (SLOTS, GROUP), 0).astype(F32)

        def one(g, carry):
            tile = x0[g // 4, g % 4, :, :, :, :GATES].reshape(GROUP, GATES)
            gate = lax.dot_general(mine, tile, (((1,), (1,)), ((), ())), preferred_element_type=F32)
            named = (gate > 0).astype(F32)
            rank = jnp.dot(named.astype(BF16), earlier, preferred_element_type=F32)
            both = []
            for e in range(2):
                hit = jnp.logical_and(slots == rank[e : e + 1] + base, gate[e : e + 1] > 0).astype(F32)
                worth = jnp.sum(hit * gate[e : e + 1], axis=1, keepdims=True)
                row_gate[e, pl.ds(g * SLOTS, SLOTS), :] = jnp.broadcast_to(worth, (SLOTS, 128))
                both.append(hit)
            both = jnp.concatenate(both, axis=0)
            pick[g] = both.astype(BF16)
            unpick[g] = both.T.astype(BF16)
            return carry

        lax.fori_loop(0, 8, one, 0, unroll=True)

    def compact(r):
        for p, lo, size, col in spans(r):
            def one(g, carry, p=p, lo=lo, size=size, col=col):
                tokens = xs[p][g // 4, g % 4, :, :, :, lo : lo + size].reshape(GROUP, size)
                rows = jnp.dot(pick[g], tokens, preferred_element_type=F32).astype(BF16)
                for e in range(2):
                    packed[e, pl.ds(g * SLOTS, SLOTS), col : col + size] = rows[e * SLOTS : (e + 1) * SLOTS]
                return carry

            lax.fori_loop(0, 8, one, 0, unroll=True)

    def gate_up(r):
        def one(e, carry):
            depth = sum(size for p, lo, size, col in spans(r))
            total = jnp.dot(
                packed[e, :, :depth], wgu[r % 2, e, :depth, :], preferred_element_type=F32
            )
            if r > 0:
                total = total + acc[e]
            if r < len(AG_ROUNDS) - 1:
                acc[e] = total
            else:
                gate, up = total[:, :FF], total[:, FF:]
                hidden[e] = (gate / (1.0 + jnp.exp(-gate)) * up).astype(BF16)
            return carry

        lax.fori_loop(0, 2, one, 0, unroll=True)


    def out_cols(p, r):
        lo, size = RS_ROUNDS[r]
        if p == 0 and lo == 0:
            lo, size = GATES, size - GATES
        return lo, size

    def down(r):
        for p in PARTS:
            lo, size = out_cols(p, r)
            col = p * W + lo - GATES

            def product(e, carry, lo=lo, size=size, col=col):
                part = jnp.dot(hidden[e], wd[e, :, col : col + size], preferred_element_type=F32)
                packed[e, :, :size] = (part * row_gate[e, :, 0:1]).astype(BF16)
                return carry

            lax.fori_loop(0, 2, product, 0, unroll=True)

            def one(i, carry, p=p, lo=lo, size=size):
                g = (i + 4 * (1 - k)) % 8
                rows = jnp.concatenate(
                    [packed[e, pl.ds(g * SLOTS, SLOTS), :size] for e in range(2)], axis=0
                )
                tokens = jnp.dot(unpick[g], rows, preferred_element_type=F32).astype(BF16)
                xs[p][g // 4, g % 4, :, :, :, lo : lo + size] = tokens.reshape(4, 4, TOK, size)
                return carry

            lax.fori_loop(0, 4, one, 0, unroll=True)
            cols = (lo, size)
            send(at(xs[p], (1 - k,), cols, {}), at(rd[p], (), cols, {}), twin, qds.at[p, r], qdr.at[p, r])
            lax.fori_loop(4, 8, one, 0, unroll=True)

    def total_into(dst, refs):
        total = refs[0][...].astype(F32)
        for ref in refs[1:]:
            total = total + ref[...].astype(F32)
        dst[...] = total.astype(BF16)

    def unit_of(ref, lead, p, r, step, pieces=1, piece=0):
        a, b, c = ORDER[p]
        fix = {c: (me[c] + step) % 4}
        if pieces == 2:
            fix[b] = pl.ds(2 * piece, 2)
        elif pieces == 4:
            fix[b] = piece
        return at(ref, lead, out_cols(p, r), fix)

    def add_unit(p, r, step):
        def one(i, carry):
            mine = unit_of(xs[p], (k,), p, r, step, 4, i)
            total_into(mine, [mine, unit_of(rd[p], (), p, r, step, 4, i)])
            return carry

        lax.fori_loop(0, 4, one, 0, unroll=True)

    def piece_of(ref, lead, p, r, fix):
        a, b, c = ORDER[p]
        index = [fix.get(axis, slice(None)) for axis in "zyx" if axis != c]
        return ref.at[(*lead, *index, slice(None), pl.ds(*out_cols(p, r)))]

    def halves(p, half):
        return 2 * half

    def s1(r):
        for p in PARTS:
            cols = out_cols(p, r)
            wait(at(rd[p], (), cols, {}), qdr.at[p, r])
            add_unit(p, r, 2)
            c = ORDER[p][2]
            for half, way in ((0, 1), (1, -1)):
                src = unit_of(xs[p], (k,), p, r, 2, 2, half)
                send(src, half_slot(p, r, half), device(me, k, c, way), qfs.at[p, r], qfr.at[p, r, half])
            add_unit(p, r, 1)
            add_unit(p, r, -1)

    def half_slot(p, r, half, i=None):
        b = ORDER[p][1]
        fix = {} if i is None else {b: i}
        a, b, c = ORDER[p]
        index = [fix.get(axis, slice(None)) for axis in "zyx" if axis != c]
        return rf[p].at[(half, *index, slice(None), pl.ds(*out_cols(p, r)))]

    def s2(r):
        for p in PARTS:
            c = ORDER[p][2]
            for half, way in ((0, 1), (1, -1)):
                wait(half_slot(p, r, half), qfr.at[p, r, half])

                def one(i, carry, half=half, way=way):
                    mine = unit_of(xs[p], (k,), p, r, way, 4, 2 * half + i)
                    total_into(mine, [mine, half_slot(p, r, half, i)])
                    return carry

                lax.fori_loop(0, 2, one, 0, unroll=True)
                src = unit_of(xs[p], (k,), p, r, way)
                slot = piece_of(rr[p], (half,), p, r, {})
                send(src, slot, device(me, k, c, way), q3s.at[p, r], q3r.at[p, r])
            add_unit(p, r, 0)

    def s3(r):
        for p in PARTS:
            a, b, c = ORDER[p]
            wait(piece_of(rr[p], (slice(None),), p, r, {}), q3r.at[p, r])

            def one(i, carry, b=b):
                mine = unit_of(xs[p], (k,), p, r, 0, 4, i)
                total_into(mine, [mine] + [piece_of(rr[p], (h,), p, r, {b: i}) for h in range(2)])
                return carry

            lax.fori_loop(0, 4, one, 0, unroll=True)
            for step in (2, 1, 3):
                src = unit_of(xs[p], (k,), p, r, 0, 4, (me[b] + step) % 4)
                slot = rb[p].at[step - 1, :, :, pl.ds(*out_cols(p, r))]
                send(src, slot, device(me, k, b, step), q2s.at[p, r], q2r.at[p, r])

    def s4(r):
        for p in PARTS:
            a, b, c = ORDER[p]
            cols = pl.ds(*out_cols(p, r))
            wait(rb[p].at[:, :, :, cols], q2r.at[p, r])
            mine = unit_of(xs[p], (k,), p, r, 0, 4, me[b])
            total_into(mine, [mine] + [rb[p].at[j, :, :, cols] for j in range(3)])
            for step in (2, 1, 3):
                src = at(xs[p], (k,), out_cols(p, r), {**me, a: (me[a] + step) % 4})
                send(src, ra[p].at[step - 1, :, cols], device(me, k, a, step), q1s.at[p, r], q1r.at[p, r])

    def s5(r):
        for p in PARTS:
            lo, size = out_cols(p, r)
            cols = pl.ds(lo, size)
            wait(ra[p].at[:, :, cols], q1r.at[p, r])
            total = at(xs[p], (k,), (lo, size), me)[...].astype(F32)
            for j in range(3):
                total = total + ra[p][j, :, cols].astype(F32)
            col = p * W + lo - GATES
            span = slice(col, col + size)
            out_ref[:, span] = (mixed_ref[:, span].astype(F32) + total).astype(BF16)


    for p in PARTS:
        p1_start(p)
    for p in PARTS:
        p1_wait(p)
        for r in range(3):
            p2_start(p, r)
    p3_start(0)
    p3_start(1)
    p3_forward(0)
    p3_start(2)
    p3_finish(0)
    twin_wait(0)
    selections()
    p3_forward(1)
    compact(0)
    weights_wait(0)
    gate_up(0)
    weights_start(2)
    p3_finish(1)
    p3_forward(2)
    twin_wait(1)
    compact(1)
    weights_wait(1)
    gate_up(1)
    p3_finish(2)
    twin_wait(2)
    compact(2)
    weights_wait(2)
    gate_up(2)
    load_down.wait()
    for p in PARTS:
        wait(xs[p].at[0, 0, 0, pl.ds(0, 3)], p1s.at[p])
        for r in range(3):
            cols = pl.ds(*AG_ROUNDS[r])
            wait(p2_bytes(p, r), p2s.at[p, r])
            wait(xs[p].at[0, pl.ds(0, 3), :, :, :, cols], p3s.at[p, r])
            wait(xs[p].at[0, :, :, :, :, cols], ds.at[p, r])
    down(0)
    s1(0)
    down(1)
    s2(0)
    s1(1)
    down(2)
    s2(1)
    s1(2)
    s3(0)
    s2(2)
    s4(0)
    s3(1)
    s5(0)
    s4(1)
    s3(2)
    s5(1)
    s4(2)
    s5(2)
    for p in PARTS:
        for r in range(3):
            cols = pl.ds(*out_cols(p, r))
            wait(xs[p].at[0, :, :, :, :, cols], qds.at[p, r])
            wait(rf[p].at[:, :, :, :, cols], qfs.at[p, r])
            wait(rr[p].at[:, :, :, :, cols], q3s.at[p, r])
            wait(rb[p].at[:, :, :, cols], q2s.at[p, r])
            wait(ra[p].at[:, :, cols], q1s.at[p, r])


def experts(rows, mixed, w_gate, w_up, w_down):
    vmem = pl.BlockSpec(memory_space=pltpu.VMEM)
    hbm = pl.BlockSpec(memory_space=pl.ANY)
    dma = pltpu.SemaphoreType.DMA

    def half_shape(p):
        a, b, c = ORDER[p]
        return (2, *[2 if axis == b else 4 for axis in "zyx" if axis != c], TOK, W)

    scratch = (
        [pltpu.VMEM((2, 4, 4, 4, TOK, W), BF16)] * 3
        + [pltpu.VMEM((4, 4, 4, TOK, W), BF16)] * 3
        + [pltpu.VMEM(half_shape(p), BF16) for p in PARTS]
        + [pltpu.VMEM((2, 4, 4, TOK, W), BF16)] * 3
        + [pltpu.VMEM((3, 4, TOK, W), BF16)] * 3
        + [pltpu.VMEM((3, TOK, W), BF16)] * 3
        + [
            pltpu.VMEM((2, 2, 1536, 2 * FF), BF16),
            pltpu.VMEM((2, FF, D), BF16),
            pltpu.VMEM((2, 8 * SLOTS, 1536), BF16),
            pltpu.VMEM((2, 8 * SLOTS, 2 * FF), F32),
            pltpu.VMEM((2, 8 * SLOTS, FF), BF16),
            pltpu.VMEM((8, 2 * SLOTS, GROUP), BF16),
            pltpu.VMEM((8, GROUP, 2 * SLOTS), BF16),
            pltpu.VMEM((2, 8 * SLOTS, 128), F32),
        ]
        + [dma((4,)), dma((3,)), dma((3,)), dma((3, 3)), dma((3, 3)), dma((3, 3)), dma((3, 3, 3)), dma((3, 3)), dma((3, 3))]
        + [dma((3, 3)), dma((3, 3)), dma((3, 3)), dma((3, 3, 2))]
        + [dma((3, 3))] * 6
    )
    return pl.pallas_call(
        expert_kernel,
        out_shape=jax.ShapeDtypeStruct((TOK, D), BF16),
        in_specs=[vmem, vmem, hbm, hbm, hbm],
        out_specs=vmem,
        scratch_shapes=scratch,
        compiler_params=pltpu.CompilerParams(
            collective_id=1, has_side_effects=True, vmem_limit_bytes=VMEM
        ),
    )(rows, mixed, w_gate, w_up, w_down)


def on_device(
    query_rows,
    key_rows,
    value_rows,
    residual,
    out_proj,
    post_gain,
    router,
    routes,
    w_gate,
    w_up,
    w_down,
):
    rows, mixed = front(
        query_rows, key_rows, value_rows, residual, out_proj, post_gain, router, routes
    )
    return experts(rows, mixed, w_gate, w_up, w_down)[None]


def solution(mesh):
    in_specs = (
        P("dp", "ctx", "tensor"),
        P("dp", "ctx", None),
        P("dp", "ctx", None),
        P("dp", ("ctx", "tensor"), None),
        P("tensor", None),
        P(),
        P(),
        P("dp", ("ctx", "tensor"), None),
        P(("ctx", "tensor"), None, "dp"),
        P(("ctx", "tensor"), None, "dp"),
        P(("ctx", "tensor"), "dp", None),
    )
    out_specs = P("dp", ("ctx", "tensor"), None)
    return jax.shard_map(
        on_device, mesh=mesh, in_specs=in_specs, out_specs=out_specs, check_vma=False
    )
```

```python
import jax
import jax.numpy as jnp
import numpy as np
from jax import lax
from jax.experimental import pallas as pl
from jax.experimental.pallas import tpu as pltpu
from jax.sharding import PartitionSpec as P

MESH = pl.DeviceIdType.MESH
F32 = jnp.float32
BF16 = jnp.bfloat16

D = 4096
HEAD = 128
HEADS = 4
SEQ = 512
LOCAL = 128
TOK = 16
EXPERTS = 64
FF = 384
CAP = 4
GATES = 128
WIDE = D + GATES
W = WIDE // 3
GROUP = 256
SLOTS = TOK * CAP

ORDER = (("x", "y", "z"), ("y", "z", "x"), ("z", "x", "y"))
PARTS = range(3)
AG_ROUNDS = ((0, 512), (512, 512), (1024, 384))
RS_ROUNDS = ((0, 384), (384, 512), (896, 512))
VMEM = 63 * 2**20


def rope_tables():
    half = HEAD // 2
    places = np.arange(SEQ).astype(np.float32)
    freqs = np.power(
        np.float32(1000000.0), -(np.arange(half).astype(np.float32) * np.float32(2.0) / np.float32(HEAD))
    ).astype(np.float32)
    angles = (places[:, None] * freqs[None, :]).astype(np.float32)
    cosine, sine = np.cos(angles), np.sin(angles)
    return (
        np.concatenate([cosine, cosine], axis=1).astype(np.float32),
        np.concatenate([-sine, sine], axis=1).astype(np.float32),
    )


def place():
    t = lax.axis_index("tensor")
    return {"x": t // 2, "y": lax.axis_index("ctx"), "z": lax.axis_index("dp")}, t % 2


def device(me, k, axis, step):
    value = (me[axis] + step) % 4
    if axis == "x":
        return {"tensor": value * 2 + k}
    return {"ctx" if axis == "y" else "dp": value}


def sibling(me, k):
    return {"tensor": me["x"] * 2 + 1 - k}


def greet(me, k, axes):
    barrier = pltpu.get_barrier_semaphore()
    for axis in axes:
        for step in (1, 2, 3):
            pl.semaphore_signal(
                barrier, inc=1, device_id=device(me, k, axis, step), device_id_type=MESH
            )
    pl.semaphore_signal(barrier, inc=1, device_id=sibling(me, k), device_id_type=MESH)
    pl.semaphore_wait(barrier, 3 * len(axes) + 1)


def send(src, dst, to, send_sem, recv_sem):
    pltpu.make_async_remote_copy(
        src_ref=src,
        dst_ref=dst,
        send_sem=send_sem,
        recv_sem=recv_sem,
        device_id=to,
        device_id_type=MESH,
    ).start()


def wait(ref, sem):
    pltpu.make_async_copy(ref, ref, sem).wait()


def turn(values, cosine, sine):
    values = values.astype(F32)
    return (values * cosine + pltpu.roll(values, HEAD // 2, 1) * sine).astype(BF16)


def layer_kernel(
    query_hbm, key_hbm, value_hbm, residual_hbm, proj_hbm, gain_hbm, router_hbm, routes_hbm,
    cos_hbm, sin_hbm, gate_hbm, up_hbm, down_hbm, out_ref,
    query, residual, gain, router, routes, cosine, sine,
    kv, qrot, krot, far, from_sibling, from_ring, mixed,
    x0, x1, x2, rd0, rd1, rd2, rf0, rf1, rf2, rr0, rr1, rr2, rb0, rb1, rb2, ra0, ra1, ra2,
    wgu, wd, packed, acc, hidden, pick, unpick, row_gate,
    in_sem, kv_send, kv_recv, sib_send, sib_recv, ring_send, ring_recv,
    w_sem, p1s, p1r, p2s, p2r, p3s, p3r, ds, dr,
    qds, qdr, qfs, qfr, q3s, q3r, q2s, q2r, q1s, q1r,
):
    xs, rd, rf, rr = (x0, x1, x2), (rd0, rd1, rd2), (rf0, rf1, rf2), (rr0, rr1, rr2)
    rb, ra = (rb0, rb1, rb2), (ra0, ra1, ra2)
    me, k = place()
    twin = sibling(me, k)

    def spans(r):
        found, at_col = [], 0
        for p in PARTS:
            lo, size = AG_ROUNDS[r]
            if p == 0 and lo == 0:
                lo, size = GATES, size - GATES
            found.append((p, lo, size, at_col))
            at_col += size
        return found

    def weights(r):
        copies = []
        for e in range(2):
            for n, hbm in enumerate((gate_hbm, up_hbm)):
                for p, lo, size, col in spans(r):
                    from_row = p * W + lo - GATES
                    copies.append(
                        pltpu.make_async_copy(
                            hbm.at[e, pl.ds(from_row, size), :],
                            wgu.at[r % 2, e, pl.ds(col, size), pl.ds(n * FF, FF)],
                            w_sem.at[r],
                        )
                    )
        return copies

    def weights_start(r):
        for copy in weights(r):
            copy.start()

    def weights_wait(r):
        total = sum(size for p, lo, size, col in spans(r))
        wait(wgu.at[r % 2, :, pl.ds(0, total), :], w_sem.at[r])

    load_down = pltpu.make_async_copy(down_hbm, wd, w_sem.at[3])


    head = pl.multiple_of((lax.axis_index("tensor") // 4) * HEAD, HEAD)
    y = me["y"]
    loads = [
        pltpu.make_async_copy(src, dst, in_sem.at[i])
        for i, (src, dst) in enumerate(
            (
                (key_hbm.at[0, :, pl.ds(head, HEAD)], kv.at[y, 0]),
                (value_hbm.at[0, :, pl.ds(head, HEAD)], kv.at[y, 1]),
                (query_hbm.at[0], query),
                (cos_hbm, cosine),
                (sin_hbm, sine),
                (proj_hbm.at[pl.ds(0, FF)], wd.at[0]),
                (proj_hbm.at[pl.ds(FF, HEADS * HEAD - FF)], wd.at[1, pl.ds(0, HEADS * HEAD - FF)]),
                (residual_hbm.at[0], residual),
                (gain_hbm, gain),
                (router_hbm, router),
                (routes_hbm.at[0], routes),
            )
        )
    ]
    for load in loads:
        load.start()
    weights_start(0)
    weights_start(1)
    greet(me, k, "xyz")
    for load in loads[:2]:
        load.wait()
    for step in (2, 1, 3):
        send(kv.at[y], kv.at[y], device(me, k, "y", step), kv_send, kv_recv)
    for load in loads[2:5]:
        load.wait()
    own = pl.ds(pl.multiple_of(y * LOCAL, LOCAL), LOCAL)
    for h in range(HEADS):
        qrot[pl.ds(h * LOCAL, LOCAL), :] = turn(
            query[:, h * HEAD : (h + 1) * HEAD], cosine[own, :], sine[own, :]
        )
    wait(kv.at[pl.ds(0, 3)], kv_recv)
    for c in range(4):
        span = pl.ds(c * LOCAL, LOCAL)
        krot[span, :] = turn(kv[c, 0], cosine[span, :], sine[span, :])
    values = kv[:, 1].reshape(SEQ, HEAD)
    place_q = y * LOCAL + lax.broadcasted_iota(jnp.int32, (LOCAL, SEQ), 0)
    causal = place_q >= lax.broadcasted_iota(jnp.int32, (LOCAL, SEQ), 1)
    attended = []
    for h in range(HEADS):
        score = lax.dot_general(
            qrot[pl.ds(h * LOCAL, LOCAL), :], krot[...], (((1,), (1,)), ((), ())),
            preferred_element_type=F32,
        ) / jnp.sqrt(F32(HEAD))
        score = jnp.where(causal, score, F32(-1e30))
        peak = jnp.max(score, axis=-1, keepdims=True)
        expon = jnp.where(causal, jnp.exp(score - peak), F32(0.0))
        total = jnp.sum(expon, axis=-1, keepdims=True)
        summed = jnp.dot(expon.astype(BF16), values, preferred_element_type=F32)
        attended.append((summed / total).astype(BF16))
    attended = jnp.concatenate(attended, axis=1)
    for load in loads[5:]:
        load.wait()
    for c in range(8):
        cols = slice(c * 512, (c + 1) * 512)
        out = jnp.dot(attended[:, :FF], wd[0, :, cols], preferred_element_type=F32) + jnp.dot(
            attended[:, FF:], wd[1, : HEADS * HEAD - FF, cols], preferred_element_type=F32
        )
        acc[c // 4, pl.ds((c % 4) * LOCAL, LOCAL), :512] = out
        for v in range(4):
            rows = pl.ds(pl.multiple_of((c % 4) * LOCAL + (2 * v + 1 - k) * TOK, TOK), TOK)
            far[v, :, cols] = acc[c // 4, rows, :512].astype(BF16)
        if c % 4 == 3:
            half = pl.ds((c // 4) * 2048, 2048)
            send(
                far.at[:, :, half], from_sibling.at[:, :, half], twin,
                sib_send.at[c // 4], sib_recv.at[c // 4],
            )
    load_down.start()

    def chip_sum(v, c):
        rows = pl.ds(pl.multiple_of((c % 4) * LOCAL + (2 * v + k) * TOK, TOK), TOK)
        return acc[c // 4, rows, :512] + from_sibling[v, :, c * 512 : (c + 1) * 512].astype(F32)

    for i in range(2):
        half = pl.ds(i * 2048, 2048)
        wait(far.at[:, :, half], sib_send.at[i])
        wait(from_sibling.at[:, :, half], sib_recv.at[i])
        for step in (2, 1, 3):
            v = (me["x"] + step) % 4
            for c in range(4 * i, 4 * i + 4):
                far[v, :, c * 512 : (c + 1) * 512] = chip_sum(v, c).astype(BF16)
            send(
                far.at[v, :, half], from_ring.at[step - 1, :, half], device(me, k, "x", step),
                ring_send.at[i], ring_recv.at[i],
            )
    square = jnp.zeros((TOK, 1), F32)
    for c in range(8):
        cols = slice(c * 512, (c + 1) * 512)
        if c % 4 == 0:
            wait(from_ring.at[:, :, pl.ds((c // 4) * 2048, 2048)], ring_recv.at[c // 4])
        projected = chip_sum(me["x"], c)
        for j in range(3):
            projected = projected + from_ring[j, :, cols].astype(F32)
        wide = (residual[:, cols].astype(F32) + projected).astype(BF16)
        mixed[:, cols] = wide
        wide = wide.astype(F32)
        square = square + jnp.sum(wide * wide, axis=-1, keepdims=True)
    scale = lax.rsqrt(square / D + 1e-06)
    for c in range(D // 128):
        wide = mixed[:, c * 128 : (c + 1) * 128].astype(F32)
        normed = (wide * scale * gain[c : c + 1, :].astype(F32)).astype(BF16)
        col = GATES + c * 128
        xs[col // W][k, me["z"], me["y"], me["x"], :, col % W : col % W + 128] = normed
    def at(ref, lead, cols, fix):
        index = [fix.get(axis, slice(None)) for axis in "zyx"]
        return ref.at[(*lead, *index, slice(None), pl.ds(*cols))]


    def p1_start(p):
        a = ORDER[p][0]
        block = at(xs[p], (k,), (0, W), me)
        for step in (2, 1, 3):
            send(block, block, device(me, k, a, step), p1s.at[p], p1r.at[p])

    def p1_wait(p):
        wait(xs[p].at[0, 0, 0, pl.ds(0, 3)], p1r.at[p])

    def p2_start(p, r):
        a, b, c = ORDER[p]
        unit = at(xs[p], (k,), AG_ROUNDS[r], {b: me[b], c: me[c]})
        for step in (2, 1, 3):
            send(unit, unit, device(me, k, b, step), p2s.at[p, r], p2r.at[p, r])

    def p2_bytes(p, r):
        return xs[p].at[0, 0, pl.ds(0, 3), :, :, pl.ds(*AG_ROUNDS[r])]

    def p3_unit(p, r, step, half=None):
        a, b, c = ORDER[p]
        fix = {c: (me[c] + step) % 4}
        if half is not None:
            fix[b] = pl.ds(2 * half, 2)
        return at(xs[p], (k,), AG_ROUNDS[r], fix)

    def p3_send(p, r, step, half, way):
        unit = p3_unit(p, r, step, half)
        recv = p3r.at[p, r, 2] if half is not None else p3r.at[p, r, 0 if way == 1 else 1]
        send(unit, unit, device(me, k, ORDER[p][2], way), p3s.at[p, r], recv)

    def twin_send(p, r, step):
        unit = p3_unit(p, r, step)
        send(unit, unit, twin, ds.at[p, r], dr.at[p, r])

    def p3_start(r):
        for p in PARTS:
            wait(p2_bytes(p, r), p2r.at[p, r])
            p3_send(p, r, 0, None, 1)
            p3_send(p, r, 0, None, -1)

    def p3_forward(r):
        for p in PARTS:
            wait(p3_unit(p, r, -1), p3r.at[p, r, 0])
            p3_send(p, r, -1, 0, 1)
            wait(p3_unit(p, r, 1), p3r.at[p, r, 1])
            p3_send(p, r, 1, 1, -1)
        for p in PARTS:
            for step in (0, -1, 1):
                twin_send(p, r, step)

    def p3_finish(r):
        for p in PARTS:
            wait(p3_unit(p, r, 2), p3r.at[p, r, 2])
            twin_send(p, r, 2)

    def twin_wait(r):
        for p in PARTS:
            wait(xs[p].at[1 - k, :, :, :, :, pl.ds(*AG_ROUNDS[r])], dr.at[p, r])

    def gates():
        logits = jnp.zeros((EXPERTS, TOK), F32)
        for p in PARTS:
            lo = GATES if p == 0 else 0
            col = p * W + lo - GATES
            normed = xs[p][k, me["z"], me["y"], me["x"], :, lo:W]
            logits = logits + lax.dot_general(
                router[:, col : col + W - lo], normed, (((1,), (1,)), ((), ())),
                preferred_element_type=F32,
            )
        expert = lax.broadcasted_iota(jnp.int32, (EXPERTS, TOK), 0)
        chosen = expert == routes[0:1, :]
        for j in range(1, 8):
            chosen = jnp.logical_or(chosen, expert == routes[j : j + 1, :])
        peak = jnp.max(jnp.where(chosen, logits, F32(-3e38)), axis=0, keepdims=True)
        expon = jnp.where(chosen, jnp.exp(logits - peak), F32(0.0))
        gate = expon / jnp.sum(expon, axis=0, keepdims=True)
        high = gate.astype(BF16).astype(F32)
        both = jnp.concatenate([high, gate - high], axis=0).astype(BF16)
        unit = lax.broadcasted_iota(jnp.int32, (TOK, TOK), 0) == lax.broadcasted_iota(
            jnp.int32, (TOK, TOK), 1
        )
        turned = lax.dot_general(
            unit.astype(F32).astype(BF16), both, (((1,), (1,)), ((), ())), preferred_element_type=F32
        )
        x0[k, me["z"], me["y"], me["x"], :, :GATES] = turned.astype(BF16)


    def selections():
        first = 2 * (me["y"] * 8 + lax.axis_index("tensor"))
        rows = lax.broadcasted_iota(jnp.int32, (8, GATES), 0)
        lanes = lax.broadcasted_iota(jnp.int32, (8, GATES), 1)
        mine = jnp.logical_and(lanes % EXPERTS == first + rows, rows < 2).astype(F32).astype(BF16)
        s = lax.broadcasted_iota(jnp.int32, (GROUP, GROUP), 0)
        u = lax.broadcasted_iota(jnp.int32, (GROUP, GROUP), 1)
        earlier = jnp.logical_and(s // TOK == u // TOK, s < u).astype(F32).astype(BF16)
        base = (lax.broadcasted_iota(jnp.int32, (1, GROUP), 1) // TOK * CAP).astype(F32)
        slots = lax.broadcasted_iota(jnp.int32, (SLOTS, GROUP), 0).astype(F32)

        def one(g, carry):
            tile = x0[g // 4, g % 4, :, :, :, :GATES].reshape(GROUP, GATES)
            gate = lax.dot_general(mine, tile, (((1,), (1,)), ((), ())), preferred_element_type=F32)
            named = (gate > 0).astype(F32)
            rank = jnp.dot(named.astype(BF16), earlier, preferred_element_type=F32)
            both = []
            for e in range(2):
                hit = jnp.logical_and(slots == rank[e : e + 1] + base, gate[e : e + 1] > 0).astype(F32)
                worth = jnp.sum(hit * gate[e : e + 1], axis=1, keepdims=True)
                row_gate[e, pl.ds(g * SLOTS, SLOTS), :] = jnp.broadcast_to(worth, (SLOTS, 128))
                both.append(hit)
            both = jnp.concatenate(both, axis=0)
            pick[g] = both.astype(BF16)
            unpick[g] = both.T.astype(BF16)
            return carry

        lax.fori_loop(0, 8, one, 0, unroll=True)

    def compact(r):
        for p, lo, size, col in spans(r):
            def one(g, carry, p=p, lo=lo, size=size, col=col):
                tokens = xs[p][g // 4, g % 4, :, :, :, lo : lo + size].reshape(GROUP, size)
                rows = jnp.dot(pick[g], tokens, preferred_element_type=F32).astype(BF16)
                for e in range(2):
                    packed[e, pl.ds(g * SLOTS, SLOTS), col : col + size] = rows[e * SLOTS : (e + 1) * SLOTS]
                return carry

            lax.fori_loop(0, 8, one, 0, unroll=True)

    def gate_up(r):
        def one(e, carry):
            depth = sum(size for p, lo, size, col in spans(r))
            total = jnp.dot(
                packed[e, :, :depth], wgu[r % 2, e, :depth, :], preferred_element_type=F32
            )
            if r > 0:
                total = total + acc[e]
            if r < len(AG_ROUNDS) - 1:
                acc[e] = total
            else:
                gate, up = total[:, :FF], total[:, FF:]
                hidden[e] = (gate / (1.0 + jnp.exp(-gate)) * up).astype(BF16)
            return carry

        lax.fori_loop(0, 2, one, 0, unroll=True)


    def out_cols(p, r):
        lo, size = RS_ROUNDS[r]
        if p == 0 and lo == 0:
            lo, size = GATES, size - GATES
        return lo, size

    def down(r):
        for p in PARTS:
            lo, size = out_cols(p, r)
            col = p * W + lo - GATES

            def product(e, carry, lo=lo, size=size, col=col):
                part = jnp.dot(hidden[e], wd[e, :, col : col + size], preferred_element_type=F32)
                packed[e, :, :size] = (part * row_gate[e, :, 0:1]).astype(BF16)
                return carry

            lax.fori_loop(0, 2, product, 0, unroll=True)

            def one(i, carry, p=p, lo=lo, size=size):
                g = (i + 4 * (1 - k)) % 8
                rows = jnp.concatenate(
                    [packed[e, pl.ds(g * SLOTS, SLOTS), :size] for e in range(2)], axis=0
                )
                tokens = jnp.dot(unpick[g], rows, preferred_element_type=F32).astype(BF16)
                xs[p][g // 4, g % 4, :, :, :, lo : lo + size] = tokens.reshape(4, 4, TOK, size)
                return carry

            lax.fori_loop(0, 4, one, 0, unroll=True)
            cols = (lo, size)
            send(at(xs[p], (1 - k,), cols, {}), at(rd[p], (), cols, {}), twin, qds.at[p, r], qdr.at[p, r])
            lax.fori_loop(4, 8, one, 0, unroll=True)

    def total_into(dst, refs):
        total = refs[0][...].astype(F32)
        for ref in refs[1:]:
            total = total + ref[...].astype(F32)
        dst[...] = total.astype(BF16)

    def unit_of(ref, lead, p, r, step, pieces=1, piece=0):
        a, b, c = ORDER[p]
        fix = {c: (me[c] + step) % 4}
        if pieces == 2:
            fix[b] = pl.ds(2 * piece, 2)
        elif pieces == 4:
            fix[b] = piece
        return at(ref, lead, out_cols(p, r), fix)

    def add_unit(p, r, step):
        def one(i, carry):
            mine = unit_of(xs[p], (k,), p, r, step, 4, i)
            total_into(mine, [mine, unit_of(rd[p], (), p, r, step, 4, i)])
            return carry

        lax.fori_loop(0, 4, one, 0, unroll=True)

    def piece_of(ref, lead, p, r, fix):
        a, b, c = ORDER[p]
        index = [fix.get(axis, slice(None)) for axis in "zyx" if axis != c]
        return ref.at[(*lead, *index, slice(None), pl.ds(*out_cols(p, r)))]

    def halves(p, half):
        return 2 * half

    def s1(r):
        for p in PARTS:
            cols = out_cols(p, r)
            wait(at(rd[p], (), cols, {}), qdr.at[p, r])
            add_unit(p, r, 2)
            c = ORDER[p][2]
            for half, way in ((0, 1), (1, -1)):
                src = unit_of(xs[p], (k,), p, r, 2, 2, half)
                send(src, half_slot(p, r, half), device(me, k, c, way), qfs.at[p, r], qfr.at[p, r, half])
            add_unit(p, r, 1)
            add_unit(p, r, -1)

    def half_slot(p, r, half, i=None):
        b = ORDER[p][1]
        fix = {} if i is None else {b: i}
        a, b, c = ORDER[p]
        index = [fix.get(axis, slice(None)) for axis in "zyx" if axis != c]
        return rf[p].at[(half, *index, slice(None), pl.ds(*out_cols(p, r)))]

    def s2(r):
        for p in PARTS:
            c = ORDER[p][2]
            for half, way in ((0, 1), (1, -1)):
                wait(half_slot(p, r, half), qfr.at[p, r, half])

                def one(i, carry, half=half, way=way):
                    mine = unit_of(xs[p], (k,), p, r, way, 4, 2 * half + i)
                    total_into(mine, [mine, half_slot(p, r, half, i)])
                    return carry

                lax.fori_loop(0, 2, one, 0, unroll=True)
                src = unit_of(xs[p], (k,), p, r, way)
                slot = piece_of(rr[p], (half,), p, r, {})
                send(src, slot, device(me, k, c, way), q3s.at[p, r], q3r.at[p, r])
            add_unit(p, r, 0)

    def s3(r):
        for p in PARTS:
            a, b, c = ORDER[p]
            wait(piece_of(rr[p], (slice(None),), p, r, {}), q3r.at[p, r])

            def one(i, carry, b=b):
                mine = unit_of(xs[p], (k,), p, r, 0, 4, i)
                total_into(mine, [mine] + [piece_of(rr[p], (h,), p, r, {b: i}) for h in range(2)])
                return carry

            lax.fori_loop(0, 4, one, 0, unroll=True)
            for step in (2, 1, 3):
                src = unit_of(xs[p], (k,), p, r, 0, 4, (me[b] + step) % 4)
                slot = rb[p].at[step - 1, :, :, pl.ds(*out_cols(p, r))]
                send(src, slot, device(me, k, b, step), q2s.at[p, r], q2r.at[p, r])

    def s4(r):
        for p in PARTS:
            a, b, c = ORDER[p]
            cols = pl.ds(*out_cols(p, r))
            wait(rb[p].at[:, :, :, cols], q2r.at[p, r])
            mine = unit_of(xs[p], (k,), p, r, 0, 4, me[b])
            total_into(mine, [mine] + [rb[p].at[j, :, :, cols] for j in range(3)])
            for step in (2, 1, 3):
                src = at(xs[p], (k,), out_cols(p, r), {**me, a: (me[a] + step) % 4})
                send(src, ra[p].at[step - 1, :, cols], device(me, k, a, step), q1s.at[p, r], q1r.at[p, r])

    def s5(r):
        for p in PARTS:
            lo, size = out_cols(p, r)
            cols = pl.ds(lo, size)
            wait(ra[p].at[:, :, cols], q1r.at[p, r])
            total = at(xs[p], (k,), (lo, size), me)[...].astype(F32)
            for j in range(3):
                total = total + ra[p][j, :, cols].astype(F32)
            col = p * W + lo - GATES
            span = slice(col, col + size)
            out_ref[:, span] = (mixed[:, span].astype(F32) + total).astype(BF16)


    p1_start(1)
    p1_start(2)
    gates()
    p1_start(0)
    for p in (1, 2, 0):
        p1_wait(p)
        for r in range(3):
            p2_start(p, r)
    p3_start(0)
    p3_start(1)
    p3_forward(0)
    p3_start(2)
    p3_finish(0)
    twin_wait(0)
    selections()
    p3_forward(1)
    compact(0)
    weights_wait(0)
    gate_up(0)
    weights_start(2)
    p3_finish(1)
    p3_forward(2)
    twin_wait(1)
    compact(1)
    weights_wait(1)
    gate_up(1)
    p3_finish(2)
    twin_wait(2)
    compact(2)
    weights_wait(2)
    gate_up(2)
    load_down.wait()
    for p in PARTS:
        wait(xs[p].at[0, 0, 0, pl.ds(0, 3)], p1s.at[p])
        for r in range(3):
            cols = pl.ds(*AG_ROUNDS[r])
            wait(p2_bytes(p, r), p2s.at[p, r])
            wait(xs[p].at[0, pl.ds(0, 3), :, :, :, cols], p3s.at[p, r])
            wait(xs[p].at[0, :, :, :, :, cols], ds.at[p, r])
    down(0)
    down(1)
    s1(0)
    down(2)
    s1(1)
    s2(0)
    s1(2)
    s2(1)
    s3(0)
    s2(2)
    s4(0)
    s3(1)
    s5(0)
    s4(1)
    s3(2)
    s5(1)
    s4(2)
    s5(2)
    wait(kv.at[pl.ds(0, 3)], kv_send)
    for i in range(2):
        wait(from_ring.at[:, :, pl.ds(i * 2048, 2048)], ring_send.at[i])
    for p in PARTS:
        for r in range(3):
            cols = pl.ds(*out_cols(p, r))
            wait(xs[p].at[0, :, :, :, :, cols], qds.at[p, r])
            wait(rf[p].at[:, :, :, :, cols], qfs.at[p, r])
            wait(rr[p].at[:, :, :, :, cols], q3s.at[p, r])
            wait(rb[p].at[:, :, :, cols], q2s.at[p, r])
            wait(ra[p].at[:, :, cols], q1s.at[p, r])


def on_device(
    query_rows,
    key_rows,
    value_rows,
    residual,
    out_proj,
    post_gain,
    router,
    routes,
    w_gate,
    w_up,
    w_down,
):
    vmem = pltpu.VMEM
    hbm = pl.BlockSpec(memory_space=pl.ANY)
    dma = pltpu.SemaphoreType.DMA
    cosine, sine = rope_tables()

    def half_shape(p):
        a, b, c = ORDER[p]
        return (2, *[2 if axis == b else 4 for axis in "zyx" if axis != c], TOK, W)

    scratch = (
        [
            vmem((LOCAL, HEADS * HEAD), BF16),
            vmem((TOK, D), BF16),
            vmem((D // 128, 128), BF16),
            vmem((EXPERTS, D), BF16),
            vmem((8, TOK), jnp.int32),
            vmem((SEQ, HEAD), F32),
            vmem((SEQ, HEAD), F32),
            vmem((4, 2, LOCAL, HEAD), BF16),
            vmem((HEADS * LOCAL, HEAD), BF16),
            vmem((SEQ, HEAD), BF16),
            vmem((4, TOK, D), BF16),
            vmem((4, TOK, D), BF16),
            vmem((3, TOK, D), BF16),
            vmem((TOK, D), BF16),
        ]
        + [vmem((2, 4, 4, 4, TOK, W), BF16)] * 3
        + [vmem((4, 4, 4, TOK, W), BF16)] * 3
        + [vmem(half_shape(p), BF16) for p in PARTS]
        + [vmem((2, 4, 4, TOK, W), BF16)] * 3
        + [vmem((3, 4, TOK, W), BF16)] * 3
        + [vmem((3, TOK, W), BF16)] * 3
        + [
            vmem((2, 2, 1536, 2 * FF), BF16),
            vmem((2, FF, D), BF16),
            vmem((2, 8 * SLOTS, 1536), BF16),
            vmem((2, 8 * SLOTS, 2 * FF), F32),
            vmem((2, 8 * SLOTS, FF), BF16),
            vmem((8, 2 * SLOTS, GROUP), BF16),
            vmem((8, GROUP, 2 * SLOTS), BF16),
            vmem((2, 8 * SLOTS, 128), F32),
        ]
        + [dma((11,)), dma, dma, dma((2,)), dma((2,)), dma((2,)), dma((2,))]
        + [dma((4,)), dma((3,)), dma((3,)), dma((3, 3)), dma((3, 3)), dma((3, 3)), dma((3, 3, 3))]
        + [dma((3, 3)), dma((3, 3))]
        + [dma((3, 3)), dma((3, 3)), dma((3, 3)), dma((3, 3, 2))]
        + [dma((3, 3))] * 6
    )
    out = pl.pallas_call(
        layer_kernel,
        out_shape=jax.ShapeDtypeStruct((TOK, D), BF16),
        in_specs=[hbm] * 13,
        out_specs=pl.BlockSpec(memory_space=pltpu.VMEM),
        scratch_shapes=scratch,
        compiler_params=pltpu.CompilerParams(
            collective_id=0, has_side_effects=True, vmem_limit_bytes=VMEM
        ),
    )(
        query_rows, key_rows, value_rows, residual, out_proj, post_gain.reshape(D // 128, 128),
        router.T, jnp.swapaxes(routes, 1, 2), jnp.asarray(cosine), jnp.asarray(sine),
        w_gate, w_up, w_down,
    )
    return out[None]


def solution(mesh):
    in_specs = (
        P("dp", "ctx", "tensor"),
        P("dp", "ctx", None),
        P("dp", "ctx", None),
        P("dp", ("ctx", "tensor"), None),
        P("tensor", None),
        P(),
        P(),
        P("dp", ("ctx", "tensor"), None),
        P(("ctx", "tensor"), None, "dp"),
        P(("ctx", "tensor"), None, "dp"),
        P(("ctx", "tensor"), "dp", None),
    )
    out_specs = P("dp", ("ctx", "tensor"), None)
    return jax.shard_map(
        on_device, mesh=mesh, in_specs=in_specs, out_specs=out_specs, check_vma=False
    )
```

```python
import jax
import jax.numpy as jnp
import numpy as np
from jax import lax
from jax.experimental import pallas as pl
from jax.experimental.pallas import tpu as pltpu
from jax.sharding import PartitionSpec as P

MESH = pl.DeviceIdType.MESH
F32 = jnp.float32
BF16 = jnp.bfloat16

D = 4096
HEAD = 128
HEADS = 4
SEQ = 512
LOCAL = 128
TOK = 16
EXPERTS = 64
FF = 384
CAP = 4
GATES = 128
WIDE = D + GATES
W = WIDE // 3
GROUP = 256
SLOTS = TOK * CAP

ORDER = (("x", "y", "z"), ("y", "z", "x"), ("z", "x", "y"))
PARTS = range(3)
AG_ROUNDS = ((0, 512), (512, 512), (1024, 384))
RS_ROUNDS = ((0, 384), (384, 512), (896, 512))
VMEM = 63 * 2**20


def rope_tables():
    half = HEAD // 2
    places = np.arange(SEQ).astype(np.float32)
    freqs = np.power(
        np.float32(1000000.0), -(np.arange(half).astype(np.float32) * np.float32(2.0) / np.float32(HEAD))
    ).astype(np.float32)
    angles = (places[:, None] * freqs[None, :]).astype(np.float32)
    cosine, sine = np.cos(angles), np.sin(angles)
    return (
        np.concatenate([cosine, cosine], axis=1).astype(np.float32),
        np.concatenate([-sine, sine], axis=1).astype(np.float32),
    )


def place():
    t = lax.axis_index("tensor")
    return {"x": t // 2, "y": lax.axis_index("ctx"), "z": lax.axis_index("dp")}, t % 2


def device(me, k, axis, step):
    value = (me[axis] + step) % 4
    if axis == "x":
        return {"tensor": value * 2 + k}
    return {"ctx" if axis == "y" else "dp": value}


def sibling(me, k):
    return {"tensor": me["x"] * 2 + 1 - k}


def greet(me, k, axes):
    barrier = pltpu.get_barrier_semaphore()
    for axis in axes:
        for step in (1, 2, 3):
            pl.semaphore_signal(
                barrier, inc=1, device_id=device(me, k, axis, step), device_id_type=MESH
            )
    pl.semaphore_signal(barrier, inc=1, device_id=sibling(me, k), device_id_type=MESH)
    pl.semaphore_wait(barrier, 3 * len(axes) + 1)


def send(src, dst, to, send_sem, recv_sem):
    pltpu.make_async_remote_copy(
        src_ref=src,
        dst_ref=dst,
        send_sem=send_sem,
        recv_sem=recv_sem,
        device_id=to,
        device_id_type=MESH,
    ).start()


def wait(ref, sem):
    pltpu.make_async_copy(ref, ref, sem).wait()


def turn(values, cosine, sine):
    values = values.astype(F32)
    return (values * cosine + pltpu.roll(values, HEAD // 2, 1) * sine).astype(BF16)


def layer_kernel(
    query_hbm, key_hbm, value_hbm, residual_hbm, proj_hbm, gain_hbm, router_hbm, routes_hbm,
    cos_hbm, sin_hbm, gate_hbm, up_hbm, down_hbm, out_ref,
    query, residual, gain, router, routes, cosine, sine,
    kv, qrot, krot, far, from_sibling, from_ring, mixed,
    x0, x1, x2, rd0, rd1, rd2, rf0, rf1, rf2, rr0, rr1, rr2, rb0, rb1, rb2, ra0, ra1, ra2,
    wgu, wd, packed, acc, hidden, pick, unpick, row_gate,
    in_sem, kv_send, kv_recv, sib_send, sib_recv, ring_send, ring_recv,
    w_sem, p1s, p1r, p2s, p2r, p3s, p3r, ds, dr,
    qds, qdr, qfs, qfr, q3s, q3r, q2s, q2r, q1s, q1r,
):
    xs, rd, rf, rr = (x0, x1, x2), (rd0, rd1, rd2), (rf0, rf1, rf2), (rr0, rr1, rr2)
    rb, ra = (rb0, rb1, rb2), (ra0, ra1, ra2)
    me, k = place()
    twin = sibling(me, k)

    def spans(r):
        found, at_col = [], 0
        for p in PARTS:
            lo, size = AG_ROUNDS[r]
            if p == 0 and lo == 0:
                lo, size = GATES, size - GATES
            found.append((p, lo, size, at_col))
            at_col += size
        return found

    def weights(r):
        copies = []
        for e in range(2):
            for n, hbm in enumerate((gate_hbm, up_hbm)):
                for p, lo, size, col in spans(r):
                    from_row = p * W + lo - GATES
                    copies.append(
                        pltpu.make_async_copy(
                            hbm.at[e, pl.ds(from_row, size), :],
                            wgu.at[r % 2, e, pl.ds(col, size), pl.ds(n * FF, FF)],
                            w_sem.at[r],
                        )
                    )
        return copies

    def weights_start(r):
        for copy in weights(r):
            copy.start()

    def weights_wait(r):
        total = sum(size for p, lo, size, col in spans(r))
        wait(wgu.at[r % 2, :, pl.ds(0, total), :], w_sem.at[r])

    load_down = pltpu.make_async_copy(down_hbm, wd, w_sem.at[3])


    head = pl.multiple_of((lax.axis_index("tensor") // 4) * HEAD, HEAD)
    y = me["y"]
    loads = [
        pltpu.make_async_copy(src, dst, in_sem.at[i])
        for i, (src, dst) in enumerate(
            (
                (key_hbm.at[0, :, pl.ds(head, HEAD)], kv.at[y, 0]),
                (value_hbm.at[0, :, pl.ds(head, HEAD)], kv.at[y, 1]),
                (query_hbm.at[0], query),
                (cos_hbm, cosine),
                (sin_hbm, sine),
                (proj_hbm.at[pl.ds(0, FF)], wd.at[0]),
                (proj_hbm.at[pl.ds(FF, HEADS * HEAD - FF)], wd.at[1, pl.ds(0, HEADS * HEAD - FF)]),
                (residual_hbm.at[0], residual),
                (gain_hbm, gain),
                (router_hbm, router),
                (routes_hbm.at[0], routes),
            )
        )
    ]
    for load in loads:
        load.start()
    weights_start(0)
    weights_start(1)
    greet(me, k, "xyz")
    for load in loads[:2]:
        load.wait()
    for step in (2, 1, 3):
        send(kv.at[y], kv.at[y], device(me, k, "y", step), kv_send, kv_recv)
    for load in loads[2:5]:
        load.wait()
    own = pl.ds(pl.multiple_of(y * LOCAL, LOCAL), LOCAL)
    for h in range(HEADS):
        qrot[pl.ds(h * LOCAL, LOCAL), :] = turn(
            query[:, h * HEAD : (h + 1) * HEAD], cosine[own, :], sine[own, :]
        )
    wait(kv.at[pl.ds(0, 3)], kv_recv)
    for c in range(4):
        span = pl.ds(c * LOCAL, LOCAL)
        krot[span, :] = turn(kv[c, 0], cosine[span, :], sine[span, :])
    values = kv[:, 1].reshape(SEQ, HEAD)
    place_q = y * LOCAL + lax.broadcasted_iota(jnp.int32, (LOCAL, SEQ), 0)
    causal = place_q >= lax.broadcasted_iota(jnp.int32, (LOCAL, SEQ), 1)
    attended = []
    for h in range(HEADS):
        score = lax.dot_general(
            qrot[pl.ds(h * LOCAL, LOCAL), :], krot[...], (((1,), (1,)), ((), ())),
            preferred_element_type=F32,
        ) * F32(HEAD**-0.5)
        score = jnp.where(causal, score, F32(-1e30))
        peak = jnp.max(score, axis=-1, keepdims=True)
        expon = jnp.exp(score - peak)
        total = jnp.sum(expon, axis=-1, keepdims=True)
        summed = jnp.dot(expon.astype(BF16), values, preferred_element_type=F32)
        attended.append((summed / total).astype(BF16))
    attended = jnp.concatenate(attended, axis=1)
    for load in loads[5:]:
        load.wait()
    for c in range(8):
        cols = slice(c * 512, (c + 1) * 512)
        out = jnp.dot(attended[:, :FF], wd[0, :, cols], preferred_element_type=F32) + jnp.dot(
            attended[:, FF:], wd[1, : HEADS * HEAD - FF, cols], preferred_element_type=F32
        )
        acc[c // 4, pl.ds((c % 4) * LOCAL, LOCAL), :512] = out
        for v in range(4):
            rows = pl.ds(pl.multiple_of((c % 4) * LOCAL + (2 * v + 1 - k) * TOK, TOK), TOK)
            far[v, :, cols] = acc[c // 4, rows, :512].astype(BF16)
        if c % 4 == 3:
            half = pl.ds((c // 4) * 2048, 2048)
            send(
                far.at[:, :, half], from_sibling.at[:, :, half], twin,
                sib_send.at[c // 4], sib_recv.at[c // 4],
            )
    load_down.start()

    def chip_sum(v, c):
        rows = pl.ds(pl.multiple_of((c % 4) * LOCAL + (2 * v + k) * TOK, TOK), TOK)
        return acc[c // 4, rows, :512] + from_sibling[v, :, c * 512 : (c + 1) * 512].astype(F32)

    for i in range(2):
        half = pl.ds(i * 2048, 2048)
        wait(far.at[:, :, half], sib_send.at[i])
        wait(from_sibling.at[:, :, half], sib_recv.at[i])
        for step in (2, 1, 3):
            v = (me["x"] + step) % 4
            for c in range(4 * i, 4 * i + 4):
                far[v, :, c * 512 : (c + 1) * 512] = chip_sum(v, c).astype(BF16)
            send(
                far.at[v, :, half], from_ring.at[step - 1, :, half], device(me, k, "x", step),
                ring_send.at[i], ring_recv.at[i],
            )
    square = jnp.zeros((TOK, 1), F32)
    for c in range(8):
        cols = slice(c * 512, (c + 1) * 512)
        if c % 4 == 0:
            wait(from_ring.at[:, :, pl.ds((c // 4) * 2048, 2048)], ring_recv.at[c // 4])
        projected = chip_sum(me["x"], c)
        for j in range(3):
            projected = projected + from_ring[j, :, cols].astype(F32)
        wide = (residual[:, cols].astype(F32) + projected).astype(BF16)
        mixed[:, cols] = wide
        wide = wide.astype(F32)
        square = square + jnp.sum(wide * wide, axis=-1, keepdims=True)
    scale = lax.rsqrt(square / D + 1e-06)
    for c in range(D // 128):
        wide = mixed[:, c * 128 : (c + 1) * 128].astype(F32)
        normed = (wide * scale * gain[c : c + 1, :].astype(F32)).astype(BF16)
        col = GATES + c * 128
        xs[col // W][k, me["z"], me["y"], me["x"], :, col % W : col % W + 128] = normed
    def at(ref, lead, cols, fix):
        index = [fix.get(axis, slice(None)) for axis in "zyx"]
        return ref.at[(*lead, *index, slice(None), pl.ds(*cols))]


    def p1_start(p):
        a = ORDER[p][0]
        block = at(xs[p], (k,), (0, W), me)
        for step in (2, 1, 3):
            send(block, block, device(me, k, a, step), p1s.at[p], p1r.at[p])

    def p1_wait(p):
        wait(xs[p].at[0, 0, 0, pl.ds(0, 3)], p1r.at[p])

    def p2_ahead(p):
        b = ORDER[p][1]
        block = at(xs[p], (k,), (0, W), me)
        for step in (2, 1, 3):
            send(block, block, device(me, k, b, step), p2s.at[p], p2r.at[p, 3])

    def p2_start(p, r):
        a, b, c = ORDER[p]
        for step in (2, 1, 3):
            for other in (1, 2, 3):
                unit = at(xs[p], (k,), AG_ROUNDS[r], {**me, a: (me[a] + other) % 4})
                send(unit, unit, device(me, k, b, step), p2s.at[p], p2r.at[p, r])

    def p2_bytes(p, r):
        return xs[p].at[0, 0, pl.ds(0, 3), pl.ds(0, 3), :, pl.ds(*AG_ROUNDS[r])]

    def p3_unit(p, r, step, half=None):
        a, b, c = ORDER[p]
        fix = {c: (me[c] + step) % 4}
        if half is not None:
            fix[b] = pl.ds(2 * half, 2)
        return at(xs[p], (k,), AG_ROUNDS[r], fix)

    def p3_send(p, r, step, half, way):
        unit = p3_unit(p, r, step, half)
        recv = p3r.at[p, r, 2] if half is not None else p3r.at[p, r, 0 if way == 1 else 1]
        send(unit, unit, device(me, k, ORDER[p][2], way), p3s.at[p], recv)

    def twin_send(p, r, step):
        unit = p3_unit(p, r, step)
        send(unit, unit, twin, ds.at[p], dr.at[p, r])

    def p3_start(r):
        for p in PARTS:
            if r == 0:
                wait(xs[p].at[0, 0, 0, pl.ds(0, 3)], p2r.at[p, 3])
            wait(p2_bytes(p, r), p2r.at[p, r])
            p3_send(p, r, 0, None, 1)
            p3_send(p, r, 0, None, -1)

    def p3_forward(r):
        for p in PARTS:
            wait(p3_unit(p, r, -1), p3r.at[p, r, 0])
            p3_send(p, r, -1, 0, 1)
            wait(p3_unit(p, r, 1), p3r.at[p, r, 1])
            p3_send(p, r, 1, 1, -1)
        for p in PARTS:
            for step in (0, -1, 1):
                twin_send(p, r, step)

    def p3_finish(r):
        for p in PARTS:
            wait(p3_unit(p, r, 2), p3r.at[p, r, 2])
            twin_send(p, r, 2)

    def twin_wait(r):
        for p in PARTS:
            wait(xs[p].at[1 - k, :, :, :, :, pl.ds(*AG_ROUNDS[r])], dr.at[p, r])

    def gates():
        logits = jnp.zeros((EXPERTS, TOK), F32)
        for p in PARTS:
            lo = GATES if p == 0 else 0
            col = p * W + lo - GATES
            normed = xs[p][k, me["z"], me["y"], me["x"], :, lo:W]
            logits = logits + lax.dot_general(
                router[:, col : col + W - lo], normed, (((1,), (1,)), ((), ())),
                preferred_element_type=F32,
            )
        expert = lax.broadcasted_iota(jnp.int32, (EXPERTS, TOK), 0)
        chosen = expert == routes[0:1, :]
        for j in range(1, 8):
            chosen = jnp.logical_or(chosen, expert == routes[j : j + 1, :])
        peak = jnp.max(jnp.where(chosen, logits, F32(-3e38)), axis=0, keepdims=True)
        expon = jnp.where(chosen, jnp.exp(logits - peak), F32(0.0))
        gate = expon / jnp.sum(expon, axis=0, keepdims=True)
        high = gate.astype(BF16).astype(F32)
        both = jnp.concatenate([high, gate - high], axis=0).astype(BF16)
        unit = lax.broadcasted_iota(jnp.int32, (TOK, TOK), 0) == lax.broadcasted_iota(
            jnp.int32, (TOK, TOK), 1
        )
        turned = lax.dot_general(
            unit.astype(F32).astype(BF16), both, (((1,), (1,)), ((), ())), preferred_element_type=F32
        )
        x0[k, me["z"], me["y"], me["x"], :, :GATES] = turned.astype(BF16)


    def selections():
        first = 2 * (me["y"] * 8 + lax.axis_index("tensor"))
        rows = lax.broadcasted_iota(jnp.int32, (8, GATES), 0)
        lanes = lax.broadcasted_iota(jnp.int32, (8, GATES), 1)
        mine = jnp.logical_and(lanes % EXPERTS == first + rows, rows < 2).astype(F32).astype(BF16)
        s = lax.broadcasted_iota(jnp.int32, (GROUP, GROUP), 0)
        u = lax.broadcasted_iota(jnp.int32, (GROUP, GROUP), 1)
        earlier = jnp.logical_and(s // TOK == u // TOK, s < u).astype(F32).astype(BF16)
        base = (lax.broadcasted_iota(jnp.int32, (1, GROUP), 1) // TOK * CAP).astype(F32)
        slots = lax.broadcasted_iota(jnp.int32, (SLOTS, GROUP), 0).astype(F32)

        def one(g, carry):
            tile = x0[g // 4, g % 4, :, :, :, :GATES].reshape(GROUP, GATES)
            gate = lax.dot_general(mine, tile, (((1,), (1,)), ((), ())), preferred_element_type=F32)
            named = (gate > 0).astype(F32)
            rank = jnp.dot(named.astype(BF16), earlier, preferred_element_type=F32)
            both = []
            for e in range(2):
                hit = jnp.logical_and(slots == rank[e : e + 1] + base, gate[e : e + 1] > 0).astype(F32)
                worth = jnp.sum(hit * gate[e : e + 1], axis=1, keepdims=True)
                row_gate[e, pl.ds(g * SLOTS, SLOTS), :] = jnp.broadcast_to(worth, (SLOTS, 128))
                both.append(hit)
            both = jnp.concatenate(both, axis=0)
            pick[g] = both.astype(BF16)
            unpick[g] = both.T.astype(BF16)
            return carry

        lax.fori_loop(0, 8, one, 0, unroll=True)

    def compact(r, half):
        for p, lo, size, col in spans(r):
            for z in range(4):
                tokens = xs[p][half, z, :, :, :, lo : lo + size].reshape(GROUP, size)
                rows = jnp.dot(pick[4 * half + z], tokens, preferred_element_type=F32).astype(BF16)
                for e in range(2):
                    span = pl.ds((4 * half + z) * SLOTS, SLOTS)
                    packed[e, span, col : col + size] = rows[e * SLOTS : (e + 1) * SLOTS]

    def gate_up(r, rows):
        depth = sum(size for p, lo, size, col in spans(r))
        for e in range(2):
            total = jnp.dot(
                packed[e, rows, :depth], wgu[r % 2, e, :depth, :], preferred_element_type=F32
            )
            if r > 0:
                total = total + acc[e, rows]
            if r < len(AG_ROUNDS) - 1:
                acc[e, rows] = total
            else:
                gate, up = total[:, :FF], total[:, FF:]
                hidden[e, rows] = (gate / (1.0 + jnp.exp(-gate)) * up).astype(BF16)


    def out_cols(p, r):
        lo, size = RS_ROUNDS[r]
        if p == 0 and lo == 0:
            lo, size = GATES, size - GATES
        return lo, size

    def down(r):
        def scatter(p, half):
            lo, size = out_cols(p, r)

            def one(i, carry):
                g = 4 * half + i
                rows = jnp.concatenate(
                    [
                        packed[e, pl.ds(g * SLOTS, SLOTS), 512 * p : 512 * p + size]
                        for e in range(2)
                    ],
                    axis=0,
                )
                tokens = jnp.dot(unpick[g], rows, preferred_element_type=F32).astype(BF16)
                xs[p][half, i, :, :, :, lo : lo + size] = tokens.reshape(4, 4, TOK, size)
                return carry

            lax.fori_loop(0, 4, one, 0, unroll=True)

        def to_twin(p, step):
            src = unit_of(xs[p], (1 - k,), p, r, step)
            recv = qdr.at[p, r, 0 if step == 2 else 1]
            send(src, unit_of(rd[p], (), p, r, step), twin, qds.at[p], recv)

        for p in PARTS:
            lo, size = out_cols(p, r)
            col = p * W + lo - GATES
            for e in range(2):
                part = jnp.dot(hidden[e], wd[e, :, col : col + size], preferred_element_type=F32)
                packed[e, :, 512 * p : 512 * p + size] = (part * row_gate[e, :, 0:1]).astype(BF16)
            scatter(p, 1 - k)
            to_twin(p, 2)
        for p in PARTS:
            for step in (1, 3, 0):
                to_twin(p, step)
        for p in PARTS:
            scatter(p, k)

    def total_into(dst, refs):
        total = refs[0][...].astype(F32)
        for ref in refs[1:]:
            total = total + ref[...].astype(F32)
        dst[...] = total.astype(BF16)

    def unit_of(ref, lead, p, r, step, pieces=1, piece=0):
        a, b, c = ORDER[p]
        fix = {c: (me[c] + step) % 4}
        if pieces == 2:
            fix[b] = pl.ds(2 * piece, 2)
        elif pieces == 4:
            fix[b] = piece
        return at(ref, lead, out_cols(p, r), fix)

    def add_unit(p, r, step):
        def one(i, carry):
            mine = unit_of(xs[p], (k,), p, r, step, 4, i)
            total_into(mine, [mine, unit_of(rd[p], (), p, r, step, 4, i)])
            return carry

        lax.fori_loop(0, 4, one, 0, unroll=True)

    def piece_of(ref, lead, p, r, fix):
        a, b, c = ORDER[p]
        index = [fix.get(axis, slice(None)) for axis in "zyx" if axis != c]
        return ref.at[(*lead, *index, slice(None), pl.ds(*out_cols(p, r)))]

    def a1(r):
        for p in PARTS:
            c = ORDER[p][2]
            wait(unit_of(rd[p], (), p, r, 2), qdr.at[p, r, 0])
            add_unit(p, r, 2)
            for half, way in ((0, 1), (1, -1)):
                src = unit_of(xs[p], (k,), p, r, 2, 2, half)
                send(src, half_slot(p, r, half), device(me, k, c, way), qfs.at[p], qfr.at[p, r, half])

    def b1(r):
        for p in PARTS:
            wait(at(rd[p], (), out_cols(p, r), {"z": pl.ds(0, 3)}), qdr.at[p, r, 1])
            for step in (1, 3, 0):
                add_unit(p, r, step)

    def half_slot(p, r, half, i=None):
        b = ORDER[p][1]
        fix = {} if i is None else {b: i}
        a, b, c = ORDER[p]
        index = [fix.get(axis, slice(None)) for axis in "zyx" if axis != c]
        return rf[p].at[(half, *index, slice(None), pl.ds(*out_cols(p, r)))]

    def s2(r):
        for p in PARTS:
            c = ORDER[p][2]
            for half, way in ((0, 1), (1, -1)):
                wait(half_slot(p, r, half), qfr.at[p, r, half])

                def one(i, carry, half=half, way=way):
                    mine = unit_of(xs[p], (k,), p, r, way, 4, 2 * half + i)
                    total_into(mine, [mine, half_slot(p, r, half, i)])
                    return carry

                lax.fori_loop(0, 2, one, 0, unroll=True)
                src = unit_of(xs[p], (k,), p, r, way)
                slot = piece_of(rr[p], (half,), p, r, {})
                send(src, slot, device(me, k, c, way), q3s.at[p], q3r.at[p, r])

    def s3(r):
        for p in PARTS:
            a, b, c = ORDER[p]
            wait(piece_of(rr[p], (slice(None),), p, r, {}), q3r.at[p, r])

            def one(i, carry, b=b):
                mine = unit_of(xs[p], (k,), p, r, 0, 4, i)
                total_into(mine, [mine] + [piece_of(rr[p], (h,), p, r, {b: i}) for h in range(2)])
                return carry

            lax.fori_loop(0, 4, one, 0, unroll=True)
            for step in (2, 1, 3):
                src = unit_of(xs[p], (k,), p, r, 0, 4, (me[b] + step) % 4)
                slot = rb[p].at[step - 1, :, :, pl.ds(*out_cols(p, r))]
                send(src, slot, device(me, k, b, step), q2s.at[p], q2r.at[p, r])

    def s4(r):
        for p in PARTS:
            a, b, c = ORDER[p]
            cols = pl.ds(*out_cols(p, r))
            wait(rb[p].at[:, :, :, cols], q2r.at[p, r])
            mine = unit_of(xs[p], (k,), p, r, 0, 4, me[b])
            total_into(mine, [mine] + [rb[p].at[j, :, :, cols] for j in range(3)])
            for step in (2, 1, 3):
                src = at(xs[p], (k,), out_cols(p, r), {**me, a: (me[a] + step) % 4})
                send(src, ra[p].at[step - 1, :, cols], device(me, k, a, step), q1s.at[p], q1r.at[p, r])

    def s5(r):
        for p in PARTS:
            lo, size = out_cols(p, r)
            cols = pl.ds(lo, size)
            wait(ra[p].at[:, :, cols], q1r.at[p, r])
            total = at(xs[p], (k,), (lo, size), me)[...].astype(F32)
            for j in range(3):
                total = total + ra[p][j, :, cols].astype(F32)
            col = p * W + lo - GATES
            span = slice(col, col + size)
            out_ref[:, span] = (mixed[:, span].astype(F32) + total).astype(BF16)


    p1_start(1)
    p1_start(2)
    gates()
    p1_start(0)
    for p in (1, 2, 0):
        p2_ahead(p)
    for p in (1, 2, 0):
        p1_wait(p)
        for r in range(3):
            p2_start(p, r)
    p3_start(0)
    p3_start(1)
    p3_forward(0)
    p3_start(2)
    p3_finish(0)
    twin_wait(0)
    selections()
    p3_forward(1)
    everything = pl.ds(0, 8 * SLOTS)
    compact(0, 0)
    compact(0, 1)
    weights_wait(0)
    gate_up(0, everything)
    weights_start(2)
    p3_finish(1)
    p3_forward(2)
    twin_wait(1)
    compact(1, 0)
    compact(1, 1)
    weights_wait(1)
    gate_up(1, everything)
    p3_finish(2)
    weights_wait(2)
    for half in (k, 1 - k):
        if half is not k:
            twin_wait(2)
        compact(2, half)
        gate_up(2, pl.ds(pl.multiple_of(half * 4 * SLOTS, 4 * SLOTS), 4 * SLOTS))
    load_down.wait()
    for p in PARTS:
        wait(xs[p].at[0, 0, 0, pl.ds(0, 3)], p1s.at[p])
        wait(xs[p].at[0, 0, pl.ds(0, 3)], p2s.at[p])
        wait(xs[p].at[0, pl.ds(0, 3)], p3s.at[p])
        wait(xs[p].at[0], ds.at[p])
    down(0)
    a1(0)
    down(1)
    b1(0)
    a1(1)
    s2(0)
    down(2)
    b1(1)
    a1(2)
    s2(1)
    b1(2)
    s3(0)
    s2(2)
    s4(0)
    s3(1)
    s5(0)
    s4(1)
    s3(2)
    s5(1)
    s4(2)
    s5(2)
    wait(kv.at[pl.ds(0, 3)], kv_send)
    for i in range(2):
        wait(from_ring.at[:, :, pl.ds(i * 2048, 2048)], ring_send.at[i])
    for p in PARTS:
        first = out_cols(p, 0)[0]
        cols = pl.ds(first, W - first)
        wait(xs[p].at[0, :, :, :, :, cols], qds.at[p])
        wait(rf[p].at[:, :, :, :, cols], qfs.at[p])
        wait(rr[p].at[:, :, :, :, cols], q3s.at[p])
        wait(rb[p].at[:, :, :, cols], q2s.at[p])
        wait(ra[p].at[:, :, cols], q1s.at[p])


def on_device(
    query_rows,
    key_rows,
    value_rows,
    residual,
    out_proj,
    post_gain,
    router,
    routes,
    w_gate,
    w_up,
    w_down,
):
    vmem = pltpu.VMEM
    hbm = pl.BlockSpec(memory_space=pl.ANY)
    dma = pltpu.SemaphoreType.DMA
    cosine, sine = rope_tables()
    n = len(RS_ROUNDS)

    def half_shape(p):
        a, b, c = ORDER[p]
        return (2, *[2 if axis == b else 4 for axis in "zyx" if axis != c], TOK, W)

    scratch = (
        [
            vmem((LOCAL, HEADS * HEAD), BF16),
            vmem((TOK, D), BF16),
            vmem((D // 128, 128), BF16),
            vmem((EXPERTS, D), BF16),
            vmem((8, TOK), jnp.int32),
            vmem((SEQ, HEAD), F32),
            vmem((SEQ, HEAD), F32),
            vmem((4, 2, LOCAL, HEAD), BF16),
            vmem((HEADS * LOCAL, HEAD), BF16),
            vmem((SEQ, HEAD), BF16),
            vmem((4, TOK, D), BF16),
            vmem((4, TOK, D), BF16),
            vmem((3, TOK, D), BF16),
            vmem((TOK, D), BF16),
        ]
        + [vmem((2, 4, 4, 4, TOK, W), BF16)] * 3
        + [vmem((4, 4, 4, TOK, W), BF16)] * 3
        + [vmem(half_shape(p), BF16) for p in PARTS]
        + [vmem((2, 4, 4, TOK, W), BF16)] * 3
        + [vmem((3, 4, TOK, W), BF16)] * 3
        + [vmem((3, TOK, W), BF16)] * 3
        + [
            vmem((2, 2, 1536, 2 * FF), BF16),
            vmem((2, FF, D), BF16),
            vmem((2, 8 * SLOTS, 1536), BF16),
            vmem((2, 8 * SLOTS, 2 * FF), F32),
            vmem((2, 8 * SLOTS, FF), BF16),
            vmem((8, 2 * SLOTS, GROUP), BF16),
            vmem((8, GROUP, 2 * SLOTS), BF16),
            vmem((2, 8 * SLOTS, 128), F32),
        ]
        + [dma((11,)), dma, dma, dma((2,)), dma((2,)), dma((2,)), dma((2,))]
        + [dma((4,)), dma((3,)), dma((3,)), dma((3,)), dma((3, 4)), dma((3,)), dma((3, 3, 3))]
        + [dma((3,)), dma((3, 3))]
        + [dma((3,)), dma((3, n, 2)), dma((3,)), dma((3, n, 2))]
        + [dma((3,)), dma((3, n))] * 3
    )
    out = pl.pallas_call(
        layer_kernel,
        out_shape=jax.ShapeDtypeStruct((TOK, D), BF16),
        in_specs=[hbm] * 13,
        out_specs=pl.BlockSpec(memory_space=pltpu.VMEM),
        scratch_shapes=scratch,
        compiler_params=pltpu.CompilerParams(
            collective_id=0, has_side_effects=True, vmem_limit_bytes=VMEM
        ),
    )(
        query_rows, key_rows, value_rows, residual, out_proj, post_gain.reshape(D // 128, 128),
        router.T, jnp.swapaxes(routes, 1, 2), jnp.asarray(cosine), jnp.asarray(sine),
        w_gate, w_up, w_down,
    )
    return out[None]


def solution(mesh):
    in_specs = (
        P("dp", "ctx", "tensor"),
        P("dp", "ctx", None),
        P("dp", "ctx", None),
        P("dp", ("ctx", "tensor"), None),
        P("tensor", None),
        P(),
        P(),
        P("dp", ("ctx", "tensor"), None),
        P(("ctx", "tensor"), None, "dp"),
        P(("ctx", "tensor"), None, "dp"),
        P(("ctx", "tensor"), "dp", None),
    )
    out_specs = P("dp", ("ctx", "tensor"), None)
    return jax.shard_map(
        on_device, mesh=mesh, in_specs=in_specs, out_specs=out_specs, check_vma=False
    )
```

```python
import jax
import jax.numpy as jnp
import numpy as np
from jax import lax
from jax.experimental import pallas as pl
from jax.experimental.pallas import tpu as pltpu
from jax.sharding import PartitionSpec as P

MESH = pl.DeviceIdType.MESH
F32 = jnp.float32
BF16 = jnp.bfloat16

D = 4096
HEAD = 128
HEADS = 4
SEQ = 512
LOCAL = 128
TOK = 16
EXPERTS = 64
FF = 384
CAP = 4
GATES = 128
WIDE = D + GATES
W = WIDE // 3
GROUP = 256
SLOTS = TOK * CAP

ORDER = (("x", "y", "z"), ("y", "z", "x"), ("z", "x", "y"))
PARTS = range(3)
AG_ROUNDS = ((0, 384), (384, 512), (896, 512))
RS_ROUNDS = ((0, 384), (384, 512), (896, 512))
VMEM = 63 * 2**20


def rope_tables():
    half = HEAD // 2
    places = np.arange(SEQ).astype(np.float32)
    freqs = np.power(
        np.float32(1000000.0), -(np.arange(half).astype(np.float32) * np.float32(2.0) / np.float32(HEAD))
    ).astype(np.float32)
    angles = (places[:, None] * freqs[None, :]).astype(np.float32)
    cosine, sine = np.cos(angles), np.sin(angles)
    return (
        np.concatenate([cosine, cosine], axis=1).astype(np.float32),
        np.concatenate([-sine, sine], axis=1).astype(np.float32),
    )


def place():
    t = lax.axis_index("tensor")
    return {"x": t // 2, "y": lax.axis_index("ctx"), "z": lax.axis_index("dp")}, t % 2


def device(me, k, axis, step):
    value = (me[axis] + step) % 4
    if axis == "x":
        return {"tensor": value * 2 + k}
    return {"ctx" if axis == "y" else "dp": value}


def sibling(me, k):
    return {"tensor": me["x"] * 2 + 1 - k}


def greet(me, k, axes):
    barrier = pltpu.get_barrier_semaphore()
    for axis in axes:
        for step in (1, 2, 3):
            pl.semaphore_signal(
                barrier, inc=1, device_id=device(me, k, axis, step), device_id_type=MESH
            )
    pl.semaphore_signal(barrier, inc=1, device_id=sibling(me, k), device_id_type=MESH)
    pl.semaphore_wait(barrier, 3 * len(axes) + 1)


def send(src, dst, to, send_sem, recv_sem):
    pltpu.make_async_remote_copy(
        src_ref=src,
        dst_ref=dst,
        send_sem=send_sem,
        recv_sem=recv_sem,
        device_id=to,
        device_id_type=MESH,
    ).start()


def wait(ref, sem):
    pltpu.make_async_copy(ref, ref, sem).wait()


def turn(values, cosine, sine):
    values = values.astype(F32)
    return (values * cosine + pltpu.roll(values, HEAD // 2, 1) * sine).astype(BF16)


def layer_kernel(
    query_hbm, key_hbm, value_hbm, residual_hbm, proj_hbm, gain_hbm, router_hbm, routes_hbm,
    cos_hbm, sin_hbm, gate_hbm, up_hbm, down_hbm, out_ref,
    query, residual, gain, router, routes, cosine, sine,
    kv, qrot, krot, far, from_sibling, from_ring, mixed,
    x0, x1, x2, rd0, rd1, rd2, rf0, rf1, rf2, rr0, rr1, rr2, rb0, rb1, rb2, ra0, ra1, ra2,
    wgu, wd, packed, acc, hidden, pick, unpick, row_gate,
    in_sem, kv_send, kv_recv, sib_send, sib_recv, ring_send, ring_recv,
    w_sem, p1s, p1r, p2s, p2r, p3s, p3r, ds, dr,
    qds, qdr, qfs, qfr, q3s, q3r, q2s, q2r, q1s, q1r,
):
    xs, rd, rf, rr = (x0, x1, x2), (rd0, rd1, rd2), (rf0, rf1, rf2), (rr0, rr1, rr2)
    rb, ra = (rb0, rb1, rb2), (ra0, ra1, ra2)
    me, k = place()
    twin = sibling(me, k)

    def spans(r):
        found, at_col = [], 0
        for p in PARTS:
            lo, size = AG_ROUNDS[r]
            if p == 0 and lo == 0:
                lo, size = GATES, size - GATES
            found.append((p, lo, size, at_col))
            at_col += size
        return found

    def weights(r):
        copies = []
        for e in range(2):
            for n, hbm in enumerate((gate_hbm, up_hbm)):
                for p, lo, size, col in spans(r):
                    from_row = p * W + lo - GATES
                    copies.append(
                        pltpu.make_async_copy(
                            hbm.at[e, pl.ds(from_row, size), :],
                            wgu.at[r % 2, e, pl.ds(col, size), pl.ds(n * FF, FF)],
                            w_sem.at[r],
                        )
                    )
        return copies

    def weights_start(r):
        for copy in weights(r):
            copy.start()

    def weights_wait(r):
        total = sum(size for p, lo, size, col in spans(r))
        wait(wgu.at[r % 2, :, pl.ds(0, total), :], w_sem.at[r])

    load_down = pltpu.make_async_copy(down_hbm, wd, w_sem.at[3])


    head = pl.multiple_of((lax.axis_index("tensor") // 4) * HEAD, HEAD)
    y = me["y"]
    loads = [
        pltpu.make_async_copy(src, dst, in_sem.at[i])
        for i, (src, dst) in enumerate(
            (
                (key_hbm.at[0, :, pl.ds(head, HEAD)], kv.at[y, 0]),
                (value_hbm.at[0, :, pl.ds(head, HEAD)], kv.at[y, 1]),
                (query_hbm.at[0], query),
                (cos_hbm, cosine),
                (sin_hbm, sine),
                (proj_hbm.at[pl.ds(0, FF)], wd.at[0]),
                (proj_hbm.at[pl.ds(FF, HEADS * HEAD - FF)], wd.at[1, pl.ds(0, HEADS * HEAD - FF)]),
                (residual_hbm.at[0], residual),
                (gain_hbm, gain),
                (router_hbm, router),
                (routes_hbm.at[0], routes),
            )
        )
    ]
    for load in loads:
        load.start()
    weights_start(0)
    weights_start(1)
    greet(me, k, "xyz")
    for load in loads[:2]:
        load.wait()
    for step in (2, 1, 3):
        send(kv.at[y], kv.at[y], device(me, k, "y", step), kv_send, kv_recv)
    for load in loads[2:5]:
        load.wait()
    own = pl.ds(pl.multiple_of(y * LOCAL, LOCAL), LOCAL)
    for h in range(HEADS):
        qrot[pl.ds(h * LOCAL, LOCAL), :] = turn(
            query[:, h * HEAD : (h + 1) * HEAD], cosine[own, :], sine[own, :]
        )
    wait(kv.at[pl.ds(0, 3)], kv_recv)
    for c in range(4):
        span = pl.ds(c * LOCAL, LOCAL)
        krot[span, :] = turn(kv[c, 0], cosine[span, :], sine[span, :])
    values = kv[:, 1].reshape(SEQ, HEAD)
    place_q = y * LOCAL + lax.broadcasted_iota(jnp.int32, (LOCAL, SEQ), 0)
    causal = place_q >= lax.broadcasted_iota(jnp.int32, (LOCAL, SEQ), 1)
    attended = []
    for h in range(HEADS):
        score = lax.dot_general(
            qrot[pl.ds(h * LOCAL, LOCAL), :], krot[...], (((1,), (1,)), ((), ())),
            preferred_element_type=F32,
        ) * F32(HEAD**-0.5)
        score = jnp.where(causal, score, F32(-1e30))
        peak = jnp.max(score, axis=-1, keepdims=True)
        expon = jnp.exp(score - peak)
        total = jnp.sum(expon, axis=-1, keepdims=True)
        summed = jnp.dot(expon.astype(BF16), values, preferred_element_type=F32)
        attended.append((summed / total).astype(BF16))
    attended = jnp.concatenate(attended, axis=1)
    for load in loads[5:]:
        load.wait()
    for c in range(8):
        cols = slice(c * 512, (c + 1) * 512)
        out = jnp.dot(attended[:, :FF], wd[0, :, cols], preferred_element_type=F32) + jnp.dot(
            attended[:, FF:], wd[1, : HEADS * HEAD - FF, cols], preferred_element_type=F32
        )
        acc[c // 4, pl.ds((c % 4) * LOCAL, LOCAL), :512] = out
        for v in range(4):
            rows = pl.ds(pl.multiple_of((c % 4) * LOCAL + (2 * v + 1 - k) * TOK, TOK), TOK)
            far[v, :, cols] = acc[c // 4, rows, :512].astype(BF16)
        if c % 2 == 1:
            half = pl.ds((c // 2) * 1024, 1024)
            send(
                far.at[:, :, half], from_sibling.at[:, :, half], twin,
                sib_send.at[c // 2], sib_recv.at[c // 2],
            )
    load_down.start()

    def chip_sum(v, c):
        rows = pl.ds(pl.multiple_of((c % 4) * LOCAL + (2 * v + k) * TOK, TOK), TOK)
        return acc[c // 4, rows, :512] + from_sibling[v, :, c * 512 : (c + 1) * 512].astype(F32)

    for i in range(4):
        half = pl.ds(i * 1024, 1024)
        wait(far.at[:, :, half], sib_send.at[i])
        wait(from_sibling.at[:, :, half], sib_recv.at[i])
        for step in (2, 1, 3):
            v = (me["x"] + step) % 4
            for c in range(2 * i, 2 * i + 2):
                far[v, :, c * 512 : (c + 1) * 512] = chip_sum(v, c).astype(BF16)
            send(
                far.at[v, :, half], from_ring.at[step - 1, :, half], device(me, k, "x", step),
                ring_send.at[i], ring_recv.at[i],
            )
    square = jnp.zeros((TOK, 1), F32)
    for c in range(8):
        cols = slice(c * 512, (c + 1) * 512)
        if c % 2 == 0:
            wait(from_ring.at[:, :, pl.ds((c // 2) * 1024, 1024)], ring_recv.at[c // 2])
        projected = chip_sum(me["x"], c)
        for j in range(3):
            projected = projected + from_ring[j, :, cols].astype(F32)
        wide = (residual[:, cols].astype(F32) + projected).astype(BF16)
        mixed[:, cols] = wide
        wide = wide.astype(F32)
        square = square + jnp.sum(wide * wide, axis=-1, keepdims=True)
    scale = lax.rsqrt(square / D + 1e-06)
    for c in range(D // 128):
        wide = mixed[:, c * 128 : (c + 1) * 128].astype(F32)
        normed = (wide * scale * gain[c : c + 1, :].astype(F32)).astype(BF16)
        col = GATES + c * 128
        xs[col // W][k, me["z"], me["y"], me["x"], :, col % W : col % W + 128] = normed
    def at(ref, lead, cols, fix):
        index = [fix.get(axis, slice(None)) for axis in "zyx"]
        return ref.at[(*lead, *index, slice(None), pl.ds(*cols))]


    def p1_start(p):
        a = ORDER[p][0]
        block = at(xs[p], (k,), (0, W), me)
        for step in (2, 1, 3):
            send(block, block, device(me, k, a, step), p1s.at[p], p1r.at[p])

    def p1_wait(p):
        wait(xs[p].at[0, 0, 0, pl.ds(0, 3)], p1r.at[p])

    def p2_ahead(p):
        b = ORDER[p][1]
        block = at(xs[p], (k,), (0, W), me)
        for step in (2, 1, 3):
            send(block, block, device(me, k, b, step), p2s.at[p], p2r.at[p, 3])

    def p2_start(p, r):
        a, b, c = ORDER[p]
        for step in (2, 1, 3):
            for other in (1, 2, 3):
                unit = at(xs[p], (k,), AG_ROUNDS[r], {**me, a: (me[a] + other) % 4})
                send(unit, unit, device(me, k, b, step), p2s.at[p], p2r.at[p, r])

    def p2_bytes(p, r):
        return xs[p].at[0, 0, pl.ds(0, 3), pl.ds(0, 3), :, pl.ds(*AG_ROUNDS[r])]

    def p3_unit(p, r, step, half=None):
        a, b, c = ORDER[p]
        fix = {c: (me[c] + step) % 4}
        if half is not None:
            fix[b] = pl.ds(2 * half, 2)
        return at(xs[p], (k,), AG_ROUNDS[r], fix)

    def p3_send(p, r, step, half, way):
        unit = p3_unit(p, r, step, half)
        recv = p3r.at[p, r, 2] if half is not None else p3r.at[p, r, 0 if way == 1 else 1]
        send(unit, unit, device(me, k, ORDER[p][2], way), p3s.at[p], recv)

    def twin_send(p, r, step):
        unit = p3_unit(p, r, step)
        send(unit, unit, twin, ds.at[p], dr.at[p, r])

    def p3_start(r):
        for p in PARTS:
            if r == 0:
                wait(xs[p].at[0, 0, 0, pl.ds(0, 3)], p2r.at[p, 3])
            wait(p2_bytes(p, r), p2r.at[p, r])
            p3_send(p, r, 0, None, 1)
            p3_send(p, r, 0, None, -1)

    def p3_forward(r):
        for p in PARTS:
            wait(p3_unit(p, r, -1), p3r.at[p, r, 0])
            p3_send(p, r, -1, 0, 1)
            wait(p3_unit(p, r, 1), p3r.at[p, r, 1])
            p3_send(p, r, 1, 1, -1)
        for p in PARTS:
            for step in (0, -1, 1):
                twin_send(p, r, step)

    def p3_finish(r):
        for p in PARTS:
            wait(p3_unit(p, r, 2), p3r.at[p, r, 2])
            twin_send(p, r, 2)

    def twin_wait(r):
        for p in PARTS:
            wait(xs[p].at[1 - k, :, :, :, :, pl.ds(*AG_ROUNDS[r])], dr.at[p, r])

    def gates():
        logits = jnp.zeros((EXPERTS, TOK), F32)
        for p in PARTS:
            lo = GATES if p == 0 else 0
            col = p * W + lo - GATES
            normed = xs[p][k, me["z"], me["y"], me["x"], :, lo:W]
            logits = logits + lax.dot_general(
                router[:, col : col + W - lo], normed, (((1,), (1,)), ((), ())),
                preferred_element_type=F32,
            )
        expert = lax.broadcasted_iota(jnp.int32, (EXPERTS, TOK), 0)
        chosen = expert == routes[0:1, :]
        for j in range(1, 8):
            chosen = jnp.logical_or(chosen, expert == routes[j : j + 1, :])
        peak = jnp.max(jnp.where(chosen, logits, F32(-3e38)), axis=0, keepdims=True)
        expon = jnp.where(chosen, jnp.exp(logits - peak), F32(0.0))
        gate = expon / jnp.sum(expon, axis=0, keepdims=True)
        high = gate.astype(BF16).astype(F32)
        both = jnp.concatenate([high, gate - high], axis=0).astype(BF16)
        unit = lax.broadcasted_iota(jnp.int32, (TOK, TOK), 0) == lax.broadcasted_iota(
            jnp.int32, (TOK, TOK), 1
        )
        turned = lax.dot_general(
            unit.astype(F32).astype(BF16), both, (((1,), (1,)), ((), ())), preferred_element_type=F32
        )
        x0[k, me["z"], me["y"], me["x"], :, :GATES] = turned.astype(BF16)


    def selections():
        first = 2 * (me["y"] * 8 + lax.axis_index("tensor"))
        rows = lax.broadcasted_iota(jnp.int32, (8, GATES), 0)
        lanes = lax.broadcasted_iota(jnp.int32, (8, GATES), 1)
        mine = jnp.logical_and(lanes % EXPERTS == first + rows, rows < 2).astype(F32).astype(BF16)
        s = lax.broadcasted_iota(jnp.int32, (GROUP, GROUP), 0)
        u = lax.broadcasted_iota(jnp.int32, (GROUP, GROUP), 1)
        earlier = jnp.logical_and(s // TOK == u // TOK, s < u).astype(F32).astype(BF16)
        base = (lax.broadcasted_iota(jnp.int32, (1, GROUP), 1) // TOK * CAP).astype(F32)
        slots = lax.broadcasted_iota(jnp.int32, (SLOTS, GROUP), 0).astype(F32)

        def one(g, carry):
            tile = x0[g // 4, g % 4, :, :, :, :GATES].reshape(GROUP, GATES)
            gate = lax.dot_general(mine, tile, (((1,), (1,)), ((), ())), preferred_element_type=F32)
            named = (gate > 0).astype(F32)
            rank = jnp.dot(named.astype(BF16), earlier, preferred_element_type=F32)
            both = []
            for e in range(2):
                hit = jnp.logical_and(slots == rank[e : e + 1] + base, gate[e : e + 1] > 0).astype(F32)
                worth = jnp.sum(hit * gate[e : e + 1], axis=1, keepdims=True)
                row_gate[e, pl.ds(g * SLOTS, SLOTS), :] = jnp.broadcast_to(worth, (SLOTS, 128))
                both.append(hit)
            both = jnp.concatenate(both, axis=0)
            pick[g] = both.astype(BF16)
            unpick[g] = both.T.astype(BF16)
            return carry

        lax.fori_loop(0, 8, one, 0, unroll=True)

    def compact(r, half):
        for p, lo, size, col in spans(r):
            for z in range(4):
                tokens = xs[p][half, z, :, :, :, lo : lo + size].reshape(GROUP, size)
                rows = jnp.dot(pick[4 * half + z], tokens, preferred_element_type=F32).astype(BF16)
                for e in range(2):
                    span = pl.ds((4 * half + z) * SLOTS, SLOTS)
                    packed[e, span, col : col + size] = rows[e * SLOTS : (e + 1) * SLOTS]

    def gate_up(r, rows):
        depth = sum(size for p, lo, size, col in spans(r))
        for e in range(2):
            total = jnp.dot(
                packed[e, rows, :depth], wgu[r % 2, e, :depth, :], preferred_element_type=F32
            )
            if r > 0:
                total = total + acc[e, rows]
            if r < len(AG_ROUNDS) - 1:
                acc[e, rows] = total
            else:
                gate, up = total[:, :FF], total[:, FF:]
                hidden[e, rows] = (gate / (1.0 + jnp.exp(-gate)) * up).astype(BF16)


    def out_cols(p, r):
        lo, size = RS_ROUNDS[r]
        if p == 0 and lo == 0:
            lo, size = GATES, size - GATES
        return lo, size

    def down(r):
        def scatter(p, half):
            lo, size = out_cols(p, r)

            def one(i, carry):
                g = 4 * half + i
                rows = jnp.concatenate(
                    [
                        packed[e, pl.ds(g * SLOTS, SLOTS), 512 * p : 512 * p + size]
                        for e in range(2)
                    ],
                    axis=0,
                )
                tokens = jnp.dot(unpick[g], rows, preferred_element_type=F32).astype(BF16)
                xs[p][half, i, :, :, :, lo : lo + size] = tokens.reshape(4, 4, TOK, size)
                return carry

            lax.fori_loop(0, 4, one, 0, unroll=True)

        def to_twin(p, step):
            src = unit_of(xs[p], (1 - k,), p, r, step)
            recv = qdr.at[p, r, 0 if step == 2 else 1]
            send(src, unit_of(rd[p], (), p, r, step), twin, qds.at[p], recv)

        for p in PARTS:
            lo, size = out_cols(p, r)
            col = p * W + lo - GATES
            for e in range(2):
                part = jnp.dot(hidden[e], wd[e, :, col : col + size], preferred_element_type=F32)
                packed[e, :, 512 * p : 512 * p + size] = (part * row_gate[e, :, 0:1]).astype(BF16)
            scatter(p, 1 - k)
            to_twin(p, 2)
        for p in PARTS:
            for step in (1, 3, 0):
                to_twin(p, step)
        for p in PARTS:
            scatter(p, k)

    def total_into(dst, refs):
        total = refs[0][...].astype(F32)
        for ref in refs[1:]:
            total = total + ref[...].astype(F32)
        dst[...] = total.astype(BF16)

    def unit_of(ref, lead, p, r, step, pieces=1, piece=0):
        a, b, c = ORDER[p]
        fix = {c: (me[c] + step) % 4}
        if pieces == 2:
            fix[b] = pl.ds(2 * piece, 2)
        elif pieces == 4:
            fix[b] = piece
        return at(ref, lead, out_cols(p, r), fix)

    def add_unit(p, r, step):
        def one(i, carry):
            mine = unit_of(xs[p], (k,), p, r, step, 4, i)
            total_into(mine, [mine, unit_of(rd[p], (), p, r, step, 4, i)])
            return carry

        lax.fori_loop(0, 4, one, 0, unroll=True)

    def piece_of(ref, lead, p, r, fix):
        a, b, c = ORDER[p]
        index = [fix.get(axis, slice(None)) for axis in "zyx" if axis != c]
        return ref.at[(*lead, *index, slice(None), pl.ds(*out_cols(p, r)))]

    def a1(r):
        for p in PARTS:
            c = ORDER[p][2]
            wait(unit_of(rd[p], (), p, r, 2), qdr.at[p, r, 0])
            add_unit(p, r, 2)
            for half, way in ((0, 1), (1, -1)):
                src = unit_of(xs[p], (k,), p, r, 2, 2, half)
                send(src, half_slot(p, r, half), device(me, k, c, way), qfs.at[p], qfr.at[p, r, half])

    def b1(r):
        for p in PARTS:
            wait(at(rd[p], (), out_cols(p, r), {"z": pl.ds(0, 3)}), qdr.at[p, r, 1])
            for step in (1, 3, 0):
                add_unit(p, r, step)

    def half_slot(p, r, half, i=None):
        b = ORDER[p][1]
        fix = {} if i is None else {b: i}
        a, b, c = ORDER[p]
        index = [fix.get(axis, slice(None)) for axis in "zyx" if axis != c]
        return rf[p].at[(half, *index, slice(None), pl.ds(*out_cols(p, r)))]

    def s2(r):
        for p in PARTS:
            c = ORDER[p][2]
            for half, way in ((0, 1), (1, -1)):
                wait(half_slot(p, r, half), qfr.at[p, r, half])

                def one(i, carry, half=half, way=way):
                    mine = unit_of(xs[p], (k,), p, r, way, 4, 2 * half + i)
                    total_into(mine, [mine, half_slot(p, r, half, i)])
                    return carry

                lax.fori_loop(0, 2, one, 0, unroll=True)
                src = unit_of(xs[p], (k,), p, r, way)
                slot = piece_of(rr[p], (half,), p, r, {})
                send(src, slot, device(me, k, c, way), q3s.at[p], q3r.at[p, r])

    def s3(r):
        for p in PARTS:
            a, b, c = ORDER[p]
            wait(piece_of(rr[p], (slice(None),), p, r, {}), q3r.at[p, r])

            def one(i, carry, b=b):
                mine = unit_of(xs[p], (k,), p, r, 0, 4, i)
                total_into(mine, [mine] + [piece_of(rr[p], (h,), p, r, {b: i}) for h in range(2)])
                return carry

            lax.fori_loop(0, 4, one, 0, unroll=True)
            for step in (2, 1, 3):
                src = unit_of(xs[p], (k,), p, r, 0, 4, (me[b] + step) % 4)
                slot = rb[p].at[step - 1, :, :, pl.ds(*out_cols(p, r))]
                send(src, slot, device(me, k, b, step), q2s.at[p], q2r.at[p, r])

    def s4(r):
        for p in PARTS:
            a, b, c = ORDER[p]
            cols = pl.ds(*out_cols(p, r))
            wait(rb[p].at[:, :, :, cols], q2r.at[p, r])
            mine = unit_of(xs[p], (k,), p, r, 0, 4, me[b])
            total_into(mine, [mine] + [rb[p].at[j, :, :, cols] for j in range(3)])
            for step in (2, 1, 3):
                src = at(xs[p], (k,), out_cols(p, r), {**me, a: (me[a] + step) % 4})
                send(src, ra[p].at[step - 1, :, cols], device(me, k, a, step), q1s.at[p], q1r.at[p, r])

    def s5(r):
        for p in PARTS:
            lo, size = out_cols(p, r)
            cols = pl.ds(lo, size)
            wait(ra[p].at[:, :, cols], q1r.at[p, r])
            total = at(xs[p], (k,), (lo, size), me)[...].astype(F32)
            for j in range(3):
                total = total + ra[p][j, :, cols].astype(F32)
            col = p * W + lo - GATES
            span = slice(col, col + size)
            out_ref[:, span] = (mixed[:, span].astype(F32) + total).astype(BF16)


    p1_start(1)
    p1_start(2)
    gates()
    p1_start(0)
    for p in (1, 2, 0):
        p2_ahead(p)
    for p in (1, 2, 0):
        p1_wait(p)
        for r in range(3):
            p2_start(p, r)
    p3_start(0)
    p3_start(1)
    p3_forward(0)
    p3_start(2)
    p3_finish(0)
    twin_wait(0)
    selections()
    p3_forward(1)
    everything = pl.ds(0, 8 * SLOTS)
    compact(0, 0)
    compact(0, 1)
    weights_wait(0)
    gate_up(0, everything)
    weights_start(2)
    p3_finish(1)
    p3_forward(2)
    twin_wait(1)
    compact(1, 0)
    compact(1, 1)
    weights_wait(1)
    gate_up(1, everything)
    p3_finish(2)
    weights_wait(2)
    for half in (k, 1 - k):
        if half is not k:
            twin_wait(2)
        compact(2, half)
        gate_up(2, pl.ds(pl.multiple_of(half * 4 * SLOTS, 4 * SLOTS), 4 * SLOTS))
    load_down.wait()
    for p in PARTS:
        wait(xs[p].at[0, 0, 0, pl.ds(0, 3)], p1s.at[p])
        wait(xs[p].at[0, 0, pl.ds(0, 3)], p2s.at[p])
        wait(xs[p].at[0, pl.ds(0, 3)], p3s.at[p])
        wait(xs[p].at[0], ds.at[p])
    down(0)
    a1(0)
    down(1)
    b1(0)
    a1(1)
    s2(0)
    down(2)
    b1(1)
    a1(2)
    s2(1)
    b1(2)
    s3(0)
    s2(2)
    s4(0)
    s3(1)
    s5(0)
    s4(1)
    s3(2)
    s5(1)
    s4(2)
    s5(2)
    wait(kv.at[pl.ds(0, 3)], kv_send)
    for i in range(4):
        wait(from_ring.at[:, :, pl.ds(i * 1024, 1024)], ring_send.at[i])
    for p in PARTS:
        first = out_cols(p, 0)[0]
        cols = pl.ds(first, W - first)
        wait(xs[p].at[0, :, :, :, :, cols], qds.at[p])
        wait(rf[p].at[:, :, :, :, cols], qfs.at[p])
        wait(rr[p].at[:, :, :, :, cols], q3s.at[p])
        wait(rb[p].at[:, :, :, cols], q2s.at[p])
        wait(ra[p].at[:, :, cols], q1s.at[p])


def on_device(
    query_rows,
    key_rows,
    value_rows,
    residual,
    out_proj,
    post_gain,
    router,
    routes,
    w_gate,
    w_up,
    w_down,
):
    vmem = pltpu.VMEM
    hbm = pl.BlockSpec(memory_space=pl.ANY)
    dma = pltpu.SemaphoreType.DMA
    cosine, sine = rope_tables()
    n = len(RS_ROUNDS)

    def half_shape(p):
        a, b, c = ORDER[p]
        return (2, *[2 if axis == b else 4 for axis in "zyx" if axis != c], TOK, W)

    scratch = (
        [
            vmem((LOCAL, HEADS * HEAD), BF16),
            vmem((TOK, D), BF16),
            vmem((D // 128, 128), BF16),
            vmem((EXPERTS, D), BF16),
            vmem((8, TOK), jnp.int32),
            vmem((SEQ, HEAD), F32),
            vmem((SEQ, HEAD), F32),
            vmem((4, 2, LOCAL, HEAD), BF16),
            vmem((HEADS * LOCAL, HEAD), BF16),
            vmem((SEQ, HEAD), BF16),
            vmem((4, TOK, D), BF16),
            vmem((4, TOK, D), BF16),
            vmem((3, TOK, D), BF16),
            vmem((TOK, D), BF16),
        ]
        + [vmem((2, 4, 4, 4, TOK, W), BF16)] * 3
        + [vmem((4, 4, 4, TOK, W), BF16)] * 3
        + [vmem(half_shape(p), BF16) for p in PARTS]
        + [vmem((2, 4, 4, TOK, W), BF16)] * 3
        + [vmem((3, 4, TOK, W), BF16)] * 3
        + [vmem((3, TOK, W), BF16)] * 3
        + [
            vmem((2, 2, 1536, 2 * FF), BF16),
            vmem((2, FF, D), BF16),
            vmem((2, 8 * SLOTS, 1536), BF16),
            vmem((2, 8 * SLOTS, 2 * FF), F32),
            vmem((2, 8 * SLOTS, FF), BF16),
            vmem((8, 2 * SLOTS, GROUP), BF16),
            vmem((8, GROUP, 2 * SLOTS), BF16),
            vmem((2, 8 * SLOTS, 128), F32),
        ]
        + [dma((11,)), dma, dma, dma((4,)), dma((4,)), dma((4,)), dma((4,))]
        + [dma((4,)), dma((3,)), dma((3,)), dma((3,)), dma((3, 4)), dma((3,)), dma((3, 3, 3))]
        + [dma((3,)), dma((3, 3))]
        + [dma((3,)), dma((3, n, 2)), dma((3,)), dma((3, n, 2))]
        + [dma((3,)), dma((3, n))] * 3
    )
    out = pl.pallas_call(
        layer_kernel,
        out_shape=jax.ShapeDtypeStruct((TOK, D), BF16),
        in_specs=[hbm] * 13,
        out_specs=pl.BlockSpec(memory_space=pltpu.VMEM),
        scratch_shapes=scratch,
        compiler_params=pltpu.CompilerParams(
            collective_id=0, has_side_effects=True, vmem_limit_bytes=VMEM
        ),
    )(
        query_rows, key_rows, value_rows, residual, out_proj, post_gain.reshape(D // 128, 128),
        router.T, jnp.swapaxes(routes, 1, 2), jnp.asarray(cosine), jnp.asarray(sine),
        w_gate, w_up, w_down,
    )
    return out[None]


def solution(mesh):
    in_specs = (
        P("dp", "ctx", "tensor"),
        P("dp", "ctx", None),
        P("dp", "ctx", None),
        P("dp", ("ctx", "tensor"), None),
        P("tensor", None),
        P(),
        P(),
        P("dp", ("ctx", "tensor"), None),
        P(("ctx", "tensor"), None, "dp"),
        P(("ctx", "tensor"), None, "dp"),
        P(("ctx", "tensor"), "dp", None),
    )
    out_specs = P("dp", ("ctx", "tensor"), None)
    return jax.shard_map(
        on_device, mesh=mesh, in_specs=in_specs, out_specs=out_specs, check_vma=False
    )
```

```python
import jax
import jax.numpy as jnp
import numpy as np
from jax import lax
from jax.experimental import pallas as pl
from jax.experimental.pallas import tpu as pltpu
from jax.sharding import PartitionSpec as P

MESH = pl.DeviceIdType.MESH
F32 = jnp.float32
BF16 = jnp.bfloat16

D = 4096
HEAD = 128
HEADS = 4
SEQ = 512
LOCAL = 128
TOK = 16
EXPERTS = 64
FF = 384
CAP = 4
GATES = 128
WIDE = D + GATES
W = WIDE // 3
GROUP = 256
SLOTS = TOK * CAP

ORDER = (("x", "y", "z"), ("y", "z", "x"), ("z", "x", "y"))
PARTS = range(3)
AG_ROUNDS = ((0, 384), (384, 512), (896, 512))
RS_ROUNDS = ((0, 384), (384, 512), (896, 512))
VMEM = 63 * 2**20


def rope_tables():
    half = HEAD // 2
    places = np.arange(SEQ).astype(np.float32)
    freqs = np.power(
        np.float32(1000000.0), -(np.arange(half).astype(np.float32) * np.float32(2.0) / np.float32(HEAD))
    ).astype(np.float32)
    angles = (places[:, None] * freqs[None, :]).astype(np.float32)
    cosine, sine = np.cos(angles), np.sin(angles)
    return (
        np.concatenate([cosine, cosine], axis=1).astype(np.float32),
        np.concatenate([-sine, sine], axis=1).astype(np.float32),
    )


def place():
    t = lax.axis_index("tensor")
    return {"x": t // 2, "y": lax.axis_index("ctx"), "z": lax.axis_index("dp")}, t % 2


def device(me, k, axis, step):
    value = (me[axis] + step) % 4
    if axis == "x":
        return {"tensor": value * 2 + k}
    return {"ctx" if axis == "y" else "dp": value}


def sibling(me, k):
    return {"tensor": me["x"] * 2 + 1 - k}


def greet(me, k, axes):
    barrier = pltpu.get_barrier_semaphore()
    for axis in axes:
        for step in (1, 2, 3):
            pl.semaphore_signal(
                barrier, inc=1, device_id=device(me, k, axis, step), device_id_type=MESH
            )
    pl.semaphore_signal(barrier, inc=1, device_id=sibling(me, k), device_id_type=MESH)
    pl.semaphore_wait(barrier, 3 * len(axes) + 1)


def send(src, dst, to, send_sem, recv_sem):
    pltpu.make_async_remote_copy(
        src_ref=src,
        dst_ref=dst,
        send_sem=send_sem,
        recv_sem=recv_sem,
        device_id=to,
        device_id_type=MESH,
    ).start()


def wait(ref, sem):
    pltpu.make_async_copy(ref, ref, sem).wait()


def turn(values, cosine, sine):
    values = values.astype(F32)
    return (values * cosine + pltpu.roll(values, HEAD // 2, 1) * sine).astype(BF16)


def layer_kernel(
    query_hbm, key_hbm, value_hbm, residual_hbm, proj_hbm, gain_hbm, router_hbm, routes_hbm,
    cos_hbm, sin_hbm, gate_hbm, up_hbm, down_hbm, out_ref,
    query, residual, gain, router, routes, cosine, sine,
    kv, qrot, krot, far, from_sibling, from_ring, mixed,
    x0, x1, x2, rd0, rd1, rd2, rf0, rf1, rf2, rr0, rr1, rr2, rb0, rb1, rb2, ra0, ra1, ra2,
    wgu, wd, packed, acc, hidden, pick, unpick, row_gate,
    in_sem, kv_send, kv_recv, sib_send, sib_recv, ring_send, ring_recv,
    w_sem, p1s, p1r, p2s, p2r, p3s, p3r, ds, dr,
    qds, qdr, qfs, qfr, q3s, q3r, q2s, q2r, q1s, q1r,
):
    xs, rd, rf, rr = (x0, x1, x2), (rd0, rd1, rd2), (rf0, rf1, rf2), (rr0, rr1, rr2)
    rb, ra = (rb0, rb1, rb2), (ra0, ra1, ra2)
    me, k = place()
    twin = sibling(me, k)

    def spans(r):
        found, at_col = [], 0
        for p in PARTS:
            lo, size = AG_ROUNDS[r]
            if p == 0 and lo == 0:
                lo, size = GATES, size - GATES
            found.append((p, lo, size, at_col))
            at_col += size
        return found

    def weights(r):
        copies = []
        for e in range(2):
            for n, hbm in enumerate((gate_hbm, up_hbm)):
                for p, lo, size, col in spans(r):
                    from_row = p * W + lo - GATES
                    copies.append(
                        pltpu.make_async_copy(
                            hbm.at[e, pl.ds(from_row, size), :],
                            wgu.at[r % 2, e, pl.ds(col, size), pl.ds(n * FF, FF)],
                            w_sem.at[r],
                        )
                    )
        return copies

    def weights_start(r):
        for copy in weights(r):
            copy.start()

    def weights_wait(r):
        total = sum(size for p, lo, size, col in spans(r))
        wait(wgu.at[r % 2, :, pl.ds(0, total), :], w_sem.at[r])

    load_down = pltpu.make_async_copy(down_hbm, wd, w_sem.at[3])


    head = pl.multiple_of((lax.axis_index("tensor") // 4) * HEAD, HEAD)
    y = me["y"]
    loads = [
        pltpu.make_async_copy(src, dst, in_sem.at[i])
        for i, (src, dst) in enumerate(
            (
                (key_hbm.at[0, :, pl.ds(head, HEAD)], kv.at[y, 0]),
                (value_hbm.at[0, :, pl.ds(head, HEAD)], kv.at[y, 1]),
                (query_hbm.at[0], query),
                (cos_hbm, cosine),
                (sin_hbm, sine),
                (proj_hbm.at[pl.ds(0, FF)], wd.at[0]),
                (proj_hbm.at[pl.ds(FF, HEADS * HEAD - FF)], wd.at[1, pl.ds(0, HEADS * HEAD - FF)]),
                (residual_hbm.at[0], residual),
                (gain_hbm, gain),
                (router_hbm, router),
                (routes_hbm.at[0], routes),
            )
        )
    ]
    for load in loads:
        load.start()
    weights_start(0)
    weights_start(1)
    greet(me, k, "xyz")
    for load in loads[:2]:
        load.wait()
    for step in (2, 1, 3):
        send(kv.at[y], kv.at[y], device(me, k, "y", step), kv_send, kv_recv)
    for load in loads[2:5]:
        load.wait()
    own = pl.ds(pl.multiple_of(y * LOCAL, LOCAL), LOCAL)
    for h in range(HEADS):
        qrot[pl.ds(h * LOCAL, LOCAL), :] = turn(
            query[:, h * HEAD : (h + 1) * HEAD], cosine[own, :], sine[own, :]
        )
    wait(kv.at[pl.ds(0, 3)], kv_recv)
    for c in range(4):
        span = pl.ds(c * LOCAL, LOCAL)
        krot[span, :] = turn(kv[c, 0], cosine[span, :], sine[span, :])
    values = kv[:, 1].reshape(SEQ, HEAD)
    place_q = y * LOCAL + lax.broadcasted_iota(jnp.int32, (LOCAL, SEQ), 0)
    causal = place_q >= lax.broadcasted_iota(jnp.int32, (LOCAL, SEQ), 1)
    attended = []
    for h in range(HEADS):
        score = lax.dot_general(
            qrot[pl.ds(h * LOCAL, LOCAL), :], krot[...], (((1,), (1,)), ((), ())),
            preferred_element_type=F32,
        ) * F32(HEAD**-0.5)
        score = jnp.where(causal, score, F32(-1e30))
        peak = jnp.max(score, axis=-1, keepdims=True)
        expon = jnp.exp(score - peak)
        total = jnp.sum(expon, axis=-1, keepdims=True)
        summed = jnp.dot(expon.astype(BF16), values, preferred_element_type=F32)
        attended.append((summed / total).astype(BF16))
    attended = jnp.concatenate(attended, axis=1)
    for load in loads[5:]:
        load.wait()
    for c in range(8):
        cols = slice(c * 512, (c + 1) * 512)
        out = jnp.dot(attended[:, :FF], wd[0, :, cols], preferred_element_type=F32) + jnp.dot(
            attended[:, FF:], wd[1, : HEADS * HEAD - FF, cols], preferred_element_type=F32
        )
        acc[c // 4, pl.ds((c % 4) * LOCAL, LOCAL), :512] = out
        for v in range(4):
            rows = pl.ds(pl.multiple_of((c % 4) * LOCAL + (2 * v + 1 - k) * TOK, TOK), TOK)
            far[v, :, cols] = acc[c // 4, rows, :512].astype(BF16)
        if c % 2 == 1:
            half = pl.ds((c // 2) * 1024, 1024)
            send(
                far.at[:, :, half], from_sibling.at[:, :, half], twin,
                sib_send.at[c // 2], sib_recv.at[c // 2],
            )
    load_down.start()

    def chip_sum(v, c):
        rows = pl.ds(pl.multiple_of((c % 4) * LOCAL + (2 * v + k) * TOK, TOK), TOK)
        return acc[c // 4, rows, :512] + from_sibling[v, :, c * 512 : (c + 1) * 512].astype(F32)

    for i in range(4):
        half = pl.ds(i * 1024, 1024)
        wait(far.at[:, :, half], sib_send.at[i])
        wait(from_sibling.at[:, :, half], sib_recv.at[i])
        for step in (2, 1, 3):
            v = (me["x"] + step) % 4
            for c in range(2 * i, 2 * i + 2):
                far[v, :, c * 512 : (c + 1) * 512] = chip_sum(v, c).astype(BF16)
            send(
                far.at[v, :, half], from_ring.at[step - 1, :, half], device(me, k, "x", step),
                ring_send.at[i], ring_recv.at[i],
            )
    square = jnp.zeros((TOK, 1), F32)
    for c in range(8):
        cols = slice(c * 512, (c + 1) * 512)
        if c % 2 == 0:
            wait(from_ring.at[:, :, pl.ds((c // 2) * 1024, 1024)], ring_recv.at[c // 2])
        projected = chip_sum(me["x"], c)
        for j in range(3):
            projected = projected + from_ring[j, :, cols].astype(F32)
        wide = (residual[:, cols].astype(F32) + projected).astype(BF16)
        mixed[:, cols] = wide
        wide = wide.astype(F32)
        square = square + jnp.sum(wide * wide, axis=-1, keepdims=True)
    scale = lax.rsqrt(square / D + 1e-06)
    for c in range(D // 128):
        wide = mixed[:, c * 128 : (c + 1) * 128].astype(F32)
        normed = (wide * scale * gain[c : c + 1, :].astype(F32)).astype(BF16)
        col = GATES + c * 128
        xs[col // W][k, me["z"], me["y"], me["x"], :, col % W : col % W + 128] = normed
    def at(ref, lead, cols, fix):
        index = [fix.get(axis, slice(None)) for axis in "zyx"]
        return ref.at[(*lead, *index, slice(None), pl.ds(*cols))]


    def p1_start(p):
        a = ORDER[p][0]
        block = at(xs[p], (k,), (0, W), me)
        for step in (2, 1, 3):
            send(block, block, device(me, k, a, step), p1s.at[p], p1r.at[p])

    def p1_wait(p):
        wait(xs[p].at[0, 0, 0, pl.ds(0, 3)], p1r.at[p])

    def p2_ahead(p):
        b = ORDER[p][1]
        block = at(xs[p], (k,), (0, W), me)
        for step in (2, 1, 3):
            send(block, block, device(me, k, b, step), p2s.at[p], p2r.at[p, 3])

    def p2_start(p, r):
        a, b, c = ORDER[p]
        for step in (2, 1, 3):
            for other in (1, 2, 3):
                unit = at(xs[p], (k,), AG_ROUNDS[r], {**me, a: (me[a] + other) % 4})
                send(unit, unit, device(me, k, b, step), p2s.at[p], p2r.at[p, r])

    def p2_bytes(p, r):
        return xs[p].at[0, 0, pl.ds(0, 3), pl.ds(0, 3), :, pl.ds(*AG_ROUNDS[r])]

    def p3_unit(p, r, step, half=None):
        a, b, c = ORDER[p]
        fix = {c: (me[c] + step) % 4}
        if half is not None:
            fix[b] = pl.ds(2 * half, 2)
        return at(xs[p], (k,), AG_ROUNDS[r], fix)

    def p3_send(p, r, step, half, way):
        unit = p3_unit(p, r, step, half)
        recv = p3r.at[p, r, 2] if half is not None else p3r.at[p, r, 0 if way == 1 else 1]
        send(unit, unit, device(me, k, ORDER[p][2], way), p3s.at[p], recv)

    def twin_send(p, r, step):
        unit = p3_unit(p, r, step)
        send(unit, unit, twin, ds.at[p], dr.at[p, r])

    def p3_start(r):
        for p in PARTS:
            if r == 0:
                wait(xs[p].at[0, 0, 0, pl.ds(0, 3)], p2r.at[p, 3])
            wait(p2_bytes(p, r), p2r.at[p, r])
            p3_send(p, r, 0, None, 1)
            p3_send(p, r, 0, None, -1)

    def p3_forward(r):
        for p in PARTS:
            wait(p3_unit(p, r, -1), p3r.at[p, r, 0])
            p3_send(p, r, -1, 0, 1)
            wait(p3_unit(p, r, 1), p3r.at[p, r, 1])
            p3_send(p, r, 1, 1, -1)
        for p in PARTS:
            for step in (0, -1, 1):
                twin_send(p, r, step)

    def p3_finish(r):
        for p in PARTS:
            wait(p3_unit(p, r, 2), p3r.at[p, r, 2])
            twin_send(p, r, 2)

    def twin_wait(r):
        for p in PARTS:
            wait(xs[p].at[1 - k, :, :, :, :, pl.ds(*AG_ROUNDS[r])], dr.at[p, r])

    def gates():
        logits = jnp.zeros((EXPERTS, TOK), F32)
        for p in PARTS:
            lo = GATES if p == 0 else 0
            col = p * W + lo - GATES
            normed = xs[p][k, me["z"], me["y"], me["x"], :, lo:W]
            logits = logits + lax.dot_general(
                router[:, col : col + W - lo], normed, (((1,), (1,)), ((), ())),
                preferred_element_type=F32,
            )
        expert = lax.broadcasted_iota(jnp.int32, (EXPERTS, TOK), 0)
        chosen = expert == routes[0:1, :]
        for j in range(1, 8):
            chosen = jnp.logical_or(chosen, expert == routes[j : j + 1, :])
        peak = jnp.max(jnp.where(chosen, logits, F32(-3e38)), axis=0, keepdims=True)
        expon = jnp.where(chosen, jnp.exp(logits - peak), F32(0.0))
        gate = expon / jnp.sum(expon, axis=0, keepdims=True)
        high = gate.astype(BF16).astype(F32)
        both = jnp.concatenate([high, gate - high], axis=0).astype(BF16)
        unit = lax.broadcasted_iota(jnp.int32, (TOK, TOK), 0) == lax.broadcasted_iota(
            jnp.int32, (TOK, TOK), 1
        )
        turned = lax.dot_general(
            unit.astype(F32).astype(BF16), both, (((1,), (1,)), ((), ())), preferred_element_type=F32
        )
        x0[k, me["z"], me["y"], me["x"], :, :GATES] = turned.astype(BF16)


    def selections():
        first = 2 * (me["y"] * 8 + lax.axis_index("tensor"))
        rows = lax.broadcasted_iota(jnp.int32, (8, GATES), 0)
        lanes = lax.broadcasted_iota(jnp.int32, (8, GATES), 1)
        mine = jnp.logical_and(lanes % EXPERTS == first + rows, rows < 2).astype(F32).astype(BF16)
        s = lax.broadcasted_iota(jnp.int32, (GROUP, GROUP), 0)
        u = lax.broadcasted_iota(jnp.int32, (GROUP, GROUP), 1)
        earlier = jnp.logical_and(s // TOK == u // TOK, s < u).astype(F32).astype(BF16)
        base = (lax.broadcasted_iota(jnp.int32, (1, GROUP), 1) // TOK * CAP).astype(F32)
        slots = lax.broadcasted_iota(jnp.int32, (SLOTS, GROUP), 0).astype(F32)

        def one(g, carry):
            tile = x0[g // 4, g % 4, :, :, :, :GATES].reshape(GROUP, GATES)
            gate = lax.dot_general(mine, tile, (((1,), (1,)), ((), ())), preferred_element_type=F32)
            named = (gate > 0).astype(F32)
            rank = jnp.dot(named.astype(BF16), earlier, preferred_element_type=F32)
            both = []
            for e in range(2):
                hit = jnp.logical_and(slots == rank[e : e + 1] + base, gate[e : e + 1] > 0).astype(F32)
                worth = jnp.sum(hit * gate[e : e + 1], axis=1, keepdims=True)
                row_gate[e, pl.ds(g * SLOTS, SLOTS), :] = jnp.broadcast_to(worth, (SLOTS, 128))
                both.append(hit)
            both = jnp.concatenate(both, axis=0)
            pick[g] = both.astype(BF16)
            unpick[g] = both.T.astype(BF16)
            return carry

        lax.fori_loop(0, 8, one, 0, unroll=True)

    def compact(r, half):
        for p, lo, size, col in spans(r):
            for z in range(4):
                tokens = xs[p][half, z, :, :, :, lo : lo + size].reshape(GROUP, size)
                rows = jnp.dot(pick[4 * half + z], tokens, preferred_element_type=F32).astype(BF16)
                for e in range(2):
                    span = pl.ds((4 * half + z) * SLOTS, SLOTS)
                    packed[e, span, col : col + size] = rows[e * SLOTS : (e + 1) * SLOTS]

    def gate_up(r, rows):
        depth = sum(size for p, lo, size, col in spans(r))
        for e in range(2):
            total = jnp.dot(
                packed[e, rows, :depth], wgu[r % 2, e, :depth, :], preferred_element_type=F32
            )
            if r > 0:
                total = total + acc[e, rows]
            if r < len(AG_ROUNDS) - 1:
                acc[e, rows] = total
            else:
                gate, up = total[:, :FF], total[:, FF:]
                hidden[e, rows] = (gate / (1.0 + jnp.exp(-gate)) * up).astype(BF16)


    def out_cols(p, r):
        lo, size = RS_ROUNDS[r]
        if p == 0 and lo == 0:
            lo, size = GATES, size - GATES
        return lo, size

    def down(r):
        def scatter(p, half):
            lo, size = out_cols(p, r)

            def one(i, carry):
                g = 4 * half + i
                rows = jnp.concatenate(
                    [
                        packed[e, pl.ds(g * SLOTS, SLOTS), 512 * p : 512 * p + size]
                        for e in range(2)
                    ],
                    axis=0,
                )
                tokens = jnp.dot(unpick[g], rows, preferred_element_type=F32).astype(BF16)
                xs[p][half, i, :, :, :, lo : lo + size] = tokens.reshape(4, 4, TOK, size)
                return carry

            lax.fori_loop(0, 4, one, 0, unroll=True)

        def to_twin(p, step):
            src = unit_of(xs[p], (1 - k,), p, r, step)
            recv = qdr.at[p, r, 0 if step == 2 else 1]
            send(src, unit_of(rd[p], (), p, r, step), twin, qds.at[p], recv)

        for p in PARTS:
            lo, size = out_cols(p, r)
            col = p * W + lo - GATES
            for e in range(2):
                part = jnp.dot(hidden[e], wd[e, :, col : col + size], preferred_element_type=F32)
                packed[e, :, 512 * p : 512 * p + size] = (part * row_gate[e, :, 0:1]).astype(BF16)
            scatter(p, 1 - k)
            to_twin(p, 2)
        for p in PARTS:
            for step in (1, 3, 0):
                to_twin(p, step)
        for p in PARTS:
            scatter(p, k)

    def total_into(dst, refs):
        total = refs[0][...].astype(F32)
        for ref in refs[1:]:
            total = total + ref[...].astype(F32)
        dst[...] = total.astype(BF16)

    def unit_of(ref, lead, p, r, step, pieces=1, piece=0):
        a, b, c = ORDER[p]
        fix = {c: (me[c] + step) % 4}
        if pieces == 2:
            fix[b] = pl.ds(2 * piece, 2)
        elif pieces == 4:
            fix[b] = piece
        return at(ref, lead, out_cols(p, r), fix)

    def add_unit(p, r, step):
        def one(i, carry):
            mine = unit_of(xs[p], (k,), p, r, step, 4, i)
            total_into(mine, [mine, unit_of(rd[p], (), p, r, step, 4, i)])
            return carry

        lax.fori_loop(0, 4, one, 0, unroll=True)

    def piece_of(ref, lead, p, r, fix):
        a, b, c = ORDER[p]
        index = [fix.get(axis, slice(None)) for axis in "zyx" if axis != c]
        return ref.at[(*lead, *index, slice(None), pl.ds(*out_cols(p, r)))]

    def a1(r):
        for p in PARTS:
            c = ORDER[p][2]
            wait(unit_of(rd[p], (), p, r, 2), qdr.at[p, r, 0])
            add_unit(p, r, 2)
            for half, way in ((0, 1), (1, -1)):
                src = unit_of(xs[p], (k,), p, r, 2, 2, half)
                send(src, half_slot(p, r, half), device(me, k, c, way), qfs.at[p], qfr.at[p, r, half])

    def b1(r):
        for p in PARTS:
            wait(at(rd[p], (), out_cols(p, r), {"z": pl.ds(0, 3)}), qdr.at[p, r, 1])
            for step in (1, 3, 0):
                add_unit(p, r, step)

    def half_slot(p, r, half, i=None):
        b = ORDER[p][1]
        fix = {} if i is None else {b: i}
        a, b, c = ORDER[p]
        index = [fix.get(axis, slice(None)) for axis in "zyx" if axis != c]
        return rf[p].at[(half, *index, slice(None), pl.ds(*out_cols(p, r)))]

    def s2(r):
        for p in PARTS:
            c = ORDER[p][2]
            for half, way in ((0, 1), (1, -1)):
                wait(half_slot(p, r, half), qfr.at[p, r, half])

                def one(i, carry, half=half, way=way):
                    mine = unit_of(xs[p], (k,), p, r, way, 4, 2 * half + i)
                    total_into(mine, [mine, half_slot(p, r, half, i)])
                    return carry

                lax.fori_loop(0, 2, one, 0, unroll=True)
                src = unit_of(xs[p], (k,), p, r, way)
                slot = piece_of(rr[p], (half,), p, r, {})
                send(src, slot, device(me, k, c, way), q3s.at[p], q3r.at[p, r])

    def s3(r):
        for p in PARTS:
            a, b, c = ORDER[p]
            wait(piece_of(rr[p], (slice(None),), p, r, {}), q3r.at[p, r])

            def one(i, carry, b=b):
                mine = unit_of(xs[p], (k,), p, r, 0, 4, i)
                total_into(mine, [mine] + [piece_of(rr[p], (h,), p, r, {b: i}) for h in range(2)])
                return carry

            lax.fori_loop(0, 4, one, 0, unroll=True)
            for step in (2, 1, 3):
                src = unit_of(xs[p], (k,), p, r, 0, 4, (me[b] + step) % 4)
                slot = rb[p].at[step - 1, :, :, pl.ds(*out_cols(p, r))]
                send(src, slot, device(me, k, b, step), q2s.at[p], q2r.at[p, r])

    def s4(r):
        for p in PARTS:
            a, b, c = ORDER[p]
            cols = pl.ds(*out_cols(p, r))
            wait(rb[p].at[:, :, :, cols], q2r.at[p, r])
            mine = unit_of(xs[p], (k,), p, r, 0, 4, me[b])
            total_into(mine, [mine] + [rb[p].at[j, :, :, cols] for j in range(3)])
            for step in (2, 1, 3):
                src = at(xs[p], (k,), out_cols(p, r), {**me, a: (me[a] + step) % 4})
                send(src, ra[p].at[step - 1, :, cols], device(me, k, a, step), q1s.at[p], q1r.at[p, r])

    def s5(r):
        for p in PARTS:
            lo, size = out_cols(p, r)
            cols = pl.ds(lo, size)
            wait(ra[p].at[:, :, cols], q1r.at[p, r])
            total = at(xs[p], (k,), (lo, size), me)[...].astype(F32)
            for j in range(3):
                total = total + ra[p][j, :, cols].astype(F32)
            col = p * W + lo - GATES
            span = slice(col, col + size)
            out_ref[:, span] = (mixed[:, span].astype(F32) + total).astype(BF16)


    p1_start(1)
    p1_start(2)
    gates()
    p1_start(0)
    for p in (1, 2, 0):
        p2_ahead(p)
    for p in (1, 2, 0):
        p1_wait(p)
        for r in range(3):
            p2_start(p, r)
    p3_start(0)
    p3_start(1)
    p3_forward(0)
    p3_start(2)
    p3_finish(0)
    twin_wait(0)
    selections()
    p3_forward(1)
    everything = pl.ds(0, 8 * SLOTS)
    compact(0, 0)
    compact(0, 1)
    weights_wait(0)
    gate_up(0, everything)
    weights_start(2)
    p3_finish(1)
    p3_forward(2)
    twin_wait(1)
    compact(1, 0)
    compact(1, 1)
    weights_wait(1)
    gate_up(1, everything)
    p3_finish(2)
    weights_wait(2)
    for half in (k, 1 - k):
        if half is not k:
            twin_wait(2)
        compact(2, half)
        gate_up(2, pl.ds(pl.multiple_of(half * 4 * SLOTS, 4 * SLOTS), 4 * SLOTS))
    load_down.wait()
    for p in PARTS:
        wait(xs[p].at[0, 0, 0, pl.ds(0, 3)], p1s.at[p])
        wait(xs[p].at[0, 0, pl.ds(0, 3)], p2s.at[p])
        wait(xs[p].at[0, pl.ds(0, 3)], p3s.at[p])
        wait(xs[p].at[0], ds.at[p])
    down(0)
    a1(0)
    down(1)
    b1(0)
    a1(1)
    s2(0)
    down(2)
    b1(1)
    a1(2)
    s2(1)
    b1(2)
    s3(0)
    s2(2)
    s3(1)
    s4(0)
    s3(2)
    s4(1)
    s5(0)
    s4(2)
    s5(1)
    s5(2)
    wait(kv.at[pl.ds(0, 3)], kv_send)
    for i in range(4):
        wait(from_ring.at[:, :, pl.ds(i * 1024, 1024)], ring_send.at[i])
    for p in PARTS:
        first = out_cols(p, 0)[0]
        cols = pl.ds(first, W - first)
        wait(xs[p].at[0, :, :, :, :, cols], qds.at[p])
        wait(rf[p].at[:, :, :, :, cols], qfs.at[p])
        wait(rr[p].at[:, :, :, :, cols], q3s.at[p])
        wait(rb[p].at[:, :, :, cols], q2s.at[p])
        wait(ra[p].at[:, :, cols], q1s.at[p])


def on_device(
    query_rows,
    key_rows,
    value_rows,
    residual,
    out_proj,
    post_gain,
    router,
    routes,
    w_gate,
    w_up,
    w_down,
):
    vmem = pltpu.VMEM
    hbm = pl.BlockSpec(memory_space=pl.ANY)
    dma = pltpu.SemaphoreType.DMA
    cosine, sine = rope_tables()
    n = len(RS_ROUNDS)

    def half_shape(p):
        a, b, c = ORDER[p]
        return (2, *[2 if axis == b else 4 for axis in "zyx" if axis != c], TOK, W)

    scratch = (
        [
            vmem((LOCAL, HEADS * HEAD), BF16),
            vmem((TOK, D), BF16),
            vmem((D // 128, 128), BF16),
            vmem((EXPERTS, D), BF16),
            vmem((8, TOK), jnp.int32),
            vmem((SEQ, HEAD), F32),
            vmem((SEQ, HEAD), F32),
            vmem((4, 2, LOCAL, HEAD), BF16),
            vmem((HEADS * LOCAL, HEAD), BF16),
            vmem((SEQ, HEAD), BF16),
            vmem((4, TOK, D), BF16),
            vmem((4, TOK, D), BF16),
            vmem((3, TOK, D), BF16),
            vmem((TOK, D), BF16),
        ]
        + [vmem((2, 4, 4, 4, TOK, W), BF16)] * 3
        + [vmem((4, 4, 4, TOK, W), BF16)] * 3
        + [vmem(half_shape(p), BF16) for p in PARTS]
        + [vmem((2, 4, 4, TOK, W), BF16)] * 3
        + [vmem((3, 4, TOK, W), BF16)] * 3
        + [vmem((3, TOK, W), BF16)] * 3
        + [
            vmem((2, 2, 1536, 2 * FF), BF16),
            vmem((2, FF, D), BF16),
            vmem((2, 8 * SLOTS, 1536), BF16),
            vmem((2, 8 * SLOTS, 2 * FF), F32),
            vmem((2, 8 * SLOTS, FF), BF16),
            vmem((8, 2 * SLOTS, GROUP), BF16),
            vmem((8, GROUP, 2 * SLOTS), BF16),
            vmem((2, 8 * SLOTS, 128), F32),
        ]
        + [dma((11,)), dma, dma, dma((4,)), dma((4,)), dma((4,)), dma((4,))]
        + [dma((4,)), dma((3,)), dma((3,)), dma((3,)), dma((3, 4)), dma((3,)), dma((3, 3, 3))]
        + [dma((3,)), dma((3, 3))]
        + [dma((3,)), dma((3, n, 2)), dma((3,)), dma((3, n, 2))]
        + [dma((3,)), dma((3, n))] * 3
    )
    out = pl.pallas_call(
        layer_kernel,
        out_shape=jax.ShapeDtypeStruct((TOK, D), BF16),
        in_specs=[hbm] * 13,
        out_specs=pl.BlockSpec(memory_space=pltpu.VMEM),
        scratch_shapes=scratch,
        compiler_params=pltpu.CompilerParams(
            collective_id=0, has_side_effects=True, vmem_limit_bytes=VMEM
        ),
    )(
        query_rows, key_rows, value_rows, residual, out_proj, post_gain.reshape(D // 128, 128),
        router.T, jnp.swapaxes(routes, 1, 2), jnp.asarray(cosine), jnp.asarray(sine),
        w_gate, w_up, w_down,
    )
    return out[None]


def solution(mesh):
    in_specs = (
        P("dp", "ctx", "tensor"),
        P("dp", "ctx", None),
        P("dp", "ctx", None),
        P("dp", ("ctx", "tensor"), None),
        P("tensor", None),
        P(),
        P(),
        P("dp", ("ctx", "tensor"), None),
        P(("ctx", "tensor"), None, "dp"),
        P(("ctx", "tensor"), None, "dp"),
        P(("ctx", "tensor"), "dp", None),
    )
    out_specs = P("dp", ("ctx", "tensor"), None)
    return jax.shard_map(
        on_device, mesh=mesh, in_specs=in_specs, out_specs=out_specs, check_vma=False
    )
```

```python
import jax
import jax.numpy as jnp
import numpy as np
from jax import lax
from jax.experimental import pallas as pl
from jax.experimental.pallas import tpu as pltpu
from jax.sharding import PartitionSpec as P

MESH = pl.DeviceIdType.MESH
F32 = jnp.float32
BF16 = jnp.bfloat16

D = 4096
HEAD = 128
HEADS = 4
SEQ = 512
LOCAL = 128
TOK = 16
EXPERTS = 64
FF = 384
CAP = 4
GATES = 128
WIDE = D + GATES
W = WIDE // 3
GROUP = 256
SLOTS = TOK * CAP

ORDER = (("x", "y", "z"), ("y", "z", "x"), ("z", "x", "y"))
PARTS = range(3)
AG_ROUNDS = ((0, 384), (384, 512), (896, 512))
RS_ROUNDS = ((0, 384), (384, 512), (896, 512))
VMEM = 63 * 2**20


def rope_tables():
    half = HEAD // 2
    places = np.arange(SEQ).astype(np.float32)
    freqs = np.power(
        np.float32(1000000.0), -(np.arange(half).astype(np.float32) * np.float32(2.0) / np.float32(HEAD))
    ).astype(np.float32)
    angles = (places[:, None] * freqs[None, :]).astype(np.float32)
    cosine, sine = np.cos(angles), np.sin(angles)
    return (
        np.concatenate([cosine, cosine], axis=1).astype(np.float32),
        np.concatenate([-sine, sine], axis=1).astype(np.float32),
    )


def place():
    t = lax.axis_index("tensor")
    return {"x": t // 2, "y": lax.axis_index("ctx"), "z": lax.axis_index("dp")}, t % 2


def device(me, k, axis, step):
    value = (me[axis] + step) % 4
    if axis == "x":
        return {"tensor": value * 2 + k}
    return {"ctx" if axis == "y" else "dp": value}


def sibling(me, k):
    return {"tensor": me["x"] * 2 + 1 - k}


def greet(me, k, axes):
    barrier = pltpu.get_barrier_semaphore()
    for axis in axes:
        for step in (1, 2, 3):
            pl.semaphore_signal(
                barrier, inc=1, device_id=device(me, k, axis, step), device_id_type=MESH
            )
    pl.semaphore_signal(barrier, inc=1, device_id=sibling(me, k), device_id_type=MESH)
    pl.semaphore_wait(barrier, 3 * len(axes) + 1)


def send(src, dst, to, send_sem, recv_sem):
    pltpu.make_async_remote_copy(
        src_ref=src,
        dst_ref=dst,
        send_sem=send_sem,
        recv_sem=recv_sem,
        device_id=to,
        device_id_type=MESH,
    ).start()


def wait(ref, sem):
    pltpu.make_async_copy(ref, ref, sem).wait()


def turn(values, cosine, sine):
    values = values.astype(F32)
    return (values * cosine + pltpu.roll(values, HEAD // 2, 1) * sine).astype(BF16)


def layer_kernel(
    query_hbm, key_hbm, value_hbm, residual_hbm, proj_hbm, gain_hbm, router_hbm, routes_hbm,
    cos_hbm, sin_hbm, gate_hbm, up_hbm, down_hbm, out_ref,
    query, residual, gain, router, routes, cosine, sine,
    kv, qrot, krot, far, from_sibling, from_ring, mixed,
    x0, x1, x2, rd0, rd1, rd2, rf0, rf1, rf2, rr0, rr1, rr2, rb0, rb1, rb2, ra0, ra1, ra2,
    wgu, wd, packed, acc, hidden, pick, unpick, row_gate,
    in_sem, kv_send, kv_recv, sib_send, sib_recv, ring_send, ring_recv,
    w_sem, p1s, p1r, p2s, p2r, p3s, p3r, ds, dr,
    qds, qdr, qfs, qfr, q3s, q3r, q2s, q2r, q1s, q1r,
):
    xs, rd, rf, rr = (x0, x1, x2), (rd0, rd1, rd2), (rf0, rf1, rf2), (rr0, rr1, rr2)
    rb, ra = (rb0, rb1, rb2), (ra0, ra1, ra2)
    me, k = place()
    twin = sibling(me, k)

    def spans(r):
        found, at_col = [], 0
        for p in PARTS:
            lo, size = AG_ROUNDS[r]
            if p == 0 and lo == 0:
                lo, size = GATES, size - GATES
            found.append((p, lo, size, at_col))
            at_col += size
        return found

    def weights(r):
        copies = []
        for e in range(2):
            for n, hbm in enumerate((gate_hbm, up_hbm)):
                for p, lo, size, col in spans(r):
                    from_row = p * W + lo - GATES
                    copies.append(
                        pltpu.make_async_copy(
                            hbm.at[e, pl.ds(from_row, size), :],
                            wgu.at[r % 2, e, pl.ds(col, size), pl.ds(n * FF, FF)],
                            w_sem.at[r],
                        )
                    )
        return copies

    def weights_start(r):
        for copy in weights(r):
            copy.start()

    def weights_wait(r):
        total = sum(size for p, lo, size, col in spans(r))
        wait(wgu.at[r % 2, :, pl.ds(0, total), :], w_sem.at[r])

    load_down = pltpu.make_async_copy(down_hbm, wd, w_sem.at[3])


    head = pl.multiple_of((lax.axis_index("tensor") // 4) * HEAD, HEAD)
    y = me["y"]
    loads = [
        pltpu.make_async_copy(src, dst, in_sem.at[i])
        for i, (src, dst) in enumerate(
            (
                (key_hbm.at[0, :, pl.ds(head, HEAD)], kv.at[y, 0]),
                (value_hbm.at[0, :, pl.ds(head, HEAD)], kv.at[y, 1]),
                (query_hbm.at[0], query),
                (cos_hbm, cosine),
                (sin_hbm, sine),
                (proj_hbm.at[pl.ds(0, FF)], wd.at[0]),
                (proj_hbm.at[pl.ds(FF, HEADS * HEAD - FF)], wd.at[1, pl.ds(0, HEADS * HEAD - FF)]),
                (residual_hbm.at[0], residual),
                (gain_hbm, gain),
                (router_hbm, router),
                (routes_hbm.at[0], routes),
            )
        )
    ]
    for load in loads:
        load.start()
    weights_start(0)
    weights_start(1)
    greet(me, k, "xyz")
    for load in loads[:2]:
        load.wait()
    for step in (2, 1, 3):
        send(kv.at[y], kv.at[y], device(me, k, "y", step), kv_send, kv_recv)
    for load in loads[2:5]:
        load.wait()
    own = pl.ds(pl.multiple_of(y * LOCAL, LOCAL), LOCAL)
    for h in range(HEADS):
        qrot[pl.ds(h * LOCAL, LOCAL), :] = turn(
            query[:, h * HEAD : (h + 1) * HEAD], cosine[own, :], sine[own, :]
        )
    wait(kv.at[pl.ds(0, 3)], kv_recv)
    for c in range(4):
        span = pl.ds(c * LOCAL, LOCAL)
        krot[span, :] = turn(kv[c, 0], cosine[span, :], sine[span, :])
    values = kv[:, 1].reshape(SEQ, HEAD)
    place_q = y * LOCAL + lax.broadcasted_iota(jnp.int32, (LOCAL, SEQ), 0)
    causal = place_q >= lax.broadcasted_iota(jnp.int32, (LOCAL, SEQ), 1)
    attended = []
    for h in range(HEADS):
        score = lax.dot_general(
            qrot[pl.ds(h * LOCAL, LOCAL), :], krot[...], (((1,), (1,)), ((), ())),
            preferred_element_type=F32,
        ) * F32(HEAD**-0.5)
        score = jnp.where(causal, score, F32(-1e30))
        peak = jnp.max(score, axis=-1, keepdims=True)
        expon = jnp.exp(score - peak)
        total = jnp.sum(expon, axis=-1, keepdims=True)
        summed = jnp.dot(expon.astype(BF16), values, preferred_element_type=F32)
        attended.append((summed / total).astype(BF16))
    attended = jnp.concatenate(attended, axis=1)
    for load in loads[5:]:
        load.wait()
    for c in range(8):
        cols = slice(c * 512, (c + 1) * 512)
        out = jnp.dot(attended[:, :FF], wd[0, :, cols], preferred_element_type=F32) + jnp.dot(
            attended[:, FF:], wd[1, : HEADS * HEAD - FF, cols], preferred_element_type=F32
        )
        acc[c // 4, pl.ds((c % 4) * LOCAL, LOCAL), :512] = out
        for v in range(4):
            rows = pl.ds(pl.multiple_of((c % 4) * LOCAL + (2 * v + 1 - k) * TOK, TOK), TOK)
            far[v, :, cols] = acc[c // 4, rows, :512].astype(BF16)
        if c % 2 == 1:
            half = pl.ds((c // 2) * 1024, 1024)
            send(
                far.at[:, :, half], from_sibling.at[:, :, half], twin,
                sib_send.at[c // 2], sib_recv.at[c // 2],
            )
    load_down.start()

    def chip_sum(v, c):
        rows = pl.ds(pl.multiple_of((c % 4) * LOCAL + (2 * v + k) * TOK, TOK), TOK)
        return acc[c // 4, rows, :512] + from_sibling[v, :, c * 512 : (c + 1) * 512].astype(F32)

    for i in range(4):
        half = pl.ds(i * 1024, 1024)
        wait(far.at[:, :, half], sib_send.at[i])
        wait(from_sibling.at[:, :, half], sib_recv.at[i])
        for step in (2, 1, 3):
            v = (me["x"] + step) % 4
            for c in range(2 * i, 2 * i + 2):
                far[v, :, c * 512 : (c + 1) * 512] = chip_sum(v, c).astype(BF16)
            send(
                far.at[v, :, half], from_ring.at[step - 1, :, half], device(me, k, "x", step),
                ring_send.at[i], ring_recv.at[i],
            )
    square = jnp.zeros((TOK, 1), F32)
    for c in range(8):
        cols = slice(c * 512, (c + 1) * 512)
        if c % 2 == 0:
            wait(from_ring.at[:, :, pl.ds((c // 2) * 1024, 1024)], ring_recv.at[c // 2])
        projected = chip_sum(me["x"], c)
        for j in range(3):
            projected = projected + from_ring[j, :, cols].astype(F32)
        wide = (residual[:, cols].astype(F32) + projected).astype(BF16)
        mixed[:, cols] = wide
        wide = wide.astype(F32)
        square = square + jnp.sum(wide * wide, axis=-1, keepdims=True)
    scale = lax.rsqrt(square / D + 1e-06)
    for c in range(D // 128):
        wide = mixed[:, c * 128 : (c + 1) * 128].astype(F32)
        normed = (wide * scale * gain[c : c + 1, :].astype(F32)).astype(BF16)
        col = GATES + c * 128
        xs[col // W][k, me["z"], me["y"], me["x"], :, col % W : col % W + 128] = normed
    def at(ref, lead, cols, fix):
        index = [fix.get(axis, slice(None)) for axis in "zyx"]
        return ref.at[(*lead, *index, slice(None), pl.ds(*cols))]


    def p1_start(p):
        a = ORDER[p][0]
        block = at(xs[p], (k,), (0, W), me)
        for step in (2, 1, 3):
            send(block, block, device(me, k, a, step), p1s.at[p], p1r.at[p])

    def p1_wait(p):
        wait(xs[p].at[0, 0, 0, pl.ds(0, 3)], p1r.at[p])

    def p2_ahead(p):
        b = ORDER[p][1]
        block = at(xs[p], (k,), (0, W), me)
        for step in (2, 1, 3):
            send(block, block, device(me, k, b, step), p2s.at[p], p2r.at[p, 3])

    def p2_start(p, r):
        a, b, c = ORDER[p]
        for step in (2, 1, 3):
            for other in (1, 2, 3):
                unit = at(xs[p], (k,), AG_ROUNDS[r], {**me, a: (me[a] + other) % 4})
                send(unit, unit, device(me, k, b, step), p2s.at[p], p2r.at[p, r])

    def p2_bytes(p, r):
        return xs[p].at[0, 0, pl.ds(0, 3), pl.ds(0, 3), :, pl.ds(*AG_ROUNDS[r])]

    def p3_unit(p, r, step, half=None):
        a, b, c = ORDER[p]
        fix = {c: (me[c] + step) % 4}
        if half is not None:
            fix[b] = pl.ds(2 * half, 2)
        return at(xs[p], (k,), AG_ROUNDS[r], fix)

    def p3_send(p, r, step, half, way):
        unit = p3_unit(p, r, step, half)
        recv = p3r.at[p, r, 2] if half is not None else p3r.at[p, r, 0 if way == 1 else 1]
        send(unit, unit, device(me, k, ORDER[p][2], way), p3s.at[p], recv)

    def twin_send(p, r, step):
        unit = p3_unit(p, r, step)
        send(unit, unit, twin, ds.at[p], dr.at[p, r])

    def p3_start(r):
        for p in PARTS:
            if r == 0:
                wait(xs[p].at[0, 0, 0, pl.ds(0, 3)], p2r.at[p, 3])
            wait(p2_bytes(p, r), p2r.at[p, r])
            p3_send(p, r, 0, None, 1)
            p3_send(p, r, 0, None, -1)

    def p3_forward(r):
        for p in PARTS:
            wait(p3_unit(p, r, -1), p3r.at[p, r, 0])
            p3_send(p, r, -1, 0, 1)
            wait(p3_unit(p, r, 1), p3r.at[p, r, 1])
            p3_send(p, r, 1, 1, -1)
        for p in PARTS:
            for step in (0, -1, 1):
                twin_send(p, r, step)

    def p3_finish(r):
        for p in PARTS:
            wait(p3_unit(p, r, 2), p3r.at[p, r, 2])
            twin_send(p, r, 2)

    def twin_wait(r):
        for p in PARTS:
            wait(xs[p].at[1 - k, :, :, :, :, pl.ds(*AG_ROUNDS[r])], dr.at[p, r])

    def gates():
        logits = jnp.zeros((EXPERTS, TOK), F32)
        for p in PARTS:
            lo = GATES if p == 0 else 0
            col = p * W + lo - GATES
            normed = xs[p][k, me["z"], me["y"], me["x"], :, lo:W]
            logits = logits + lax.dot_general(
                router[:, col : col + W - lo], normed, (((1,), (1,)), ((), ())),
                preferred_element_type=F32,
            )
        expert = lax.broadcasted_iota(jnp.int32, (EXPERTS, TOK), 0)
        chosen = expert == routes[0:1, :]
        for j in range(1, 8):
            chosen = jnp.logical_or(chosen, expert == routes[j : j + 1, :])
        peak = jnp.max(jnp.where(chosen, logits, F32(-3e38)), axis=0, keepdims=True)
        expon = jnp.where(chosen, jnp.exp(logits - peak), F32(0.0))
        gate = expon / jnp.sum(expon, axis=0, keepdims=True)
        high = gate.astype(BF16).astype(F32)
        both = jnp.concatenate([high, gate - high], axis=0).astype(BF16)
        unit = lax.broadcasted_iota(jnp.int32, (TOK, TOK), 0) == lax.broadcasted_iota(
            jnp.int32, (TOK, TOK), 1
        )
        turned = lax.dot_general(
            unit.astype(F32).astype(BF16), both, (((1,), (1,)), ((), ())), preferred_element_type=F32
        )
        x0[k, me["z"], me["y"], me["x"], :, :GATES] = turned.astype(BF16)


    def selections():
        first = 2 * (me["y"] * 8 + lax.axis_index("tensor"))
        rows = lax.broadcasted_iota(jnp.int32, (8, GATES), 0)
        lanes = lax.broadcasted_iota(jnp.int32, (8, GATES), 1)
        mine = jnp.logical_and(lanes % EXPERTS == first + rows, rows < 2).astype(F32).astype(BF16)
        s = lax.broadcasted_iota(jnp.int32, (GROUP, GROUP), 0)
        u = lax.broadcasted_iota(jnp.int32, (GROUP, GROUP), 1)
        earlier = jnp.logical_and(s // TOK == u // TOK, s < u).astype(F32).astype(BF16)
        base = (lax.broadcasted_iota(jnp.int32, (1, GROUP), 1) // TOK * CAP).astype(F32)
        slots = lax.broadcasted_iota(jnp.int32, (SLOTS, GROUP), 0).astype(F32)

        def one(g, carry):
            tile = x0[g // 4, g % 4, :, :, :, :GATES].reshape(GROUP, GATES)
            gate = lax.dot_general(mine, tile, (((1,), (1,)), ((), ())), preferred_element_type=F32)
            named = (gate > 0).astype(F32)
            rank = jnp.dot(named.astype(BF16), earlier, preferred_element_type=F32)
            both = []
            for e in range(2):
                hit = jnp.logical_and(slots == rank[e : e + 1] + base, gate[e : e + 1] > 0).astype(F32)
                worth = jnp.sum(hit * gate[e : e + 1], axis=1, keepdims=True)
                row_gate[e, pl.ds(g * SLOTS, SLOTS), :] = jnp.broadcast_to(worth, (SLOTS, 128))
                both.append(hit)
            both = jnp.concatenate(both, axis=0)
            pick[g] = both.astype(BF16)
            unpick[g] = both.T.astype(BF16)
            return carry

        lax.fori_loop(0, 8, one, 0, unroll=True)

    def compact(r, half):
        for p, lo, size, col in spans(r):
            for z in range(4):
                tokens = xs[p][half, z, :, :, :, lo : lo + size].reshape(GROUP, size)
                rows = jnp.dot(pick[4 * half + z], tokens, preferred_element_type=F32).astype(BF16)
                for e in range(2):
                    span = pl.ds((4 * half + z) * SLOTS, SLOTS)
                    packed[e, span, col : col + size] = rows[e * SLOTS : (e + 1) * SLOTS]

    def gate_up(r, rows):
        depth = sum(size for p, lo, size, col in spans(r))
        for e in range(2):
            total = jnp.dot(
                packed[e, rows, :depth], wgu[r % 2, e, :depth, :], preferred_element_type=F32
            )
            if r > 0:
                total = total + acc[e, rows]
            if r < len(AG_ROUNDS) - 1:
                acc[e, rows] = total
            else:
                gate, up = total[:, :FF], total[:, FF:]
                hidden[e, rows] = (gate / (1.0 + jnp.exp(-gate)) * up).astype(BF16)


    def out_cols(p, r):
        lo, size = RS_ROUNDS[r]
        if p == 0 and lo == 0:
            lo, size = GATES, size - GATES
        return lo, size

    def down(r):
        def scatter(p, half):
            lo, size = out_cols(p, r)

            def one(i, carry):
                g = 4 * half + i
                rows = jnp.concatenate(
                    [
                        packed[e, pl.ds(g * SLOTS, SLOTS), 512 * p : 512 * p + size]
                        for e in range(2)
                    ],
                    axis=0,
                )
                tokens = jnp.dot(unpick[g], rows, preferred_element_type=F32).astype(BF16)
                xs[p][half, i, :, :, :, lo : lo + size] = tokens.reshape(4, 4, TOK, size)
                return carry

            lax.fori_loop(0, 4, one, 0, unroll=True)

        def to_twin(p, step):
            src = unit_of(xs[p], (1 - k,), p, r, step)
            recv = qdr.at[p, r, 0 if step == 2 else 1]
            send(src, unit_of(rd[p], (), p, r, step), twin, qds.at[p], recv)

        for p in PARTS:
            lo, size = out_cols(p, r)
            col = p * W + lo - GATES
            for e in range(2):
                part = jnp.dot(hidden[e], wd[e, :, col : col + size], preferred_element_type=F32)
                packed[e, :, 512 * p : 512 * p + size] = (part * row_gate[e, :, 0:1]).astype(BF16)
            scatter(p, 1 - k)
            to_twin(p, 2)
        for p in PARTS:
            for step in (1, 3, 0):
                to_twin(p, step)
        for p in PARTS:
            scatter(p, k)

    def total_into(dst, refs):
        total = refs[0][...].astype(F32)
        for ref in refs[1:]:
            total = total + ref[...].astype(F32)
        dst[...] = total.astype(BF16)

    def unit_of(ref, lead, p, r, step, pieces=1, piece=0):
        a, b, c = ORDER[p]
        fix = {c: (me[c] + step) % 4}
        if pieces == 2:
            fix[b] = pl.ds(2 * piece, 2)
        elif pieces == 4:
            fix[b] = piece
        return at(ref, lead, out_cols(p, r), fix)

    def add_unit(p, r, step):
        def one(i, carry):
            mine = unit_of(xs[p], (k,), p, r, step, 4, i)
            total_into(mine, [mine, unit_of(rd[p], (), p, r, step, 4, i)])
            return carry

        lax.fori_loop(0, 4, one, 0, unroll=True)

    def piece_of(ref, lead, p, r, fix):
        a, b, c = ORDER[p]
        index = [fix.get(axis, slice(None)) for axis in "zyx" if axis != c]
        return ref.at[(*lead, *index, slice(None), pl.ds(*out_cols(p, r)))]

    def a1(r):
        for p in PARTS:
            c = ORDER[p][2]
            wait(unit_of(rd[p], (), p, r, 2), qdr.at[p, r, 0])
            add_unit(p, r, 2)
            for half, way in ((0, 1), (1, -1)):
                src = unit_of(xs[p], (k,), p, r, 2, 2, half)
                send(src, half_slot(p, r, half), device(me, k, c, way), qfs.at[p], qfr.at[p, r, half])

    def b1(r):
        for p in PARTS:
            wait(at(rd[p], (), out_cols(p, r), {"z": pl.ds(0, 3)}), qdr.at[p, r, 1])
            for step in (1, 3, 0):
                add_unit(p, r, step)

    def half_slot(p, r, half, i=None):
        b = ORDER[p][1]
        fix = {} if i is None else {b: i}
        a, b, c = ORDER[p]
        index = [fix.get(axis, slice(None)) for axis in "zyx" if axis != c]
        return rf[p].at[(half, *index, slice(None), pl.ds(*out_cols(p, r)))]

    def s2(r):
        for p in PARTS:
            c = ORDER[p][2]
            for half, way in ((0, 1), (1, -1)):
                wait(half_slot(p, r, half), qfr.at[p, r, half])

                def one(i, carry, half=half, way=way):
                    mine = unit_of(xs[p], (k,), p, r, way, 4, 2 * half + i)
                    total_into(mine, [mine, half_slot(p, r, half, i)])
                    return carry

                lax.fori_loop(0, 2, one, 0, unroll=True)
                src = unit_of(xs[p], (k,), p, r, way)
                slot = piece_of(rr[p], (half,), p, r, {})
                send(src, slot, device(me, k, c, way), q3s.at[p], q3r.at[p, r])

    def s3(r):
        for p in PARTS:
            a, b, c = ORDER[p]
            wait(piece_of(rr[p], (slice(None),), p, r, {}), q3r.at[p, r])

            def one(i, carry, b=b):
                mine = unit_of(xs[p], (k,), p, r, 0, 4, i)
                total_into(mine, [mine] + [piece_of(rr[p], (h,), p, r, {b: i}) for h in range(2)])
                return carry

            lax.fori_loop(0, 4, one, 0, unroll=True)
            for step in (2, 1, 3):
                src = unit_of(xs[p], (k,), p, r, 0, 4, (me[b] + step) % 4)
                slot = rb[p].at[step - 1, :, :, pl.ds(*out_cols(p, r))]
                send(src, slot, device(me, k, b, step), q2s.at[p], q2r.at[p, r])

    def s4(r):
        for p in PARTS:
            a, b, c = ORDER[p]
            cols = pl.ds(*out_cols(p, r))
            wait(rb[p].at[:, :, :, cols], q2r.at[p, r])
            mine = unit_of(xs[p], (k,), p, r, 0, 4, me[b])
            total_into(mine, [mine] + [rb[p].at[j, :, :, cols] for j in range(3)])
            for step in (2, 1, 3):
                src = at(xs[p], (k,), out_cols(p, r), {**me, a: (me[a] + step) % 4})
                send(src, ra[p].at[step - 1, :, cols], device(me, k, a, step), q1s.at[p], q1r.at[p, r])

    def s5(r):
        for p in PARTS:
            lo, size = out_cols(p, r)
            cols = pl.ds(lo, size)
            wait(ra[p].at[:, :, cols], q1r.at[p, r])
            total = at(xs[p], (k,), (lo, size), me)[...].astype(F32)
            for j in range(3):
                total = total + ra[p][j, :, cols].astype(F32)
            col = p * W + lo - GATES
            span = slice(col, col + size)
            out_ref[:, span] = (mixed[:, span].astype(F32) + total).astype(BF16)


    p1_start(1)
    p1_start(2)
    gates()
    p1_start(0)
    for p in (1, 2, 0):
        p2_ahead(p)
    for p in (1, 2, 0):
        p1_wait(p)
        for r in range(3):
            p2_start(p, r)
    p3_start(0)
    p3_start(1)
    p3_forward(0)
    p3_start(2)
    p3_finish(0)
    twin_wait(0)
    selections()
    p3_forward(1)
    everything = pl.ds(0, 8 * SLOTS)
    compact(0, 0)
    compact(0, 1)
    weights_wait(0)
    gate_up(0, everything)
    weights_start(2)
    p3_forward(2)
    p3_finish(1)
    twin_wait(1)
    compact(1, 0)
    compact(1, 1)
    weights_wait(1)
    gate_up(1, everything)
    p3_finish(2)
    weights_wait(2)
    for half in (k, 1 - k):
        if half is not k:
            twin_wait(2)
        compact(2, half)
        gate_up(2, pl.ds(pl.multiple_of(half * 4 * SLOTS, 4 * SLOTS), 4 * SLOTS))
    load_down.wait()
    for p in PARTS:
        wait(xs[p].at[0, 0, 0, pl.ds(0, 3)], p1s.at[p])
        wait(xs[p].at[0, 0, pl.ds(0, 3)], p2s.at[p])
        wait(xs[p].at[0, pl.ds(0, 3)], p3s.at[p])
        wait(xs[p].at[0], ds.at[p])
    down(0)
    a1(0)
    down(1)
    b1(0)
    a1(1)
    s2(0)
    down(2)
    b1(1)
    a1(2)
    s2(1)
    b1(2)
    s3(0)
    s2(2)
    s3(1)
    s4(0)
    s3(2)
    s4(1)
    s5(0)
    s4(2)
    s5(1)
    s5(2)
    wait(kv.at[pl.ds(0, 3)], kv_send)
    for i in range(4):
        wait(from_ring.at[:, :, pl.ds(i * 1024, 1024)], ring_send.at[i])
    for p in PARTS:
        first = out_cols(p, 0)[0]
        cols = pl.ds(first, W - first)
        wait(xs[p].at[0, :, :, :, :, cols], qds.at[p])
        wait(rf[p].at[:, :, :, :, cols], qfs.at[p])
        wait(rr[p].at[:, :, :, :, cols], q3s.at[p])
        wait(rb[p].at[:, :, :, cols], q2s.at[p])
        wait(ra[p].at[:, :, cols], q1s.at[p])


def on_device(
    query_rows,
    key_rows,
    value_rows,
    residual,
    out_proj,
    post_gain,
    router,
    routes,
    w_gate,
    w_up,
    w_down,
):
    vmem = pltpu.VMEM
    hbm = pl.BlockSpec(memory_space=pl.ANY)
    dma = pltpu.SemaphoreType.DMA
    cosine, sine = rope_tables()
    n = len(RS_ROUNDS)

    def half_shape(p):
        a, b, c = ORDER[p]
        return (2, *[2 if axis == b else 4 for axis in "zyx" if axis != c], TOK, W)

    scratch = (
        [
            vmem((LOCAL, HEADS * HEAD), BF16),
            vmem((TOK, D), BF16),
            vmem((D // 128, 128), BF16),
            vmem((EXPERTS, D), BF16),
            vmem((8, TOK), jnp.int32),
            vmem((SEQ, HEAD), F32),
            vmem((SEQ, HEAD), F32),
            vmem((4, 2, LOCAL, HEAD), BF16),
            vmem((HEADS * LOCAL, HEAD), BF16),
            vmem((SEQ, HEAD), BF16),
            vmem((4, TOK, D), BF16),
            vmem((4, TOK, D), BF16),
            vmem((3, TOK, D), BF16),
            vmem((TOK, D), BF16),
        ]
        + [vmem((2, 4, 4, 4, TOK, W), BF16)] * 3
        + [vmem((4, 4, 4, TOK, W), BF16)] * 3
        + [vmem(half_shape(p), BF16) for p in PARTS]
        + [vmem((2, 4, 4, TOK, W), BF16)] * 3
        + [vmem((3, 4, TOK, W), BF16)] * 3
        + [vmem((3, TOK, W), BF16)] * 3
        + [
            vmem((2, 2, 1536, 2 * FF), BF16),
            vmem((2, FF, D), BF16),
            vmem((2, 8 * SLOTS, 1536), BF16),
            vmem((2, 8 * SLOTS, 2 * FF), F32),
            vmem((2, 8 * SLOTS, FF), BF16),
            vmem((8, 2 * SLOTS, GROUP), BF16),
            vmem((8, GROUP, 2 * SLOTS), BF16),
            vmem((2, 8 * SLOTS, 128), F32),
        ]
        + [dma((11,)), dma, dma, dma((4,)), dma((4,)), dma((4,)), dma((4,))]
        + [dma((4,)), dma((3,)), dma((3,)), dma((3,)), dma((3, 4)), dma((3,)), dma((3, 3, 3))]
        + [dma((3,)), dma((3, 3))]
        + [dma((3,)), dma((3, n, 2)), dma((3,)), dma((3, n, 2))]
        + [dma((3,)), dma((3, n))] * 3
    )
    out = pl.pallas_call(
        layer_kernel,
        out_shape=jax.ShapeDtypeStruct((TOK, D), BF16),
        in_specs=[hbm] * 13,
        out_specs=pl.BlockSpec(memory_space=pltpu.VMEM),
        scratch_shapes=scratch,
        compiler_params=pltpu.CompilerParams(
            collective_id=0, has_side_effects=True, vmem_limit_bytes=VMEM
        ),
    )(
        query_rows, key_rows, value_rows, residual, out_proj, post_gain.reshape(D // 128, 128),
        router.T, jnp.swapaxes(routes, 1, 2), jnp.asarray(cosine), jnp.asarray(sine),
        w_gate, w_up, w_down,
    )
    return out[None]


def solution(mesh):
    in_specs = (
        P("dp", "ctx", "tensor"),
        P("dp", "ctx", None),
        P("dp", "ctx", None),
        P("dp", ("ctx", "tensor"), None),
        P("tensor", None),
        P(),
        P(),
        P("dp", ("ctx", "tensor"), None),
        P(("ctx", "tensor"), None, "dp"),
        P(("ctx", "tensor"), None, "dp"),
        P(("ctx", "tensor"), "dp", None),
    )
    out_specs = P("dp", ("ctx", "tensor"), None)
    return jax.shard_map(
        on_device, mesh=mesh, in_specs=in_specs, out_specs=out_specs, check_vma=False
    )
```
